32 devices in a mesh: dp: 8 (over y, x, core), tensor: 4 (over z).
Axes of the slice: x: 2, y: 2, z: 4, core: 2. Of those that a mesh axis runs over, the one named last changes fastest.
Arguments:
- tokens: bfloat16 [9216, 2048], P(('dp', 'tensor')), may hold values from -6 to 6
- lengths: int32 [8, 4], P('dp'), may hold values from 1 to 1024, 1152 in all within a row
- attention_gain: bfloat16 [2048], replicated, may hold values from 0.099609375 to 1.8984375
- w_inputs: bfloat16 [2048, 3072], P('dp', 'tensor'), may hold values from -0.125 to 0.125
- w_output: bfloat16 [2048, 2048], P('tensor', 'dp'), may hold values from -1 to 1
- feed_gain: bfloat16 [2048], replicated, may hold values from 0.099609375 to 1.8984375
- w_gate: bfloat16 [2048, 8192], P('dp', 'tensor'), may hold values from -0.125 to 0.125
- w_up: bfloat16 [2048, 8192], P('dp', 'tensor'), may hold values from -0.125 to 0.125
- w_down: bfloat16 [8192, 2048], P('tensor', 'dp'), may hold values from -0.0625 to 0.0625
- cotangent: bfloat16 [9216, 2048], P(('dp', 'tensor')), may hold values from -6 to 6
Outputs:
- block_out: bfloat16 [9216, 2048], P(('dp', 'tensor'))
- tokens_grad: bfloat16 [9216, 2048], P(('dp', 'tensor'))
- attention_gain_grad: float32 [2048], P(('dp', 'tensor'))
- w_inputs_grad: float32 [2048, 3072], P('dp', 'tensor')
- w_output_grad: float32 [2048, 2048], P('tensor', 'dp')
- feed_gain_grad: float32 [2048], P(('dp', 'tensor'))
- w_gate_grad: float32 [2048, 8192], P('dp', 'tensor')
- w_up_grad: float32 [2048, 8192], P('dp', 'tensor')
- w_down_grad: float32 [8192, 2048], P('tensor', 'dp')
The draws below stay inside these ranges and needn't reach their ends.
Inputs may be any that keep to these rules, and one draw needn't show every extreme that they name: Each row of lengths holds the lengths of the 4 sequences of one group, in order; they sum to 1152, and the longest of each row is 1024.
All inputs are finite; a program needn't handle non-finite values.
Results may differ from the reference program's by a relative error of at most 0.018.
Values may be sent and summed in bfloat16 or wider, within the bound.
No kernel may reach another device: no remote copies, remote signals or barrier semaphores. Data moves between devices by JAX's collectives and lax.ppermute only.
A program may use at most 256 MiB of HBM per device.

```python
import math
import jax
import jax.numpy as jnp
import numpy as np
from jax import lax

D = 2048
FF = 8192
H = 32
KV = 8
HD = 64
LONGEST = 1024
GROUP = 1152
QPK = 4
SEQS = 4
TOKENS = 9216
N_DP = 8


def shard_levels(rng, extent, shards, smallest, high):
    def one(dim, shards_of):
        steps = jax.random.uniform(jax.random.fold_in(jax.random.fold_in(rng, 6), dim), (shards_of,), jnp.float32, smallest / len(shards), high / len(shards))
        return jnp.repeat(jnp.exp(steps), extent[dim] // shards_of).reshape((-1,) + (1,) * (len(extent) - dim - 1))

    loudness = one(*shards[0])
    for cut in shards[1:]:
        loudness = loudness * one(*cut)
    return loudness


def split_up(count, total, limit, slope):
    portions = [(1 << 20) // math.isqrt(grade ** slope) + 1 for grade in range(2, count + 1)]
    surplus, counts = total - limit - (count - 1), [1] * (count - 1)
    while surplus > 0:
        movable = [i for i in range(count - 1) if counts[i] < limit]
        whole, budget = sum([portions[i] for i in movable]), surplus
        for i in movable:
            extra = min(limit - counts[i], max(1, budget * portions[i] // whole), surplus)
            counts[i] = counts[i] + extra
            surplus = surplus - extra
    return np.array([limit] + counts)


def ragged_sizes(own_key, number_of, total, limit, skew):
    if number_of == 2:
        one = jax.random.randint(own_key, (), max(1, total - limit), min(limit, total - 1) + 1)
        return jnp.stack([one, total - one])
    sizes = jnp.asarray(split_up(number_of, total, limit, skew), jnp.int32)
    twos = (number_of - 1) // 2
    donor, taker = sizes[1:1 + 2 * twos:2], sizes[2:2 + 2 * twos:2]
    slack = jnp.minimum(donor - 1, limit - taker)
    passed = jax.random.randint(jax.random.fold_in(own_key, 1), (twos,), 0, 1 << 20) % (slack + 1)
    sizes = sizes.at[1:1 + 2 * twos:2].set(donor - passed).at[2:2 + 2 * twos:2].set(taker + passed)
    return sizes[jax.random.permutation(jax.random.fold_in(own_key, 2), number_of)]


def gaussian(own_key, extent, deviation, most, cuts=(), held_as=jnp.bfloat16):
    values = jax.random.normal(own_key, extent, jnp.float32) * deviation
    if len(cuts) > 0:
        values = shard_levels(own_key, extent, cuts, -0.22, 0.18) * values
    return jnp.clip(values, min=-most, max=most).astype(held_as)


def setup_inputs(seed: int = 0) -> dict:
    seeds = jax.random.split(jax.random.key(seed), 11)
    return {
        "tokens": gaussian(seeds[0], (TOKENS, D), 1.0, 6.0, ((0, 32),)),
        "lengths": jax.vmap(lambda own: ragged_sizes(own, SEQS, GROUP, LONGEST, 2))(jax.random.split(seeds[1], N_DP)).reshape((N_DP, SEQS)).astype(jnp.int32),
        "attention_gain": jnp.clip(1.0 + 0.18 * jax.random.normal(seeds[2], (D,), jnp.float32), 0.099609375, 1.8984375).astype(jnp.bfloat16),
        "w_inputs": gaussian(seeds[3], (D, (H + 2 * KV) * HD), D ** -0.5, 0.125, ((0, 8), (1, 4))),
        "w_output": gaussian(seeds[4], (H * HD, D), (H * HD * 16 // LONGEST) ** -0.5, 1.0, ((0, 4), (1, 8))),
        "feed_gain": jnp.clip(1.0 + 0.18 * jax.random.normal(seeds[5], (D,), jnp.float32), 0.099609375, 1.8984375).astype(jnp.bfloat16),
        "w_gate": gaussian(seeds[6], (D, FF), D ** -0.5, 0.125, ((0, 8), (1, 4))),
        "w_up": gaussian(seeds[7], (D, FF), D ** -0.5, 0.125, ((0, 8), (1, 4))),
        "w_down": gaussian(seeds[8], (FF, D), FF ** -0.5, 0.0625, ((0, 4), (1, 8))),
        "cotangent": gaussian(seeds[9], (TOKENS, D), 1.0, 6.0, ((0, 32),)),
    }


EPS = 1e-05
THETA = 500000.0
FLOOR = -1e+30
HIGH = lax.Precision.HIGHEST

@jax.custom_vjp
def low(v):
    return lax.optimization_barrier(v.astype(jnp.bfloat16)).astype(jnp.float32)

@jax.custom_vjp
def low_back(v):
    return v

def low_keep(v):
    return (low(v), None)

def low_pass(kept, grad):
    return (grad,)

def back_keep(v):
    return (v, None)

def back_low(kept, grad):
    return (low(grad),)
low.defvjp(low_keep, low_pass)
low_back.defvjp(back_keep, back_low)

def layout(lens, rows_count):
    lens = lens.astype(jnp.int32)
    ends = jnp.cumsum(lens).astype(jnp.int32)
    rows = jnp.arange(rows_count, dtype=jnp.int32)
    segment = lax.optimization_barrier(jnp.sum((rows[:, None] >= ends[None, :]).astype(jnp.int32), axis=1)).astype(jnp.int32)
    starts = ends - lens
    numbers = jnp.arange(lens.shape[0], dtype=jnp.int32)
    picked = jnp.where(segment[:, None] == numbers[None, :], starts[None, :], 0)
    position = (rows - lax.optimization_barrier(jnp.sum(picked, axis=1))).astype(jnp.int32)
    return (segment, position)

def rotary(position):
    index = jnp.arange(HD // 2, dtype=jnp.float32)
    inverse = jnp.exp(index * (-2.0 * math.log(THETA) / HD))
    angle = position.astype(jnp.float32)[:, None] * inverse[None, :]
    cosine = jnp.cos(angle)
    sine = jnp.sin(angle)
    return (jnp.concatenate([cosine, cosine], 1), jnp.concatenate([sine, sine], 1))

def turn(value, cosine, sine):
    half = value.shape[-1] // 2
    rotated = jnp.concatenate([-value[..., half:], value[..., :half]], -1)
    return value * cosine + rotated * sine

def block_mask(segment, start, block):
    total = segment.shape[0]
    query_rows = start + jnp.arange(block, dtype=jnp.int32)
    key_rows = jnp.arange(total, dtype=jnp.int32)
    query_segment = lax.dynamic_slice_in_dim(segment, start, block, 0)
    return (query_segment[:, None] == segment[None, :]) & (key_rows[None, :] <= query_rows[:, None])

def normalize(value, gain):
    scale = lax.rsqrt(lax.optimization_barrier(jnp.mean(value * value, axis=1, keepdims=True)) + EPS)
    return value * scale * gain[None, :]

def product(left, right):
    return jnp.dot(left, right, precision=HIGH, preferred_element_type=jnp.float32)

def attend(joint, segment, position):
    rows_count = joint.shape[0]
    cosine, sine = rotary(position)
    grouped = joint.reshape(rows_count, KV, QPK + 2, HD)
    query = low(turn(grouped[:, :, :QPK, :], cosine[:, None, None, :], sine[:, None, None, :]))
    key = low(turn(grouped[:, :, QPK, :], cosine[:, None, :], sine[:, None, :]))
    value = low(grouped[:, :, QPK + 1, :])
    block = rows_count // 2
    scale = 1.0 / math.sqrt(HD)

    @jax.checkpoint
    def one_block(index):
        start = index * block
        query_block = lax.dynamic_slice_in_dim(query, start, block, 0)
        allowed = block_mask(segment, start, block)
        scores = low_back(jnp.einsum('qgjd,kgd->gjqk', query_block, key, precision=HIGH) * scale)
        scores = jnp.where(allowed[None, None], scores, FLOOR)
        top = lax.optimization_barrier(jnp.max(scores, axis=-1, keepdims=True))
        weights = jnp.exp(scores - top)
        probs = low(weights / lax.optimization_barrier(jnp.sum(weights, axis=-1, keepdims=True)))
        return jnp.einsum('gjqk,kgd->qgjd', probs, value, precision=HIGH)
    outputs = lax.map(one_block, jnp.arange(2, dtype=jnp.int32))
    return outputs.reshape(rows_count, KV * QPK * HD)

def group_forward(tokens, lens, attention_gain, w_inputs, w_output, feed_gain, w_gate, w_up, w_down):
    segment, position = layout(lens, tokens.shape[0])
    first = low(normalize(tokens, attention_gain))
    joint = low_back(product(first, w_inputs))
    heads = low_back(low(attend(joint, segment, position)))
    mixed = tokens + low_back(product(heads, w_output))
    second = low(normalize(mixed, feed_gain))
    gate = low_back(product(second, w_gate))
    up = low_back(product(second, w_up))
    hidden = low(jax.nn.silu(gate) * up)
    return mixed + low_back(product(hidden, w_down))

def reference(tokens, lengths, attention_gain, w_inputs, w_output, feed_gain, w_gate, w_up, w_down, cotangent):

    def forward(tokens_wide, gain_one, inputs_wide, output_wide, gain_two, gate_wide, up_wide, down_wide):
        stacked = tokens_wide.reshape(N_DP, GROUP, D)

        def per_group(item):
            return jax.checkpoint(group_forward)(item[0], item[1], gain_one, inputs_wide, output_wide, gain_two, gate_wide, up_wide, down_wide)
        return lax.map(per_group, (stacked, lengths)).reshape(N_DP * GROUP, D)
    primals = (tokens.astype(jnp.float32), attention_gain.astype(jnp.float32), w_inputs.astype(jnp.float32), w_output.astype(jnp.float32), feed_gain.astype(jnp.float32), w_gate.astype(jnp.float32), w_up.astype(jnp.float32), w_down.astype(jnp.float32))
    result, pull = jax.vjp(forward, *primals)
    grads = pull(cotangent.astype(jnp.float32))
    return (result.astype(jnp.bfloat16), grads[0].astype(jnp.bfloat16), grads[1], grads[2], grads[3], grads[4], grads[5], grads[6], grads[7])
```

```python
import math

import jax
import jax.numpy as jnp
from jax import lax
from jax.experimental import pallas as pl
from jax.experimental.pallas import tpu as pltpu
from jax.sharding import PartitionSpec as P

KV = 8
HD = 64
QPK = 4
EPS = 1e-05
THETA = 500000.0
FLOOR = -1e30
LANES = 128
BLOCK = 128
PARTS = 3
VMEM = 56 << 20
NT = (((1,), (1,)), ((), ()))
NN = (((1,), (0,)), ((), ()))
TN = (((0,), (0,)), ((), ()))


def layout(lens, rows_count):
    ends = jnp.cumsum(lens)
    rows = jnp.arange(rows_count, dtype=jnp.int32)
    segment = jnp.sum((rows[:, None] >= ends[None, :]).astype(jnp.int32), axis=1)
    starts = ends - lens
    numbers = jnp.arange(lens.shape[0], dtype=jnp.int32)
    picked = jnp.where(segment[:, None] == numbers[None, :], starts[None, :], 0)
    return segment, rows - jnp.sum(picked, axis=1)


def tables(lens, rows_count):
    segment, position = layout(lens, rows_count)
    index = (jnp.arange(LANES, dtype=jnp.int32) % (HD // 2)).astype(jnp.float32)
    inverse = jnp.exp(index * (-2.0 * math.log(THETA) / HD))
    angle = position.astype(jnp.float32)[:, None] * inverse[None, :]
    count = lens.shape[0]
    lane = jnp.arange(LANES, dtype=jnp.int32)[None, :] - HD
    same = lane == segment[:, None]
    inside = (lane >= 0) & (lane < count)
    extra = (lane >= count) & (lane < count + PARTS)
    key_lanes = jnp.where((same & inside) | extra, 1.0, 0.0).astype(jnp.bfloat16)
    query_lanes = jnp.where(inside & ~same, FLOOR, 0.0).astype(jnp.bfloat16)
    return jnp.cos(angle), jnp.sin(angle), query_lanes, key_lanes


def dot(left, right, dims=NN):
    return lax.dot_general(left, right, dims, preferred_element_type=jnp.float32)


def rotate(value, cosine, sine):
    low = lax.broadcasted_iota(jnp.int32, value.shape, 1) % HD < HD // 2
    up = pltpu.roll(value, LANES - HD // 2, 1)
    down = pltpu.roll(value, HD // 2, 1)
    return value * cosine + jnp.where(low, -up, down) * sine


def unrotate(value, cosine, sine):
    low = lax.broadcasted_iota(jnp.int32, value.shape, 1) % HD < HD // 2
    scaled = value * sine
    up = pltpu.roll(scaled, LANES - HD // 2, 1)
    down = pltpu.roll(scaled, HD // 2, 1)
    return value * cosine + jnp.where(low, up, -down)


def split(value, parts):
    out = []
    for _ in range(parts):
        piece = value.astype(jnp.bfloat16).astype(jnp.float32)
        out.append(piece)
        value = value - piece
    return out


def forward_kernel(count, joint, cos, sin, query_lanes, key_lanes, heads, query, key, value):
    rows = joint.shape[0]
    cosine, sine = cos[...], sin[...]
    lane = lax.broadcasted_iota(jnp.int32, (rows, LANES), 1)
    left = lane < HD
    beside = query_lanes[...].astype(jnp.float32)
    for pair in range(QPK // 2):
        both = rotate(joint[:, pair * LANES : (pair + 1) * LANES], cosine, sine) * (1.0 / math.sqrt(HD))
        query[2 * pair] = jnp.where(left, both, beside).astype(jnp.bfloat16)
        query[2 * pair + 1] = jnp.where(left, pltpu.roll(both, HD, 1), beside).astype(jnp.bfloat16)
    last = joint[:, QPK * HD : QPK * HD + LANES]
    key[...] = jnp.where(left, rotate(last, cosine, sine), key_lanes[...].astype(jnp.float32)).astype(
        jnp.bfloat16
    )
    ones = jnp.where((lane >= HD) & (lane < HD + PARTS), 1.0, 0.0)
    value[...] = jnp.where(left, pltpu.roll(last, HD, 1), ones).astype(jnp.bfloat16)
    lower = lax.broadcasted_iota(jnp.int32, (BLOCK, BLOCK), 1) <= lax.broadcasted_iota(
        jnp.int32, (BLOCK, BLOCK), 0
    )
    lower = jnp.concatenate([lower] * QPK, 0)
    narrow = lax.broadcasted_iota(jnp.int32, (QPK * BLOCK, LANES), 1)
    for block in range(rows // BLOCK):
        start = block * BLOCK
        end = start + BLOCK
        own = query[:, start:end, :].reshape(QPK * BLOCK, LANES)
        near = jnp.where(lower, dot(own, key[start:end, :], NT), FLOOR)
        top = jnp.max(near, 1, keepdims=True)
        if block:
            far = dot(own, key[0:start, :], NT)
            top = jnp.maximum(top, jnp.max(far, 1, keepdims=True))
        out = dot(jnp.exp(near - top).astype(jnp.bfloat16), value[start:end, :])
        if block:
            out = out + dot(jnp.exp(far - top).astype(jnp.bfloat16), value[0:start, :])
        total = out[:, HD : HD + 1]
        out = out * (1.0 / total)
        held = own.astype(jnp.float32)
        for part, piece in enumerate(split(top + jnp.log(total), PARTS)):
            held = jnp.where(narrow == HD + count + part, -piece, held)
        query[:, start:end, :] = held.astype(jnp.bfloat16).reshape(QPK, BLOCK, LANES)
        each = [out[head * BLOCK : (head + 1) * BLOCK] for head in range(QPK)]
        half = narrow[:BLOCK] < HD
        for pair in range(QPK // 2):
            heads[start:end, pair * LANES : (pair + 1) * LANES] = jnp.where(
                half, each[2 * pair], pltpu.roll(each[2 * pair + 1], HD, 1)
            ).astype(jnp.bfloat16)


def whole(*shape):
    return pl.BlockSpec(shape, lambda g: (0,) * len(shape))


def grouped(*shape):
    return pl.BlockSpec((None,) + shape, lambda g: (g,) + (0,) * len(shape))


def columns(rows, width):
    return pl.BlockSpec((rows, width), lambda g: (0, g))


def attention_forward(joint, held, count, groups):
    rows = joint.shape[0]
    shape = jax.ShapeDtypeStruct
    low = jnp.bfloat16
    return pl.pallas_call(
        lambda *refs: forward_kernel(count, *refs),
        grid=(groups,),
        in_specs=[columns(rows, (QPK + 2) * HD)] + [whole(rows, LANES)] * 4,
        out_specs=[
            columns(rows, QPK * HD),
            grouped(QPK, rows, LANES),
            grouped(rows, LANES),
            grouped(rows, LANES),
        ],
        out_shape=[
            shape((rows, groups * QPK * HD), low),
            shape((groups, QPK, rows, LANES), low),
            shape((groups, rows, LANES), low),
            shape((groups, rows, LANES), low),
        ],
        compiler_params=pltpu.CompilerParams(vmem_limit_bytes=VMEM),
        cost_estimate=pl.CostEstimate(
            flops=groups * 12 * rows * rows * QPK * HD,
            bytes_accessed=16 << 20,
            transcendentals=groups * QPK * rows * rows // 2,
        ),
    )(joint, *held)


def backward_kernel(query, key, value, heads, grads, cos, sin, out, query_grad, key_grad, value_grad):
    rows = key.shape[0]
    key_grad[...] = jnp.zeros_like(key_grad)
    value_grad[...] = jnp.zeros_like(value_grad)
    turned = key[...].astype(jnp.float32).T.astype(jnp.bfloat16)
    upper = lax.broadcasted_iota(jnp.int32, (BLOCK, BLOCK), 0) <= lax.broadcasted_iota(
        jnp.int32, (BLOCK, BLOCK), 1
    )
    upper = jnp.concatenate([upper] * QPK, 1)
    lane = lax.broadcasted_iota(jnp.int32, (QPK * BLOCK, LANES), 1)
    half = lane[:BLOCK] < HD

    def stacked(ref, start, end):
        pieces = []
        for pair in range(QPK // 2):
            both = ref[start:end, pair * LANES : (pair + 1) * LANES].astype(jnp.float32)
            pieces += [both, pltpu.roll(both, HD, 1)]
        return jnp.where(lane < HD, jnp.concatenate(pieces, 0), 0.0)

    for block in range(rows // BLOCK):
        start = block * BLOCK
        end = start + BLOCK
        own = query[:, start:end, :].reshape(QPK * BLOCK, LANES)
        grad = stacked(grads, start, end)
        inner = jnp.sum(grad * stacked(heads, start, end), 1, keepdims=True)
        low = grad.astype(jnp.bfloat16)
        for part, piece in enumerate(split(inner, PARTS)):
            grad = jnp.where(lane == HD + part, -piece, grad)
        beside = grad.astype(jnp.bfloat16)
        turned_grad = None
        for first, last in ([(0, start)] if block else []) + [(start, end)]:
            scores = dot(key[first:last, :], own, NT)
            if first == start:
                scores = jnp.where(upper, scores, FLOOR)
            probs = jnp.exp(scores)
            score_grad = (probs * dot(value[first:last, :], beside, NT)).astype(jnp.bfloat16)
            value_grad[first:last, :] += dot(probs.astype(jnp.bfloat16), low)
            key_grad[first:last, :] += dot(score_grad, own)
            piece = dot(turned[:, first:last], score_grad)
            turned_grad = piece if turned_grad is None else turned_grad + piece
        back = turned_grad.T * (1.0 / math.sqrt(HD))
        each = [back[head * BLOCK : (head + 1) * BLOCK] for head in range(QPK)]
        for pair in range(QPK // 2):
            query_grad[start:end, pair * LANES : (pair + 1) * LANES] = jnp.where(
                half, each[2 * pair], pltpu.roll(each[2 * pair + 1], HD, 1)
            )
    cosine, sine = cos[...], sin[...]
    for pair in range(QPK // 2):
        at = slice(pair * LANES, (pair + 1) * LANES)
        out[:, at] = unrotate(query_grad[:, at], cosine, sine).astype(jnp.bfloat16)
    left = lax.broadcasted_iota(jnp.int32, (rows, LANES), 1) < HD
    key_part = unrotate(jnp.where(left, key_grad[...], 0.0), cosine, sine)
    out[:, QPK * HD : QPK * HD + LANES] = jnp.where(
        left, key_part, pltpu.roll(value_grad[...], HD, 1)
    ).astype(jnp.bfloat16)


def attention_backward(query, key, value, heads, grads, held, groups):
    rows = key.shape[1]
    wide = (QPK + 2) * HD
    return pl.pallas_call(
        backward_kernel,
        grid=(groups,),
        in_specs=[grouped(QPK, rows, LANES), grouped(rows, LANES), grouped(rows, LANES)]
        + [columns(rows, QPK * HD)] * 2
        + [whole(rows, LANES)] * 2,
        out_specs=columns(rows, wide),
        out_shape=jax.ShapeDtypeStruct((rows, groups * wide), jnp.bfloat16),
        scratch_shapes=[
            pltpu.VMEM((rows, QPK * HD), jnp.float32),
            pltpu.VMEM((rows, LANES), jnp.float32),
            pltpu.VMEM((rows, LANES), jnp.float32),
        ],
        compiler_params=pltpu.CompilerParams(vmem_limit_bytes=VMEM),
        cost_estimate=pl.CostEstimate(
            flops=groups * 30 * rows * rows * QPK * HD,
            bytes_accessed=16 << 20,
            transcendentals=groups * QPK * rows * rows // 2,
        ),
    )(query, key, value, heads, grads, held[0], held[1])


def call(kernel, grid, operands, specs, out_specs, out_shape, flops, earlier=(), scratch=()):
    count, extra = len(operands), len(earlier)
    return pl.pallas_call(
        lambda *refs: kernel(*refs[:count], *refs[count + extra :]),
        grid=(grid,),
        in_specs=specs + [pl.BlockSpec(memory_space=pl.ANY)] * extra,
        out_specs=out_specs,
        out_shape=out_shape,
        scratch_shapes=list(scratch),
        compiler_params=pltpu.CompilerParams(vmem_limit_bytes=VMEM),
        cost_estimate=pl.CostEstimate(flops=flops, bytes_accessed=16 << 20, transcendentals=0),
    )(*operands, *earlier)


def column_block(rows, wide):
    return pl.BlockSpec((rows, wide), lambda f: (0, f))


def row_block(wide, width):
    return pl.BlockSpec((wide, width), lambda f: (f, 0))


def low_shape(*shape):
    return jax.ShapeDtypeStruct(shape, jnp.bfloat16)


def block_size(extent):
    return 256 if extent % 256 == 0 else extent


def tied(value, *earlier):
    rows, width = value.shape
    wide = rows // 2 if rows % 32 == 0 else rows

    def kernel(source, target):
        target[...] = source[...]

    block = row_block(wide, width)
    return call(kernel, rows // wide, (value,), [block], block, low_shape(rows, width), 0, earlier)


def tied_sum(left, right, *earlier):
    rows, width = left.shape
    wide = rows // 2 if rows % 32 == 0 else rows

    def kernel(left, right, out):
        out[...] = (left[...].astype(jnp.float32) + right[...].astype(jnp.float32)).astype(out.dtype)

    block = row_block(wide, width)
    return call(
        kernel, rows // wide, (left, right), [block] * 2, block, low_shape(rows, width), 0, earlier
    )


def project(slots, weight, places):
    count = len(slots)
    local, width = slots[0].shape
    extent = weight.shape[1]
    wide = block_size(extent)

    def kernel(*refs):
        places, weight, out = refs[count], refs[count + 1], refs[count + 2]
        for slot in range(count):
            start = pl.multiple_of(places[slot] * local, 16)
            out[pl.ds(start, local), :] = dot(refs[slot][...], weight[...])

    return call(
        kernel,
        extent // wide,
        (*slots, places, weight),
        [whole(local, width)] * count
        + [pl.BlockSpec(memory_space=pltpu.SMEM), column_block(width, wide)],
        column_block(count * local, wide),
        jax.ShapeDtypeStruct((count * local, extent), jnp.float32),
        2 * count * local * width * extent,
    )


def to_slots(value, places, *earlier):
    count = places.shape[0]
    rows, width = value.shape
    local = rows // count

    def kernel(value, places, *out):
        for slot in range(count):
            start = pl.multiple_of(places[slot] * local, 16)
            out[slot][...] = value[pl.ds(start, local), :]

    return call(
        kernel,
        1,
        (value, places),
        [whole(rows, width), pl.BlockSpec(memory_space=pltpu.SMEM)],
        [whole(local, width)] * count,
        [low_shape(local, width)] * count,
        0,
        earlier,
    )


def from_slots(slots, places, *earlier):
    count = len(slots)
    local, width = slots[0].shape

    def kernel(*refs):
        for slot in range(count):
            start = pl.multiple_of(refs[count][slot] * local, 16)
            refs[-1][pl.ds(start, local), :] = refs[slot][...]

    return call(
        kernel,
        1,
        (*slots, places),
        [whole(local, width)] * count + [pl.BlockSpec(memory_space=pltpu.SMEM)],
        whole(count * local, width),
        low_shape(count * local, width),
        0,
        earlier,
    )


def feed_forward(slots, w_gate, w_up, *earlier):
    count = len(slots)
    rows, width = slots[0].shape
    extent = w_gate.shape[1]
    wide = block_size(extent)

    def kernel(*refs):
        w_gate, w_up = refs[count], refs[count + 1]
        out = refs[count + 2 :]
        for slot in range(count):
            one = dot(refs[slot][...], w_gate[...])
            two = dot(refs[slot][...], w_up[...])
            out[slot][...] = (one * jax.nn.sigmoid(one) * two).astype(jnp.bfloat16)
            out[count + slot][...] = one.astype(jnp.bfloat16)
            out[2 * count + slot][...] = two.astype(jnp.bfloat16)

    out = call(
        kernel,
        extent // wide,
        (*slots, w_gate, w_up),
        [whole(rows, width)] * count + [column_block(width, wide)] * 2,
        [column_block(rows, wide)] * (3 * count),
        [low_shape(rows, extent)] * (3 * count),
        4 * count * rows * width * extent,
        earlier,
    )
    return out[:count], out[count : 2 * count], out[2 * count :]


def feed_backward(grads, w_down, gates, ups, *earlier):
    count = len(grads)
    rows, width = grads[0].shape
    extent = w_down.shape[0]
    wide = block_size(extent)

    def kernel(*refs):
        w_down = refs[3 * count]
        out = refs[3 * count + 1 :]
        for slot in range(count):
            hidden_grad = dot(refs[slot][...], w_down[...], NT)
            one = refs[count + slot][...].astype(jnp.float32)
            sigma = jax.nn.sigmoid(one)
            scaled = hidden_grad * sigma
            slope = refs[2 * count + slot][...].astype(jnp.float32) * (1.0 + one * (1.0 - sigma))
            out[slot][...] = (scaled * slope).astype(jnp.bfloat16)
            out[count + slot][...] = (scaled * one).astype(jnp.bfloat16)

    out = call(
        kernel,
        extent // wide,
        (*grads, *gates, *ups, w_down),
        [whole(rows, width)] * count
        + [column_block(rows, wide)] * (2 * count)
        + [row_block(wide, width)],
        [column_block(rows, wide)] * (2 * count),
        [low_shape(rows, extent)] * (2 * count),
        2 * count * rows * width * extent,
        earlier,
    )
    return out[:count], out[count:]


def sum_of_products(terms, *earlier):
    count = len(terms[0][0])
    rows, depth = terms[0][0][0].shape
    extent = terms[0][1].shape[0]
    wide = block_size(extent)
    total = len(terms)

    def kernel(*refs):
        weights = refs[total * count : total * count + total]
        out = refs[total * count + total :]
        for slot in range(count):
            sums = dot(refs[slot][...], weights[0][...], NT)
            for term in range(1, total):
                sums = sums + dot(refs[term * count + slot][...], weights[term][...], NT)
            out[slot][...] = sums.astype(jnp.bfloat16)

    slots = [slot for term in terms for slot in term[0]]
    return call(
        kernel,
        extent // wide,
        (*slots, *[term[1] for term in terms]),
        [whole(rows, depth)] * (total * count) + [row_block(wide, depth)] * total,
        [column_block(rows, wide)] * count,
        [low_shape(rows, extent)] * count,
        2 * total * count * rows * depth * extent,
        earlier,
    )


def product(slots, right, *earlier):
    count = len(slots)
    rows, depth = slots[0].shape
    extent = right.shape[1]
    wide = block_size(extent)

    def kernel(*refs):
        for slot in range(count):
            refs[count + 1 + slot][...] = dot(refs[slot][...], refs[count][...]).astype(jnp.bfloat16)

    return call(
        kernel,
        extent // wide,
        (*slots, right),
        [whole(rows, depth)] * count + [column_block(depth, wide)],
        [column_block(rows, wide)] * count,
        [low_shape(rows, extent)] * count,
        2 * count * rows * depth * extent,
        earlier,
    )


def weight_grad(lefts, rights, *earlier):
    count = len(lefts)
    rows, extent = lefts[0].shape
    width = rights[0].shape[1]
    wide = block_size(extent)
    narrow = 512 if width % 512 == 0 else width

    def kernel(*refs):
        out, left, right = refs[2 * count :]

        @pl.when(pl.program_id(0) == 0)
        def _():
            for slot in range(count):
                right[slot * rows : (slot + 1) * rows, :] = refs[count + slot][...]

        for slot in range(count):
            left[slot * rows : (slot + 1) * rows, :] = refs[slot][...]
        for start in range(0, width, narrow):
            at = slice(start, start + narrow)
            out[:, at] = dot(left[...], right[:, at], TN).astype(jnp.bfloat16)

    return call(
        kernel,
        extent // wide,
        (*lefts, *rights),
        [column_block(rows, wide)] * count + [whole(rows, width)] * count,
        row_block(wide, width),
        low_shape(extent, width),
        2 * count * rows * width * extent,
        earlier,
        [pltpu.VMEM((count * rows, wide), jnp.bfloat16), pltpu.VMEM((count * rows, width), jnp.bfloat16)],
    )


def after(value, *earlier):
    return lax.optimization_barrier((value,) + earlier)[0]


def ring():
    count = lax.axis_size("tensor")
    return [0] + list(range(1, count, 2)) + list(range(2, count, 2))[::-1]


def ring_shift(value, by):
    order = ring()
    count = len(order)
    return lax.ppermute(value, "tensor", [(order[k], order[(k + by) % count]) for k in range(count)])


def slot_places():
    order = ring()
    count = len(order)
    me = lax.axis_index("tensor")
    at = sum(jnp.where(me == device, place, 0) for place, device in enumerate(order))
    back = (at - jnp.arange(count, dtype=jnp.int32)) % count
    return sum(jnp.where(back == place, device, 0) for place, device in enumerate(order)).astype(jnp.int32)


def ring_gather(piece, pauses=()):
    pauses = dict(pauses)
    slots = [piece]
    for step in range(1, lax.axis_size("tensor")):
        last = slots[-1]
        if step in pauses:
            last = tied(last, *pauses[step])
        slots.append(ring_shift(last, 1))
    return slots


def ring_scatter(parts, pauses=()):
    pauses = dict(pauses)
    count = len(parts)
    arrivals = []
    moving = parts[1]
    for step in range(1, count):
        arrivals.append(ring_shift(moving, 1))
        if step < count - 1:
            if step + 1 in pauses:
                moving = tied_sum(arrivals[-1], parts[step + 1], *pauses[step + 1])
            else:
                moving = add(arrivals[-1], parts[step + 1])
    total = parts[0].astype(jnp.float32) + arrivals[-1].astype(jnp.float32)
    return total, arrivals


def add(left, right):
    return (left.astype(jnp.float32) + right.astype(jnp.float32)).astype(jnp.bfloat16)


def exchange(parts):
    count = len(parts)
    return [parts[0]] + [ring_shift(parts[count - q], q) for q in range(1, count)]


def flip(value, bits):
    count = lax.axis_size("dp")
    return lax.ppermute(value, "dp", [(k, k ^ bits) for k in range(count)])


def cube_scatter(pick):
    me = lax.axis_index("dp")
    both = {bits: add(pick(me ^ bits), flip(pick(me ^ bits ^ 1), 1)) for bits in (6, 2, 4, 0)}
    half = both[0].shape[0] // 2
    corner = both[6]
    from_x = flip(corner[:half], 2)
    from_y = flip(corner[half:], 4)
    go_y = jnp.concatenate([add(both[4][:half], from_x), both[4][half:]], 0)
    go_x = jnp.concatenate([both[2][:half], add(both[2][half:], from_y)], 0)
    wide = jnp.float32
    return both[0].astype(wide) + flip(go_x, 2).astype(wide) + flip(go_y, 4).astype(wide)


def gather_rows(piece):
    return lax.all_gather(piece, "dp", axis=0, tiled=True)


def gather_columns(piece):
    return lax.all_gather(piece, "dp", axis=1, tiled=True)


def sum_rows(value):
    return lax.psum_scatter(value, "dp", scatter_dimension=0, tiled=True).astype(jnp.float32)


def sum_columns(value):
    return lax.psum_scatter(value, "dp", scatter_dimension=1, tiled=True).astype(jnp.float32)


def sum_gain(value, places):
    count = lax.axis_size("tensor")
    copies = lax.axis_size("dp")
    me = lax.axis_index("dp")
    cut = value.reshape(copies, count, -1).transpose(1, 0, 2)
    pieces = [lax.dynamic_index_in_dim(cut, places[slot], 0, False) for slot in range(count)]
    total = sum(exchange(pieces))
    bits = copies // 2
    while bits:
        mine = (me // bits) % 2
        pair = total.reshape(2, bits, -1)
        keep = lax.dynamic_index_in_dim(pair, mine, 0, False)
        give = lax.dynamic_index_in_dim(pair, 1 - mine, 0, False)
        total = keep + lax.ppermute(give, "dp", [(k, k ^ bits) for k in range(copies)])
        bits //= 2
    return total.reshape(-1)


def scatter_product(left, right, axis):
    count = lax.axis_size("dp")
    if count != 8:
        value = dot(left, right, TN).astype(jnp.bfloat16)
        return sum_columns(value) if axis else sum_rows(value)
    if axis:
        cut = right.reshape(right.shape[0], count, -1).transpose(1, 0, 2)
        pick = lambda i: dot(left, lax.dynamic_index_in_dim(cut, i, 0, False), TN).astype(jnp.bfloat16)
    else:
        value = dot(left, right, TN).astype(jnp.bfloat16).reshape(count, -1, right.shape[1])
        pick = lambda i: lax.dynamic_index_in_dim(value, i, 0, False)
    return cube_scatter(pick)


def normalize(value, gain):
    scale = lax.rsqrt(jnp.mean(value * value, axis=1, keepdims=True) + EPS)
    return (value * scale * gain[None, :], scale)


def norm_back(grad, value, scale, gain):
    inner = grad * gain[None, :]
    mean_term = jnp.sum(inner * value, axis=1, keepdims=True) / value.shape[1]
    value_grad = scale * inner - value * (scale * scale * scale) * mean_term
    gain_grad = jnp.sum(grad * value * scale, axis=0)
    return (value_grad, gain_grad)


def per_device(
    tokens, lengths, attention_gain, w_inputs, w_output, feed_gain, w_gate, w_up, w_down, cotangent
):
    count = lax.axis_size("tensor")
    groups = KV // count
    local, width = tokens.shape
    rows = local * count
    low = jnp.bfloat16
    held = tables(lengths[0], rows)
    sequences = lengths.shape[1]
    gain_one = attention_gain.astype(jnp.float32)
    gain_two = feed_gain.astype(jnp.float32)

    places = slot_places()
    base = tokens.astype(jnp.float32)
    first, first_scale = normalize(base, gain_one)
    first = first.astype(low)
    inputs_full = gather_rows(w_inputs)
    first_slots = ring_gather(first)
    output_slots = ring_gather(w_output, {2: [first_slots[1]], 3: [first_slots[2]]})
    output_line = jnp.concatenate(output_slots, 0)
    output_full = gather_columns(output_line)
    gate_full = gather_rows(w_gate)
    up_full = gather_rows(tied(w_up, output_line))
    down_full = gather_columns(tied(w_down, output_line))

    joint = project(first_slots, inputs_full, places)
    heads, query, key, value = attention_forward(joint, held, sequences, groups)
    grad_slots = ring_gather(tied(cotangent, first_slots[-1]))
    heads_own = exchange(to_slots(heads, places, grad_slots[1]))
    heads_own = jnp.concatenate(heads_own, 1)
    mixed = base + dot(heads_own, output_full)
    second, second_scale = normalize(mixed, gain_two)
    second_slots = ring_gather(second.astype(low))
    half = max(count // 2, 1)
    ahead = feed_forward(second_slots[:half], gate_full, up_full)
    rest = feed_forward(second_slots[half:], gate_full, up_full)
    hidden, gate, up = [list(one) + list(two) for one, two in zip(ahead, rest)]
    block_parts = product(hidden, down_full)
    gate_grad, up_grad = feed_backward(grad_slots, down_full, gate, up, block_parts[0])
    block_moving = ring_shift(block_parts[1], 1)
    second_parts = sum_of_products(((gate_grad, gate_full), (up_grad, up_full)), block_moving)
    second_grad, second_back = ring_scatter(second_parts)
    down_grad = sum_columns(weight_grad(hidden, grad_slots, second_parts[0]))
    gate_wgrad = sum_rows(weight_grad(second_slots, gate_grad, second_parts[0]))
    up_wgrad = sum_rows(weight_grad(second_slots, up_grad, second_parts[0]))

    mixed_back, gain_two_part = norm_back(second_grad, mixed, second_scale, gain_two)
    mixed_total = cotangent.astype(jnp.float32) + mixed_back
    branch = mixed_total.astype(low)
    heads_back = dot(branch, output_full, NT).astype(low).reshape(local, count, -1)
    heads_grad = exchange([heads_back[:, slot] for slot in range(count)])
    block_sum, block_back = ring_scatter(block_parts, {2: [second_back[-1]], 3: [heads_grad[-1]]})
    block_out = mixed + block_sum
    heads_grad = from_slots(heads_grad, places, block_back[1])
    joint_grad = attention_backward(query, key, value, heads, heads_grad, held, groups)
    joint_slots = to_slots(joint_grad, places)
    first_parts = sum_of_products(((joint_slots, inputs_full),), block_back[2])
    first_grad, first_back = ring_scatter(first_parts)
    output_sum = scatter_product(heads_own, branch, 1).astype(low)
    output_parts = output_sum.reshape(count, -1, output_sum.shape[1])
    output_grad, _ = ring_scatter([output_parts[slot] for slot in range(count)])
    inputs_grad = scatter_product(jnp.concatenate(first_slots, 0), jnp.concatenate(joint_slots, 0), 0)
    base_back, gain_one_part = norm_back(first_grad, base, first_scale, gain_one)
    tokens_grad = (mixed_total + base_back).astype(low)
    return (
        block_out.astype(low),
        tokens_grad,
        sum_gain(gain_one_part, places),
        inputs_grad,
        output_grad,
        sum_gain(gain_two_part, places),
        gate_wgrad,
        up_wgrad,
        down_grad,
    )


def solution(mesh):
    in_specs = (
        P(("dp", "tensor"), None),
        P("dp", None),
        P(),
        P("dp", "tensor"),
        P("tensor", "dp"),
        P(),
        P("dp", "tensor"),
        P("dp", "tensor"),
        P("tensor", "dp"),
        P(("dp", "tensor"), None),
    )
    out_specs = (
        P(("dp", "tensor"), None),
        P(("dp", "tensor"), None),
        P(("dp", "tensor")),
        P("dp", "tensor"),
        P("tensor", "dp"),
        P(("dp", "tensor")),
        P("dp", "tensor"),
        P("dp", "tensor"),
        P("tensor", "dp"),
    )
    return jax.shard_map(
        per_device, mesh=mesh, in_specs=in_specs, out_specs=out_specs, check_vma=False
    )
```

```python
import math

import jax
import jax.numpy as jnp
from jax import lax
from jax.experimental import pallas as pl
from jax.experimental.pallas import tpu as pltpu
from jax.sharding import PartitionSpec as P

KV = 8
HD = 64
QPK = 4
EPS = 1e-05
THETA = 500000.0
FLOOR = -1e30
LANES = 128
BLOCK = 128
PARTS = 3
VMEM = 56 << 20
HEAVY = 10**12
NT = (((1,), (1,)), ((), ()))
NN = (((1,), (0,)), ((), ()))
TN = (((0,), (0,)), ((), ()))


def layout(lens, rows_count):
    ends = jnp.cumsum(lens)
    rows = jnp.arange(rows_count, dtype=jnp.int32)
    segment = jnp.sum((rows[:, None] >= ends[None, :]).astype(jnp.int32), axis=1)
    starts = ends - lens
    numbers = jnp.arange(lens.shape[0], dtype=jnp.int32)
    picked = jnp.where(segment[:, None] == numbers[None, :], starts[None, :], 0)
    return segment, rows - jnp.sum(picked, axis=1)


def tables(lens, rows_count):
    segment, position = layout(lens, rows_count)
    index = (jnp.arange(LANES, dtype=jnp.int32) % (HD // 2)).astype(jnp.float32)
    inverse = jnp.exp(index * (-2.0 * math.log(THETA) / HD))
    angle = position.astype(jnp.float32)[:, None] * inverse[None, :]
    count = lens.shape[0]
    lane = jnp.arange(LANES, dtype=jnp.int32)[None, :] - HD
    same = lane == segment[:, None]
    inside = (lane >= 0) & (lane < count)
    extra = (lane >= count) & (lane < count + PARTS)
    key_lanes = jnp.where((same & inside) | extra, 1.0, 0.0).astype(jnp.bfloat16)
    query_lanes = jnp.where(inside & ~same, FLOOR, 0.0).astype(jnp.bfloat16)
    return jnp.cos(angle), jnp.sin(angle), query_lanes, key_lanes


def dot(left, right, dims=NN):
    return lax.dot_general(left, right, dims, preferred_element_type=jnp.float32)


def rotate(value, cosine, sine):
    low = lax.broadcasted_iota(jnp.int32, value.shape, 1) % HD < HD // 2
    up = pltpu.roll(value, LANES - HD // 2, 1)
    down = pltpu.roll(value, HD // 2, 1)
    return value * cosine + jnp.where(low, -up, down) * sine


def unrotate(value, cosine, sine):
    low = lax.broadcasted_iota(jnp.int32, value.shape, 1) % HD < HD // 2
    scaled = value * sine
    up = pltpu.roll(scaled, LANES - HD // 2, 1)
    down = pltpu.roll(scaled, HD // 2, 1)
    return value * cosine + jnp.where(low, up, -down)


def split(value, parts):
    out = []
    for _ in range(parts):
        piece = value.astype(jnp.bfloat16).astype(jnp.float32)
        out.append(piece)
        value = value - piece
    return out


def forward_kernel(count, joint, cos, sin, query_lanes, key_lanes, heads, query, key, value):
    rows = joint.shape[0]
    cosine, sine = cos[...], sin[...]
    lane = lax.broadcasted_iota(jnp.int32, (rows, LANES), 1)
    left = lane < HD
    beside = query_lanes[...].astype(jnp.float32)
    for pair in range(QPK // 2):
        both = rotate(joint[:, pair * LANES : (pair + 1) * LANES], cosine, sine) * (1.0 / math.sqrt(HD))
        query[2 * pair] = jnp.where(left, both, beside).astype(jnp.bfloat16)
        query[2 * pair + 1] = jnp.where(left, pltpu.roll(both, HD, 1), beside).astype(jnp.bfloat16)
    last = joint[:, QPK * HD : QPK * HD + LANES]
    key[...] = jnp.where(left, rotate(last, cosine, sine), key_lanes[...].astype(jnp.float32)).astype(
        jnp.bfloat16
    )
    ones = jnp.where((lane >= HD) & (lane < HD + PARTS), 1.0, 0.0)
    value[...] = jnp.where(left, pltpu.roll(last, HD, 1), ones).astype(jnp.bfloat16)
    lower = lax.broadcasted_iota(jnp.int32, (BLOCK, BLOCK), 1) <= lax.broadcasted_iota(
        jnp.int32, (BLOCK, BLOCK), 0
    )
    lower = jnp.concatenate([lower] * QPK, 0)
    narrow = lax.broadcasted_iota(jnp.int32, (QPK * BLOCK, LANES), 1)
    for block in range(rows // BLOCK):
        start = block * BLOCK
        end = start + BLOCK
        own = query[:, start:end, :].reshape(QPK * BLOCK, LANES)
        near = jnp.where(lower, dot(own, key[start:end, :], NT), FLOOR)
        top = jnp.max(near, 1, keepdims=True)
        if block:
            far = dot(own, key[0:start, :], NT)
            top = jnp.maximum(top, jnp.max(far, 1, keepdims=True))
        out = dot(jnp.exp(near - top).astype(jnp.bfloat16), value[start:end, :])
        if block:
            out = out + dot(jnp.exp(far - top).astype(jnp.bfloat16), value[0:start, :])
        total = out[:, HD : HD + 1]
        out = out * (1.0 / total)
        held = own.astype(jnp.float32)
        for part, piece in enumerate(split(top + jnp.log(total), PARTS)):
            held = jnp.where(narrow == HD + count + part, -piece, held)
        query[:, start:end, :] = held.astype(jnp.bfloat16).reshape(QPK, BLOCK, LANES)
        each = [out[head * BLOCK : (head + 1) * BLOCK] for head in range(QPK)]
        half = narrow[:BLOCK] < HD
        for pair in range(QPK // 2):
            heads[start:end, pair * LANES : (pair + 1) * LANES] = jnp.where(
                half, each[2 * pair], pltpu.roll(each[2 * pair + 1], HD, 1)
            ).astype(jnp.bfloat16)


def whole(*shape):
    return pl.BlockSpec(shape, lambda g: (0,) * len(shape))


def grouped(*shape):
    return pl.BlockSpec((None,) + shape, lambda g: (g,) + (0,) * len(shape))


def columns(rows, width):
    return pl.BlockSpec((rows, width), lambda g: (0, g))


def attention_forward(joint, held, count, groups):
    rows = joint.shape[0]
    shape = jax.ShapeDtypeStruct
    low = jnp.bfloat16
    return pl.pallas_call(
        lambda *refs: forward_kernel(count, *refs),
        grid=(groups,),
        in_specs=[columns(rows, (QPK + 2) * HD)] + [whole(rows, LANES)] * 4,
        out_specs=[
            columns(rows, QPK * HD),
            grouped(QPK, rows, LANES),
            grouped(rows, LANES),
            grouped(rows, LANES),
        ],
        out_shape=[
            shape((rows, groups * QPK * HD), low),
            shape((groups, QPK, rows, LANES), low),
            shape((groups, rows, LANES), low),
            shape((groups, rows, LANES), low),
        ],
        compiler_params=pltpu.CompilerParams(vmem_limit_bytes=VMEM),
        cost_estimate=pl.CostEstimate(
            flops=groups * 12 * rows * rows * QPK * HD,
            bytes_accessed=1 << 20,
            transcendentals=0,
        ),
    )(joint, *held)


def backward_kernel(count, *refs):
    query, key, value, heads = refs[:4]
    places, cos, sin = refs[4 + count : 7 + count]
    out, grads, query_grad, key_grad, value_grad = refs[-5:]
    rows = key.shape[0]
    local = rows // count
    for slot in range(count):
        start = pl.multiple_of(places[slot] * local, 16)
        grads[pl.ds(start, local), :] = refs[4 + slot][...]
    key_grad[...] = jnp.zeros_like(key_grad)
    value_grad[...] = jnp.zeros_like(value_grad)
    turned = key[...].astype(jnp.float32).T.astype(jnp.bfloat16)
    upper = lax.broadcasted_iota(jnp.int32, (BLOCK, BLOCK), 0) <= lax.broadcasted_iota(
        jnp.int32, (BLOCK, BLOCK), 1
    )
    upper = jnp.concatenate([upper] * QPK, 1)
    lane = lax.broadcasted_iota(jnp.int32, (QPK * BLOCK, LANES), 1)
    half = lane[:BLOCK] < HD

    def stacked(ref, start, end):
        pieces = []
        for pair in range(QPK // 2):
            both = ref[start:end, pair * LANES : (pair + 1) * LANES].astype(jnp.float32)
            pieces += [both, pltpu.roll(both, HD, 1)]
        return jnp.where(lane < HD, jnp.concatenate(pieces, 0), 0.0)

    for block in range(rows // BLOCK):
        start = block * BLOCK
        end = start + BLOCK
        own = query[:, start:end, :].reshape(QPK * BLOCK, LANES)
        grad = stacked(grads, start, end)
        inner = jnp.sum(grad * stacked(heads, start, end), 1, keepdims=True)
        low = grad.astype(jnp.bfloat16)
        for part, piece in enumerate(split(inner, PARTS)):
            grad = jnp.where(lane == HD + part, -piece, grad)
        beside = grad.astype(jnp.bfloat16)
        turned_grad = None
        for first, last in ([(0, start)] if block else []) + [(start, end)]:
            scores = dot(key[first:last, :], own, NT)
            if first == start:
                scores = jnp.where(upper, scores, FLOOR)
            probs = jnp.exp(scores)
            score_grad = (probs * dot(value[first:last, :], beside, NT)).astype(jnp.bfloat16)
            value_grad[first:last, :] += dot(probs.astype(jnp.bfloat16), low)
            key_grad[first:last, :] += dot(score_grad, own)
            piece = dot(turned[:, first:last], score_grad)
            turned_grad = piece if turned_grad is None else turned_grad + piece
        back = turned_grad.T * (1.0 / math.sqrt(HD))
        each = [back[head * BLOCK : (head + 1) * BLOCK] for head in range(QPK)]
        for pair in range(QPK // 2):
            query_grad[start:end, pair * LANES : (pair + 1) * LANES] = jnp.where(
                half, each[2 * pair], pltpu.roll(each[2 * pair + 1], HD, 1)
            )
    cosine, sine = cos[...], sin[...]
    for pair in range(QPK // 2):
        at = slice(pair * LANES, (pair + 1) * LANES)
        out[:, at] = unrotate(query_grad[:, at], cosine, sine).astype(jnp.bfloat16)
    left = lax.broadcasted_iota(jnp.int32, (rows, LANES), 1) < HD
    key_part = unrotate(jnp.where(left, key_grad[...], 0.0), cosine, sine)
    out[:, QPK * HD : QPK * HD + LANES] = jnp.where(
        left, key_part, pltpu.roll(value_grad[...], HD, 1)
    ).astype(jnp.bfloat16)


def attention_backward(query, key, value, heads, slots, places, held, groups, *earlier):
    rows = key.shape[1]
    wide = (QPK + 2) * HD
    count = len(slots)
    operands = (query, key, value, heads, *slots, places, held[0], held[1])
    return call(
        lambda *refs: backward_kernel(count, *refs),
        groups,
        operands,
        [grouped(QPK, rows, LANES), grouped(rows, LANES), grouped(rows, LANES), columns(rows, QPK * HD)]
        + [columns(rows // count, QPK * HD)] * count
        + [pl.BlockSpec(memory_space=pltpu.SMEM)]
        + [whole(rows, LANES)] * 2,
        columns(rows, wide),
        jax.ShapeDtypeStruct((rows, groups * wide), jnp.bfloat16),
        HEAVY,
        earlier,
        [
            pltpu.VMEM((rows, QPK * HD), jnp.bfloat16),
            pltpu.VMEM((rows, QPK * HD), jnp.float32),
            pltpu.VMEM((rows, LANES), jnp.float32),
            pltpu.VMEM((rows, LANES), jnp.float32),
        ],
    )


def call(kernel, grid, operands, specs, out_specs, out_shape, flops, earlier=(), scratch=()):
    count, extra = len(operands), len(earlier)
    return pl.pallas_call(
        lambda *refs: kernel(*refs[:count], *refs[count + extra :]),
        grid=(grid,),
        in_specs=specs + [pl.BlockSpec(memory_space=pl.ANY)] * extra,
        out_specs=out_specs,
        out_shape=out_shape,
        scratch_shapes=list(scratch),
        compiler_params=pltpu.CompilerParams(vmem_limit_bytes=VMEM),
        cost_estimate=pl.CostEstimate(flops=flops, bytes_accessed=1 << 20, transcendentals=0),
    )(*operands, *earlier)


def column_block(rows, wide):
    return pl.BlockSpec((rows, wide), lambda f: (0, f))


def row_block(wide, width):
    return pl.BlockSpec((wide, width), lambda f: (f, 0))


def low_shape(*shape):
    return jax.ShapeDtypeStruct(shape, jnp.bfloat16)


def block_size(extent):
    return 256 if extent % 256 == 0 else extent


def tied(value, *earlier):
    rows, width = value.shape
    wide = rows // 2 if rows % 32 == 0 else rows

    def kernel(source, target):
        target[...] = source[...]

    block = row_block(wide, width)
    return call(kernel, rows // wide, (value,), [block], block, low_shape(rows, width), 0, earlier)


def tied_sum(left, right, weight, *earlier):
    rows, width = left.shape
    wide = rows // 2 if rows % 32 == 0 else rows

    def kernel(left, right, out):
        out[...] = (left[...].astype(jnp.float32) + right[...].astype(jnp.float32)).astype(out.dtype)

    block = row_block(wide, width)
    return call(
        kernel, rows // wide, (left, right), [block] * 2, block, low_shape(rows, width), weight, earlier
    )


def project(slots, weight, places):
    count = len(slots)
    local, width = slots[0].shape
    extent = weight.shape[1]
    wide = block_size(extent)

    def kernel(*refs):
        places, weight, out = refs[count], refs[count + 1], refs[count + 2]
        for slot in range(count):
            start = pl.multiple_of(places[slot] * local, 16)
            out[pl.ds(start, local), :] = dot(refs[slot][...], weight[...])

    return call(
        kernel,
        extent // wide,
        (*slots, places, weight),
        [whole(local, width)] * count
        + [pl.BlockSpec(memory_space=pltpu.SMEM), column_block(width, wide)],
        column_block(count * local, wide),
        jax.ShapeDtypeStruct((count * local, extent), jnp.float32),
        2 * count * local * width * extent,
    )


def to_slots(value, places, *earlier):
    count = places.shape[0]
    rows, width = value.shape
    local = rows // count

    def kernel(value, places, *out):
        for slot in range(count):
            start = pl.multiple_of(places[slot] * local, 16)
            out[slot][...] = value[pl.ds(start, local), :]

    return call(
        kernel,
        1,
        (value, places),
        [whole(rows, width), pl.BlockSpec(memory_space=pltpu.SMEM)],
        [whole(local, width)] * count,
        [low_shape(local, width)] * count,
        0,
        earlier,
    )


def from_slots(slots, places, *earlier):
    count = len(slots)
    local, width = slots[0].shape

    def kernel(*refs):
        for slot in range(count):
            start = pl.multiple_of(refs[count][slot] * local, 16)
            refs[-1][pl.ds(start, local), :] = refs[slot][...]

    return call(
        kernel,
        1,
        (*slots, places),
        [whole(local, width)] * count + [pl.BlockSpec(memory_space=pltpu.SMEM)],
        whole(count * local, width),
        low_shape(count * local, width),
        0,
        earlier,
    )


def feed_forward(slots, w_gate, w_up, *earlier):
    count = len(slots)
    rows, width = slots[0].shape
    extent = w_gate.shape[1]
    wide = block_size(extent)

    def kernel(*refs):
        w_gate, w_up = refs[count], refs[count + 1]
        out = refs[count + 2 :]
        for slot in range(count):
            one = dot(refs[slot][...], w_gate[...])
            two = dot(refs[slot][...], w_up[...])
            out[slot][...] = (one * jax.nn.sigmoid(one) * two).astype(jnp.bfloat16)
            out[count + slot][...] = one.astype(jnp.bfloat16)
            out[2 * count + slot][...] = two.astype(jnp.bfloat16)

    out = call(
        kernel,
        extent // wide,
        (*slots, w_gate, w_up),
        [whole(rows, width)] * count + [column_block(width, wide)] * 2,
        [column_block(rows, wide)] * (3 * count),
        [low_shape(rows, extent)] * (3 * count),
        4 * count * rows * width * extent,
        earlier,
    )
    return out[:count], out[count : 2 * count], out[2 * count :]


def feed_backward(grads, w_down, gates, ups, *earlier):
    count = len(grads)
    rows, width = grads[0].shape
    extent = w_down.shape[0]
    wide = block_size(extent)

    def kernel(*refs):
        w_down = refs[3 * count]
        out = refs[3 * count + 1 :]
        for slot in range(count):
            hidden_grad = dot(refs[slot][...], w_down[...], NT)
            one = refs[count + slot][...].astype(jnp.float32)
            sigma = jax.nn.sigmoid(one)
            scaled = hidden_grad * sigma
            slope = refs[2 * count + slot][...].astype(jnp.float32) * (1.0 + one * (1.0 - sigma))
            out[slot][...] = (scaled * slope).astype(jnp.bfloat16)
            out[count + slot][...] = (scaled * one).astype(jnp.bfloat16)

    out = call(
        kernel,
        extent // wide,
        (*grads, *gates, *ups, w_down),
        [whole(rows, width)] * count
        + [column_block(rows, wide)] * (2 * count)
        + [row_block(wide, width)],
        [column_block(rows, wide)] * (2 * count),
        [low_shape(rows, extent)] * (2 * count),
        2 * count * rows * width * extent,
        earlier,
    )
    return out[:count], out[count:]


def sum_of_products(terms, *earlier):
    count = len(terms[0][0])
    rows, depth = terms[0][0][0].shape
    extent = terms[0][1].shape[0]
    wide = block_size(extent)
    total = len(terms)

    def kernel(*refs):
        weights = refs[total * count : total * count + total]
        out = refs[total * count + total :]
        for slot in range(count):
            sums = dot(refs[slot][...], weights[0][...], NT)
            for term in range(1, total):
                sums = sums + dot(refs[term * count + slot][...], weights[term][...], NT)
            out[slot][...] = sums.astype(jnp.bfloat16)

    slots = [slot for term in terms for slot in term[0]]
    return call(
        kernel,
        extent // wide,
        (*slots, *[term[1] for term in terms]),
        [whole(rows, depth)] * (total * count) + [row_block(wide, depth)] * total,
        [column_block(rows, wide)] * count,
        [low_shape(rows, extent)] * count,
        2 * total * count * rows * depth * extent,
        earlier,
    )


def product(slots, right, *earlier):
    count = len(slots)
    rows, depth = slots[0].shape
    extent = right.shape[1]
    wide = block_size(extent)

    def kernel(*refs):
        for slot in range(count):
            refs[count + 1 + slot][...] = dot(refs[slot][...], refs[count][...]).astype(jnp.bfloat16)

    return call(
        kernel,
        extent // wide,
        (*slots, right),
        [whole(rows, depth)] * count + [column_block(depth, wide)],
        [column_block(rows, wide)] * count,
        [low_shape(rows, extent)] * count,
        2 * count * rows * depth * extent,
        earlier,
    )


def weight_grad(lefts, rights, *earlier, half=None, into=None):
    count = len(lefts)
    rows, extent = lefts[0].shape
    width = rights[0].shape[1]
    wide = block_size(extent)
    narrow = 512 if width % 512 == 0 else width
    total = 2 * count + (into is not None) + len(earlier)

    def kernel(*refs):
        out, left, right = refs[total:]

        @pl.when(pl.program_id(0) == 0)
        def _():
            for slot in range(count):
                right[slot * rows : (slot + 1) * rows, :] = refs[count + slot][...]

        for slot in range(count):
            left[slot * rows : (slot + 1) * rows, :] = refs[slot][...]
        for start in range(0, width, narrow):
            at = slice(start, start + narrow)
            out[:, at] = dot(left[...], right[:, at], TN).astype(jnp.bfloat16)

    held = () if into is None else (into,)
    return pl.pallas_call(
        kernel,
        grid=(extent // wide,),
        in_specs=[column_block(rows, wide)] * count
        + [whole(rows, width)] * count
        + [pl.BlockSpec(memory_space=pl.ANY)] * (len(held) + len(earlier)),
        out_specs=pl.BlockSpec((wide, width), lambda f: (f, half or 0)),
        out_shape=low_shape(extent, width if half is None else 2 * width),
        input_output_aliases={} if into is None else {2 * count: 0},
        scratch_shapes=[
            pltpu.VMEM((count * rows, wide), jnp.bfloat16),
            pltpu.VMEM((count * rows, width), jnp.bfloat16),
        ],
        compiler_params=pltpu.CompilerParams(vmem_limit_bytes=VMEM),
        cost_estimate=pl.CostEstimate(
            flops=2 * count * rows * width * extent, bytes_accessed=1 << 20, transcendentals=0
        ),
    )(*lefts, *rights, *held, *earlier)


def spread_product(value, weight, places, slots, *earlier):
    count = places.shape[0]
    rows, depth = value.shape
    local = rows // count
    extent = weight.shape[0]
    wide = extent // 2 if extent % 512 == 0 else extent

    def kernel(value, places, weight, *out):
        for at, slot in enumerate(slots):
            start = pl.multiple_of(places[slot] * local, 16)
            out[at][...] = dot(value[pl.ds(start, local), :], weight[...], NT).astype(jnp.bfloat16)

    return call(
        kernel,
        extent // wide,
        (value, places, weight),
        [whole(rows, depth), pl.BlockSpec(memory_space=pltpu.SMEM), row_block(wide, depth)],
        [column_block(local, wide)] * len(slots),
        [low_shape(local, extent)] * len(slots),
        2 * len(slots) * local * depth * extent,
        earlier,
    )


def cube_call(kernel, operands, specs, piece, scratch, flops, earlier):
    count, extra = len(operands), len(earlier)

    def body(me, *refs):
        away, home = refs[count + extra : count + extra + 2]
        value = kernel(*refs[:count], *refs[count + extra + 2 :])
        step = pl.program_id(0)

        @pl.when(step < 4)
        def _():
            away[...] = value

        @pl.when(step >= 4)
        def _():
            home[...] = value

    me = lax.axis_index("dp").astype(jnp.int32).reshape(1)
    return pl.pallas_call(
        body,
        grid_spec=pltpu.PrefetchScalarGridSpec(
            num_scalar_prefetch=1,
            grid=(8,),
            in_specs=specs + [pl.BlockSpec(memory_space=pl.ANY)] * extra,
            out_specs=[
                pl.BlockSpec((None,) + piece, lambda i, me: (jnp.minimum(i, 3), 0, 0)),
                pl.BlockSpec((None,) + piece, lambda i, me: (jnp.maximum(i - 4, 0), 0, 0)),
            ],
            scratch_shapes=scratch,
        ),
        out_shape=[low_shape(4, *piece)] * 2,
        compiler_params=pltpu.CompilerParams(vmem_limit_bytes=VMEM),
        cost_estimate=pl.CostEstimate(flops=flops, bytes_accessed=1 << 20, transcendentals=0),
    )(me, *operands, *earlier)


def cube_place(step, me):
    return jnp.bitwise_xor(me[0], 2 * (step % 4) + 1 - step // 4)


def cube_columns(lefts, right, *earlier):
    count = len(lefts)
    rows, wide = lefts[0].shape
    block = right.shape[1] // 8

    def kernel(*refs):
        left = refs[-1]

        @pl.when(pl.program_id(0) == 0)
        def _():
            for slot in range(count):
                turned = refs[slot][...].astype(jnp.float32).T
                left[slot * wide : (slot + 1) * wide, :] = turned.astype(jnp.bfloat16)

        return dot(left[...], refs[count][...]).astype(jnp.bfloat16)

    fixed = pl.BlockSpec((rows, wide), lambda i, me: (0, 0))
    moving = pl.BlockSpec((rows, block), lambda i, me: (0, cube_place(i, me)))
    scratch = [pltpu.VMEM((count * wide, rows), jnp.bfloat16)]
    flops = 2 * rows * count * wide * right.shape[1]
    piece = (count * wide, block)
    return cube_call(kernel, (*lefts, right), [fixed] * count + [moving], piece, scratch, flops, earlier)


def cube_rows(lefts, right, places, cost, *earlier):
    count = len(lefts)
    rows, width = lefts[0].shape
    extent = right.shape[1]
    block = width // 8

    def kernel(*refs):
        left, turned = refs[-2:]

        @pl.when(pl.program_id(0) == 0)
        def _():
            for slot in range(count):
                start = pl.multiple_of(refs[count + 1][slot] * rows, 16)
                turned[slot * rows : (slot + 1) * rows, :] = refs[count][pl.ds(start, rows), :]

        for slot in range(count):
            left[slot * rows : (slot + 1) * rows, :] = refs[slot][...]
        return dot(left[...], turned[...], TN).astype(jnp.bfloat16)

    moving = pl.BlockSpec((rows, block), lambda i, me: (0, cube_place(i, me)))
    fixed = pl.BlockSpec((count * rows, extent), lambda i, me: (0, 0))
    scratch = [
        pltpu.VMEM((count * rows, block), jnp.bfloat16),
        pltpu.VMEM((count * rows, extent), jnp.bfloat16),
    ]
    specs = [moving] * count + [fixed, pl.BlockSpec(memory_space=pltpu.SMEM)]
    return cube_call(kernel, (*lefts, right, places), specs, (block, extent), scratch, cost, earlier)


def cube_pair(home, arrived, *earlier):
    _, rows, width = home.shape
    half = rows // 2

    def kernel(home, arrived, own, over_x, over_y, top, bottom):
        total = lambda at: (
            home[at].astype(jnp.float32) + arrived[at].astype(jnp.float32)
        ).astype(jnp.bfloat16)
        own[...] = total(0)
        over_x[...] = total(1)
        over_y[...] = total(2)
        corner = total(3)
        top[...] = corner[:half]
        bottom[...] = corner[half:]

    full, part = whole(rows, width), whole(half, width)
    return call(
        kernel,
        1,
        (home, arrived),
        [whole(4, rows, width)] * 2,
        [full] * 3 + [part] * 2,
        [low_shape(rows, width)] * 3 + [low_shape(half, width)] * 2,
        0,
        earlier,
    )


def cube_turn(over_x, over_y, from_x, from_y, *earlier):
    rows, width = over_x.shape
    half = rows // 2

    def kernel(over_x, over_y, from_x, from_y, go_x, go_y):
        both = lambda one, two: (one.astype(jnp.float32) + two.astype(jnp.float32)).astype(jnp.bfloat16)
        go_y[:half, :] = both(over_y[:half, :], from_x[...])
        go_y[half:, :] = over_y[half:, :]
        go_x[:half, :] = over_x[:half, :]
        go_x[half:, :] = both(over_x[half:, :], from_y[...])

    full, part = whole(rows, width), whole(half, width)
    return call(
        kernel,
        1,
        (over_x, over_y, from_x, from_y),
        [full] * 2 + [part] * 2,
        [full] * 2,
        [low_shape(rows, width)] * 2,
        0,
        earlier,
    )


def total_of(terms, dtype, *earlier):
    rows, width = terms[0].shape
    wide = rows // 2 if rows % 32 == 0 else rows

    def kernel(*refs):
        total = refs[0][...].astype(jnp.float32)
        for ref in refs[1:-1]:
            total = total + ref[...].astype(jnp.float32)
        refs[-1][...] = total.astype(dtype)

    block = row_block(wide, width)
    shape = jax.ShapeDtypeStruct((rows, width), dtype)
    return call(kernel, rows // wide, tuple(terms), [block] * len(terms), block, shape, 0, earlier)


def norm_grad(grads, value, gain, beside):
    width = value.shape[1]
    grad = grads[0].astype(jnp.float32)
    for term in grads[1:]:
        grad = grad + term.astype(jnp.float32)
    value = value.astype(jnp.float32)
    scale = lax.rsqrt(jnp.sum(value * value, 1, keepdims=True) * (1.0 / width) + EPS)
    scaled = value * scale
    inner = grad * gain.astype(jnp.float32)
    mean = jnp.sum(inner * scaled, 1, keepdims=True) * (1.0 / width)
    return beside.astype(jnp.float32) + scale * (inner - scaled * mean)


def norm_backward(grads, value, gain, beside, *earlier):
    rows, width = value.shape
    terms = len(grads)
    wide = 96 if rows % 96 == 0 else rows

    def kernel(*refs):
        value, gain, beside, out = refs[terms:]
        grads = [ref[...] for ref in refs[:terms]]
        out[...] = norm_grad(grads, value[...], gain[...], beside[...]).astype(out.dtype)

    block = row_block(wide, width)
    return call(
        kernel,
        rows // wide,
        (*grads, value, gain.reshape(1, width), beside),
        [block] * (terms + 1) + [whole(1, width), block],
        block,
        low_shape(rows, width),
        0,
        earlier,
    )


def norm_split(grads, value, gain, beside, right, count, *earlier):
    rows, width = value.shape
    terms = len(grads)
    wide = right.shape[0] // count

    def kernel(*refs):
        value, gain, beside, right, total, rounded = refs[terms : terms + 6]
        out = refs[terms + 6 :]

        @pl.when(pl.program_id(0) == 0)
        def _():
            for at in [slice(start, start + 96) for start in range(0, rows, 96)] if rows % 96 == 0 else [slice(0, rows)]:
                one = norm_grad([ref[at, :] for ref in refs[:terms]], value[at, :], gain[...], beside[at, :])
                total[at, :] = one
                rounded[at, :] = one.astype(jnp.bfloat16)

        part = dot(rounded[...], right[...], NT).astype(jnp.bfloat16)
        for slot in range(count):

            @pl.when(pl.program_id(0) == slot)
            def _(slot=slot):
                out[slot][...] = part

    block = whole(rows, width)
    out = call(
        kernel,
        count,
        (*grads, value, gain.reshape(1, width), beside, right),
        [block] * (terms + 1) + [whole(1, width), block, row_block(wide, width)],
        [block] * 2 + [whole(rows, wide)] * count,
        [jax.ShapeDtypeStruct((rows, width), jnp.float32), low_shape(rows, width)]
        + [low_shape(rows, wide)] * count,
        HEAVY,
        earlier,
    )
    return out[0], out[1], out[2:]


def widen(terms, weight, part=0, *earlier):
    rows, width = weight.shape
    wide = rows // 2 if rows % 32 == 0 else rows
    count = len(terms)

    def kernel(*refs):
        weight, out, share = refs[count:]
        total = refs[0][...].astype(jnp.float32)
        for ref in refs[1:count]:
            total = total + ref[...].astype(jnp.float32)
        out[...] = total
        share[...] = jnp.sum(total * weight[...].astype(jnp.float32), 1, keepdims=True)

    block = row_block(wide, width)
    return call(
        kernel,
        rows // wide,
        (*terms, weight),
        [pl.BlockSpec((wide, width), lambda f: (f, part))] * count + [block],
        [block, row_block(wide, 1)],
        [jax.ShapeDtypeStruct((rows, width), jnp.float32), jax.ShapeDtypeStruct((rows, 1), jnp.float32)],
        0,
        earlier,
    )


def widen_turned(value, part):
    rows, width = value.shape
    width = width // 2
    wide = 256 if width % 256 == 0 else width
    blocks = width // wide

    def kernel(source, target):
        target[...] = source[...].astype(jnp.float32).T

    return call(
        kernel,
        blocks,
        (value,),
        [pl.BlockSpec((rows, wide), lambda f: (0, part * blocks + f))],
        row_block(wide, rows),
        jax.ShapeDtypeStruct((width, rows), jnp.float32),
        0,
    )


def after(value, *earlier):
    return lax.optimization_barrier((value,) + earlier)[0]


def ring():
    count = lax.axis_size("tensor")
    return [0] + list(range(1, count, 2)) + list(range(2, count, 2))[::-1]


def ring_shift(value, by):
    order = ring()
    count = len(order)
    return lax.ppermute(value, "tensor", [(order[k], order[(k + by) % count]) for k in range(count)])


def slot_places():
    order = ring()
    count = len(order)
    me = lax.axis_index("tensor")
    at = sum(jnp.where(me == device, place, 0) for place, device in enumerate(order))
    back = (at - jnp.arange(count, dtype=jnp.int32)) % count
    return sum(jnp.where(back == place, device, 0) for place, device in enumerate(order)).astype(jnp.int32)


def ring_gather(piece, pauses=()):
    pauses = dict(pauses)
    slots = [piece]
    for step in range(1, lax.axis_size("tensor")):
        last = slots[-1]
        if step in pauses:
            last = tied(last, *pauses[step])
        slots.append(ring_shift(last, 1))
    return slots


def direct_gather(piece):
    return [piece] + [ring_shift(piece, by) for by in range(1, lax.axis_size("tensor"))]


def ring_scatter(parts, pauses=(), heavy=0):
    pauses = dict(pauses)
    count = len(parts)
    arrivals = []
    moving = parts[1]
    for step in range(1, count):
        arrivals.append(ring_shift(moving, 1))
        if step < count - 1:
            if step + 1 in pauses:
                moving = tied_sum(
                    arrivals[-1], parts[step + 1], HEAVY if step + 1 == heavy else 0, *pauses[step + 1]
                )
            else:
                moving = add(arrivals[-1], parts[step + 1])
    return (parts[0], arrivals[-1]), arrivals


def add(left, right):
    return (left.astype(jnp.float32) + right.astype(jnp.float32)).astype(jnp.bfloat16)


def exchange(parts):
    count = len(parts)
    return [parts[0]] + [ring_shift(parts[count - q], q) for q in range(1, count)]


def flip(value, bits):
    count = lax.axis_size("dp")
    return lax.ppermute(value, "dp", [(k, k ^ bits) for k in range(count)])


def cube_pairs(parts, *earlier):
    away, home = parts
    return cube_pair(home, flip(away, 1), *earlier)


def cube_turns(pairs, *earlier):
    _, over_x, over_y, top, bottom = pairs
    return cube_turn(over_x, over_y, flip(top, 2), flip(bottom, 4), *earlier)


def cube_terms(pairs, turns):
    return (pairs[0], flip(turns[0], 2), flip(turns[1], 4))


def cube_total(pairs, turns, dtype, *earlier):
    return total_of(cube_terms(pairs, turns), dtype, *earlier)


def gather_rows(piece):
    return lax.all_gather(piece, "dp", axis=0, tiled=True)


def gather_columns(piece):
    return lax.all_gather(piece, "dp", axis=1, tiled=True)


def sum_rows(value):
    return lax.psum_scatter(value, "dp", scatter_dimension=0, tiled=True)


def sum_columns(value):
    return lax.psum_scatter(value, "dp", scatter_dimension=1, tiled=True)


def gain_sums(shares, gains, places):
    count = places.shape[0]
    rows = shares[0].shape[0]
    start = lax.axis_index("dp") * rows
    own = [share[:, 0] / lax.dynamic_slice_in_dim(gain, start, rows, 0) for share, gain in zip(shares, gains)]
    cut = jnp.stack(own).reshape(len(own), count, -1)
    pieces = [lax.dynamic_index_in_dim(cut, places[slot], 1, False) for slot in range(count)]
    return sum(exchange(pieces))


def normalize(value, gain):
    scale = lax.rsqrt(jnp.mean(value * value, axis=1, keepdims=True) + EPS)
    return (value * scale * gain[None, :], scale)


def per_device(
    tokens, lengths, attention_gain, w_inputs, w_output, feed_gain, w_gate, w_up, w_down, cotangent
):
    count = lax.axis_size("tensor")
    groups = KV // count
    local, width = tokens.shape
    rows = local * count
    low = jnp.bfloat16
    held = tables(lengths[0], rows)
    sequences = lengths.shape[1]
    gain_one = attention_gain.astype(jnp.float32)
    gain_two = feed_gain.astype(jnp.float32)

    places = slot_places()
    base = tokens.astype(jnp.float32)
    first = normalize(base, gain_one)[0].astype(low)
    inputs_full = gather_rows(w_inputs)
    first_slots = ring_gather(first)
    output_line = jnp.concatenate(direct_gather(w_output), 0)
    output_full = gather_columns(output_line)
    gate_full = gather_rows(w_gate)
    up_full = gather_rows(w_up)
    down_full = gather_columns(w_down)

    joint = project(first_slots, inputs_full, places)
    heads, query, key, value = attention_forward(joint, held, sequences, groups)
    grad_slots = ring_gather(tied(cotangent, first_slots[-1]))
    heads_own = exchange(to_slots(heads, places, grad_slots[1]))
    mixed = base + dot(jnp.concatenate(heads_own, 1), output_full)
    second = normalize(mixed, gain_two)[0].astype(low)
    second_slots = ring_gather(second)
    half = max(count // 2, 1)
    ahead = feed_forward(second_slots[:half], gate_full, up_full)
    rest = feed_forward(second_slots[half:], gate_full, up_full)
    hidden, gate, up = [list(one) + list(two) for one, two in zip(ahead, rest)]
    block_parts = product(hidden, down_full)
    gate_grad, up_grad = feed_backward(grad_slots, down_full, gate, up, block_parts[0])
    block_moving = ring_shift(block_parts[1], 1)
    pick = lambda slots: ((([gate_grad[s] for s in slots]), gate_full), ([up_grad[s] for s in slots], up_full))
    part_one = sum_of_products(pick([1]), block_moving)
    others = [0] + list(range(2, count))
    part_others = sum_of_products(pick(others), part_one[0])
    second_parts = [part_others[0], part_one[0]] + list(part_others[1:])
    second_early = ring_shift(second_parts[1], 1)
    gate_wpart = weight_grad(second_slots, gate_grad, second_early)
    gate_wgrad = sum_rows(gate_wpart)
    second_grad, second_back = ring_scatter(second_parts, {3: [gate_wpart]}, 3)
    up_wpart = weight_grad(second_slots, up_grad, second_back[1], half=0)

    mixed_total, branch, heads_back = norm_split(
        second_grad, mixed, gain_two, cotangent, output_full, count, up_wpart
    )
    heads_grad = exchange(heads_back)
    both_wpart = weight_grad(grad_slots, hidden, branch, half=1, into=up_wpart)
    both_wgrad = sum_rows(both_wpart)
    block_sum, block_back = ring_scatter(block_parts, {2: [second_back[-1]], 3: [heads_grad[-1]]})
    cube = lax.axis_size("dp") == 8
    output_parts = cube_columns(heads_own, branch, both_wpart) if cube else ()
    joint_grad = attention_backward(
        query, key, value, heads, heads_grad, places, held, groups, block_back[1], both_wpart, *output_parts[:1]
    )
    first_one = spread_product(joint_grad, inputs_full, places, [1], block_back[2])
    first_others = spread_product(joint_grad, inputs_full, places, others, first_one[0])
    first_parts = [first_others[0], first_one[0]] + list(first_others[1:])
    gate_wgrad, gate_share = widen([gate_wgrad], w_gate)
    if cube:
        output_pairs = cube_pairs(output_parts, first_one[0])
        output_turns = cube_turns(output_pairs)
        inputs_parts = cube_rows(first_slots, joint_grad, places, HEAVY, output_pairs[0])
        second_pause = [output_turns[0], inputs_parts[0]]
        first_next = tied_sum(ring_shift(first_parts[1], 1), first_parts[2], 0, *second_pause)
        inputs_pairs = cube_pairs(inputs_parts, first_next)
        third_pause = [inputs_pairs[0], gate_wgrad]
        first_last = tied_sum(ring_shift(first_next, 1), first_parts[3], 0, *third_pause)
        inputs_turns = cube_turns(inputs_pairs, first_last)
        output_sum = cube_total(output_pairs, output_turns, low, first_last)
        first_grad, first_back = ring_scatter(first_parts, {2: second_pause, 3: third_pause})
        block_out = total_of((*block_sum, mixed), low, first_last)
        inputs_grad, inputs_share = widen(cube_terms(inputs_pairs, inputs_turns), w_inputs)
    else:
        first_grad, first_back = ring_scatter(first_parts)
        block_out = total_of((*block_sum, mixed), low)
        output_sum = sum_columns(weight_grad([jnp.concatenate(heads_own, 1)], [branch]))
        inputs_grad = sum_rows(weight_grad(first_slots, to_slots(joint_grad, places)))
        inputs_grad, inputs_share = widen([inputs_grad], w_inputs)
    output_cut = output_sum.reshape(count, -1, output_sum.shape[1])
    output_grad = total_of(exchange([output_cut[slot] for slot in range(count)]), jnp.float32)
    up_wgrad, up_share = widen([both_wgrad], w_up)
    down_grad = widen_turned(both_wgrad, 1)
    gain_grads = gain_sums([inputs_share, gate_share + up_share], [gain_one, gain_two], places)
    tokens_grad = norm_backward(first_grad, tokens, gain_one, mixed_total)
    return (
        block_out,
        tokens_grad,
        gain_grads[0],
        inputs_grad,
        output_grad,
        gain_grads[1],
        gate_wgrad,
        up_wgrad,
        down_grad,
    )


def solution(mesh):
    in_specs = (
        P(("dp", "tensor"), None),
        P("dp", None),
        P(),
        P("dp", "tensor"),
        P("tensor", "dp"),
        P(),
        P("dp", "tensor"),
        P("dp", "tensor"),
        P("tensor", "dp"),
        P(("dp", "tensor"), None),
    )
    out_specs = (
        P(("dp", "tensor"), None),
        P(("dp", "tensor"), None),
        P(("dp", "tensor")),
        P("dp", "tensor"),
        P("tensor", "dp"),
        P(("dp", "tensor")),
        P("dp", "tensor"),
        P("dp", "tensor"),
        P("tensor", "dp"),
    )
    return jax.shard_map(
        per_device, mesh=mesh, in_specs=in_specs, out_specs=out_specs, check_vma=False
    )
```

```python
import math

import jax
import jax.numpy as jnp
from jax import lax
from jax.experimental import pallas as pl
from jax.experimental.pallas import tpu as pltpu
from jax.sharding import PartitionSpec as P

KV = 8
HD = 64
QPK = 4
EPS = 1e-05
THETA = 500000.0
FLOOR = -1e30
LANES = 128
BLOCK = 128
PARTS = 3
VMEM = 56 << 20
HEAVY = 10**12
NT = (((1,), (1,)), ((), ()))
NN = (((1,), (0,)), ((), ()))
TN = (((0,), (0,)), ((), ()))


def layout(lens, rows_count):
    ends = jnp.cumsum(lens)
    rows = jnp.arange(rows_count, dtype=jnp.int32)
    segment = jnp.sum((rows[:, None] >= ends[None, :]).astype(jnp.int32), axis=1)
    starts = ends - lens
    numbers = jnp.arange(lens.shape[0], dtype=jnp.int32)
    picked = jnp.where(segment[:, None] == numbers[None, :], starts[None, :], 0)
    return segment, rows - jnp.sum(picked, axis=1)


def tables(lens, rows_count):
    segment, position = layout(lens, rows_count)
    index = (jnp.arange(LANES, dtype=jnp.int32) % (HD // 2)).astype(jnp.float32)
    inverse = jnp.exp(index * (-2.0 * math.log(THETA) / HD))
    angle = position.astype(jnp.float32)[:, None] * inverse[None, :]
    count = lens.shape[0]
    lane = jnp.arange(LANES, dtype=jnp.int32)[None, :] - HD
    same = lane == segment[:, None]
    inside = (lane >= 0) & (lane < count)
    extra = (lane >= count) & (lane < count + PARTS)
    key_lanes = jnp.where((same & inside) | extra, 1.0, 0.0).astype(jnp.bfloat16)
    query_lanes = jnp.where(inside & ~same, FLOOR, 0.0).astype(jnp.bfloat16)
    return jnp.cos(angle), jnp.sin(angle), query_lanes, key_lanes


def dot(left, right, dims=NN):
    return lax.dot_general(left, right, dims, preferred_element_type=jnp.float32)


def rotate(value, cosine, sine):
    low = lax.broadcasted_iota(jnp.int32, value.shape, 1) % HD < HD // 2
    up = pltpu.roll(value, LANES - HD // 2, 1)
    down = pltpu.roll(value, HD // 2, 1)
    return value * cosine + jnp.where(low, -up, down) * sine


def unrotate(value, cosine, sine):
    low = lax.broadcasted_iota(jnp.int32, value.shape, 1) % HD < HD // 2
    scaled = value * sine
    up = pltpu.roll(scaled, LANES - HD // 2, 1)
    down = pltpu.roll(scaled, HD // 2, 1)
    return value * cosine + jnp.where(low, up, -down)


def split(value, parts):
    out = []
    for _ in range(parts):
        piece = value.astype(jnp.bfloat16).astype(jnp.float32)
        out.append(piece)
        value = value - piece
    return out


def forward_kernel(count, joint, cos, sin, query_lanes, key_lanes, heads, query, key, value):
    rows = joint.shape[0]
    cosine, sine = cos[...], sin[...]
    lane = lax.broadcasted_iota(jnp.int32, (rows, LANES), 1)
    left = lane < HD
    beside = query_lanes[...].astype(jnp.float32)
    for pair in range(QPK // 2):
        both = rotate(joint[:, pair * LANES : (pair + 1) * LANES], cosine, sine) * (1.0 / math.sqrt(HD))
        query[2 * pair] = jnp.where(left, both, beside).astype(jnp.bfloat16)
        query[2 * pair + 1] = jnp.where(left, pltpu.roll(both, HD, 1), beside).astype(jnp.bfloat16)
    last = joint[:, QPK * HD : QPK * HD + LANES]
    key[...] = jnp.where(left, rotate(last, cosine, sine), key_lanes[...].astype(jnp.float32)).astype(
        jnp.bfloat16
    )
    ones = jnp.where((lane >= HD) & (lane < HD + PARTS), 1.0, 0.0)
    value[...] = jnp.where(left, pltpu.roll(last, HD, 1), ones).astype(jnp.bfloat16)
    lower = lax.broadcasted_iota(jnp.int32, (BLOCK, BLOCK), 1) <= lax.broadcasted_iota(
        jnp.int32, (BLOCK, BLOCK), 0
    )
    lower = jnp.concatenate([lower] * QPK, 0)
    narrow = lax.broadcasted_iota(jnp.int32, (QPK * BLOCK, LANES), 1)
    for block in range(rows // BLOCK):
        start = block * BLOCK
        end = start + BLOCK
        own = query[:, start:end, :].reshape(QPK * BLOCK, LANES)
        near = jnp.where(lower, dot(own, key[start:end, :], NT), FLOOR)
        top = jnp.max(near, 1, keepdims=True)
        if block:
            far = dot(own, key[0:start, :], NT)
            top = jnp.maximum(top, jnp.max(far, 1, keepdims=True))
        out = dot(jnp.exp(near - top).astype(jnp.bfloat16), value[start:end, :])
        if block:
            out = out + dot(jnp.exp(far - top).astype(jnp.bfloat16), value[0:start, :])
        total = out[:, HD : HD + 1]
        out = out * (1.0 / total)
        held = own.astype(jnp.float32)
        for part, piece in enumerate(split(top + jnp.log(total), PARTS)):
            held = jnp.where(narrow == HD + count + part, -piece, held)
        query[:, start:end, :] = held.astype(jnp.bfloat16).reshape(QPK, BLOCK, LANES)
        each = [out[head * BLOCK : (head + 1) * BLOCK] for head in range(QPK)]
        half = narrow[:BLOCK] < HD
        for pair in range(QPK // 2):
            heads[start:end, pair * LANES : (pair + 1) * LANES] = jnp.where(
                half, each[2 * pair], pltpu.roll(each[2 * pair + 1], HD, 1)
            ).astype(jnp.bfloat16)


def whole(*shape):
    return pl.BlockSpec(shape, lambda g: (0,) * len(shape))


def grouped(*shape):
    return pl.BlockSpec((None,) + shape, lambda g: (g,) + (0,) * len(shape))


def columns(rows, width):
    return pl.BlockSpec((rows, width), lambda g: (0, g))


def attention_forward(joint, held, count, groups):
    rows = joint.shape[0]
    shape = jax.ShapeDtypeStruct
    low = jnp.bfloat16
    return pl.pallas_call(
        lambda *refs: forward_kernel(count, *refs),
        grid=(groups,),
        in_specs=[columns(rows, (QPK + 2) * HD)] + [whole(rows, LANES)] * 4,
        out_specs=[
            columns(rows, QPK * HD),
            grouped(QPK, rows, LANES),
            grouped(rows, LANES),
            grouped(rows, LANES),
        ],
        out_shape=[
            shape((rows, groups * QPK * HD), low),
            shape((groups, QPK, rows, LANES), low),
            shape((groups, rows, LANES), low),
            shape((groups, rows, LANES), low),
        ],
        compiler_params=pltpu.CompilerParams(vmem_limit_bytes=VMEM),
        cost_estimate=pl.CostEstimate(
            flops=groups * 12 * rows * rows * QPK * HD,
            bytes_accessed=1 << 20,
            transcendentals=0,
        ),
    )(joint, *held)


def backward_kernel(count, *refs):
    query, key, value, heads = refs[:4]
    places, cos, sin = refs[4 + count : 7 + count]
    out, grads, query_grad, key_grad, value_grad = refs[-5:]
    rows = key.shape[0]
    local = rows // count
    for slot in range(count):
        start = pl.multiple_of(places[slot] * local, 16)
        grads[pl.ds(start, local), :] = refs[4 + slot][...]
    key_grad[...] = jnp.zeros_like(key_grad)
    value_grad[...] = jnp.zeros_like(value_grad)
    turned = key[...].astype(jnp.float32).T.astype(jnp.bfloat16)
    upper = lax.broadcasted_iota(jnp.int32, (BLOCK, BLOCK), 0) <= lax.broadcasted_iota(
        jnp.int32, (BLOCK, BLOCK), 1
    )
    upper = jnp.concatenate([upper] * QPK, 1)
    lane = lax.broadcasted_iota(jnp.int32, (QPK * BLOCK, LANES), 1)
    half = lane[:BLOCK] < HD

    def stacked(ref, start, end):
        pieces = []
        for pair in range(QPK // 2):
            both = ref[start:end, pair * LANES : (pair + 1) * LANES].astype(jnp.float32)
            pieces += [both, pltpu.roll(both, HD, 1)]
        return jnp.where(lane < HD, jnp.concatenate(pieces, 0), 0.0)

    for block in range(rows // BLOCK):
        start = block * BLOCK
        end = start + BLOCK
        own = query[:, start:end, :].reshape(QPK * BLOCK, LANES)
        grad = stacked(grads, start, end)
        inner = jnp.sum(grad * stacked(heads, start, end), 1, keepdims=True)
        low = grad.astype(jnp.bfloat16)
        for part, piece in enumerate(split(inner, PARTS)):
            grad = jnp.where(lane == HD + part, -piece, grad)
        beside = grad.astype(jnp.bfloat16)
        turned_grad = None
        for first, last in ([(0, start)] if block else []) + [(start, end)]:
            scores = dot(key[first:last, :], own, NT)
            if first == start:
                scores = jnp.where(upper, scores, FLOOR)
            probs = jnp.exp(scores)
            score_grad = (probs * dot(value[first:last, :], beside, NT)).astype(jnp.bfloat16)
            value_grad[first:last, :] += dot(probs.astype(jnp.bfloat16), low)
            key_grad[first:last, :] += dot(score_grad, own)
            piece = dot(turned[:, first:last], score_grad)
            turned_grad = piece if turned_grad is None else turned_grad + piece
        back = turned_grad.T * (1.0 / math.sqrt(HD))
        each = [back[head * BLOCK : (head + 1) * BLOCK] for head in range(QPK)]
        for pair in range(QPK // 2):
            query_grad[start:end, pair * LANES : (pair + 1) * LANES] = jnp.where(
                half, each[2 * pair], pltpu.roll(each[2 * pair + 1], HD, 1)
            )
    cosine, sine = cos[...], sin[...]
    for pair in range(QPK // 2):
        at = slice(pair * LANES, (pair + 1) * LANES)
        out[:, at] = unrotate(query_grad[:, at], cosine, sine).astype(jnp.bfloat16)
    left = lax.broadcasted_iota(jnp.int32, (rows, LANES), 1) < HD
    key_part = unrotate(jnp.where(left, key_grad[...], 0.0), cosine, sine)
    out[:, QPK * HD : QPK * HD + LANES] = jnp.where(
        left, key_part, pltpu.roll(value_grad[...], HD, 1)
    ).astype(jnp.bfloat16)


def attention_backward(query, key, value, heads, slots, places, held, groups, *earlier):
    rows = key.shape[1]
    wide = (QPK + 2) * HD
    count = len(slots)
    operands = (query, key, value, heads, *slots, places, held[0], held[1])
    return call(
        lambda *refs: backward_kernel(count, *refs),
        groups,
        operands,
        [grouped(QPK, rows, LANES), grouped(rows, LANES), grouped(rows, LANES), columns(rows, QPK * HD)]
        + [columns(rows // count, QPK * HD)] * count
        + [pl.BlockSpec(memory_space=pltpu.SMEM)]
        + [whole(rows, LANES)] * 2,
        columns(rows, wide),
        jax.ShapeDtypeStruct((rows, groups * wide), jnp.bfloat16),
        HEAVY,
        earlier,
        [
            pltpu.VMEM((rows, QPK * HD), jnp.bfloat16),
            pltpu.VMEM((rows, QPK * HD), jnp.float32),
            pltpu.VMEM((rows, LANES), jnp.float32),
            pltpu.VMEM((rows, LANES), jnp.float32),
        ],
    )


def call(kernel, grid, operands, specs, out_specs, out_shape, flops, earlier=(), scratch=()):
    count, extra = len(operands), len(earlier)
    return pl.pallas_call(
        lambda *refs: kernel(*refs[:count], *refs[count + extra :]),
        grid=(grid,),
        in_specs=specs + [pl.BlockSpec(memory_space=pl.ANY)] * extra,
        out_specs=out_specs,
        out_shape=out_shape,
        scratch_shapes=list(scratch),
        compiler_params=pltpu.CompilerParams(vmem_limit_bytes=VMEM),
        cost_estimate=pl.CostEstimate(flops=flops, bytes_accessed=1 << 20, transcendentals=0),
    )(*operands, *earlier)


def column_block(rows, wide):
    return pl.BlockSpec((rows, wide), lambda f: (0, f))


def row_block(wide, width):
    return pl.BlockSpec((wide, width), lambda f: (f, 0))


def low_shape(*shape):
    return jax.ShapeDtypeStruct(shape, jnp.bfloat16)


def block_size(extent):
    return 256 if extent % 256 == 0 else extent


def tied(value, *earlier):
    rows, width = value.shape
    wide = rows // 2 if rows % 32 == 0 else rows

    def kernel(source, target):
        target[...] = source[...]

    block = row_block(wide, width)
    return call(kernel, rows // wide, (value,), [block], block, low_shape(rows, width), 0, earlier)


def tied_sum(left, right, weight, *earlier):
    rows, width = left.shape
    wide = rows // 2 if rows % 32 == 0 else rows

    def kernel(left, right, out):
        out[...] = (left[...].astype(jnp.float32) + right[...].astype(jnp.float32)).astype(out.dtype)

    block = row_block(wide, width)
    return call(
        kernel, rows // wide, (left, right), [block] * 2, block, low_shape(rows, width), weight, earlier
    )


def project(slots, weight, places):
    count = len(slots)
    local, width = slots[0].shape
    extent = weight.shape[1]
    wide = block_size(extent)

    def kernel(*refs):
        places, weight, out = refs[count], refs[count + 1], refs[count + 2]
        for slot in range(count):
            start = pl.multiple_of(places[slot] * local, 16)
            out[pl.ds(start, local), :] = dot(refs[slot][...], weight[...])

    return call(
        kernel,
        extent // wide,
        (*slots, places, weight),
        [whole(local, width)] * count
        + [pl.BlockSpec(memory_space=pltpu.SMEM), column_block(width, wide)],
        column_block(count * local, wide),
        jax.ShapeDtypeStruct((count * local, extent), jnp.float32),
        2 * count * local * width * extent,
    )


def to_slots(value, places, *earlier):
    count = places.shape[0]
    rows, width = value.shape
    local = rows // count

    def kernel(value, places, *out):
        for slot in range(count):
            start = pl.multiple_of(places[slot] * local, 16)
            out[slot][...] = value[pl.ds(start, local), :]

    return call(
        kernel,
        1,
        (value, places),
        [whole(rows, width), pl.BlockSpec(memory_space=pltpu.SMEM)],
        [whole(local, width)] * count,
        [low_shape(local, width)] * count,
        0,
        earlier,
    )


def from_slots(slots, places, *earlier):
    count = len(slots)
    local, width = slots[0].shape

    def kernel(*refs):
        for slot in range(count):
            start = pl.multiple_of(refs[count][slot] * local, 16)
            refs[-1][pl.ds(start, local), :] = refs[slot][...]

    return call(
        kernel,
        1,
        (*slots, places),
        [whole(local, width)] * count + [pl.BlockSpec(memory_space=pltpu.SMEM)],
        whole(count * local, width),
        low_shape(count * local, width),
        0,
        earlier,
    )


def feed_forward(slots, w_gate, w_up, *earlier):
    count = len(slots)
    rows, width = slots[0].shape
    extent = w_gate.shape[1]
    wide = block_size(extent)

    def kernel(*refs):
        w_gate, w_up = refs[count], refs[count + 1]
        out = refs[count + 2 :]
        for slot in range(count):
            one = dot(refs[slot][...], w_gate[...])
            two = dot(refs[slot][...], w_up[...])
            out[slot][...] = (one * jax.nn.sigmoid(one) * two).astype(jnp.bfloat16)
            out[count + slot][...] = one.astype(jnp.bfloat16)
            out[2 * count + slot][...] = two.astype(jnp.bfloat16)

    out = call(
        kernel,
        extent // wide,
        (*slots, w_gate, w_up),
        [whole(rows, width)] * count + [column_block(width, wide)] * 2,
        [column_block(rows, wide)] * (3 * count),
        [low_shape(rows, extent)] * (3 * count),
        4 * count * rows * width * extent,
        earlier,
    )
    return out[:count], out[count : 2 * count], out[2 * count :]


def feed_backward(grads, w_down, gates, ups, *earlier):
    count = len(grads)
    rows, width = grads[0].shape
    extent = w_down.shape[0]
    wide = block_size(extent)

    def kernel(*refs):
        w_down = refs[3 * count]
        out = refs[3 * count + 1 :]
        for slot in range(count):
            hidden_grad = dot(refs[slot][...], w_down[...], NT)
            one = refs[count + slot][...].astype(jnp.float32)
            sigma = jax.nn.sigmoid(one)
            scaled = hidden_grad * sigma
            slope = refs[2 * count + slot][...].astype(jnp.float32) * (1.0 + one * (1.0 - sigma))
            out[slot][...] = (scaled * slope).astype(jnp.bfloat16)
            out[count + slot][...] = (scaled * one).astype(jnp.bfloat16)

    out = call(
        kernel,
        extent // wide,
        (*grads, *gates, *ups, w_down),
        [whole(rows, width)] * count
        + [column_block(rows, wide)] * (2 * count)
        + [row_block(wide, width)],
        [column_block(rows, wide)] * (2 * count),
        [low_shape(rows, extent)] * (2 * count),
        2 * count * rows * width * extent,
        earlier,
    )
    return out[:count], out[count:]


def sum_of_products(terms, *earlier):
    count = len(terms[0][0])
    rows, depth = terms[0][0][0].shape
    extent = terms[0][1].shape[0]
    wide = block_size(extent)
    total = len(terms)

    def kernel(*refs):
        weights = refs[total * count : total * count + total]
        out = refs[total * count + total :]
        for slot in range(count):
            sums = dot(refs[slot][...], weights[0][...], NT)
            for term in range(1, total):
                sums = sums + dot(refs[term * count + slot][...], weights[term][...], NT)
            out[slot][...] = sums.astype(jnp.bfloat16)

    slots = [slot for term in terms for slot in term[0]]
    return call(
        kernel,
        extent // wide,
        (*slots, *[term[1] for term in terms]),
        [whole(rows, depth)] * (total * count) + [row_block(wide, depth)] * total,
        [column_block(rows, wide)] * count,
        [low_shape(rows, extent)] * count,
        2 * total * count * rows * depth * extent,
        earlier,
    )


def product(slots, right, *earlier):
    count = len(slots)
    rows, depth = slots[0].shape
    extent = right.shape[1]
    wide = block_size(extent)

    def kernel(*refs):
        for slot in range(count):
            refs[count + 1 + slot][...] = dot(refs[slot][...], refs[count][...]).astype(jnp.bfloat16)

    return call(
        kernel,
        extent // wide,
        (*slots, right),
        [whole(rows, depth)] * count + [column_block(depth, wide)],
        [column_block(rows, wide)] * count,
        [low_shape(rows, extent)] * count,
        2 * count * rows * depth * extent,
        earlier,
    )


def weight_grad(lefts, rights, *earlier, half=None, into=None):
    count = len(lefts)
    rows, extent = lefts[0].shape
    width = rights[0].shape[1]
    wide = block_size(extent)
    narrow = 512 if width % 512 == 0 else width
    total = 2 * count + (into is not None) + len(earlier)

    def kernel(*refs):
        out, left, right = refs[total:]

        @pl.when(pl.program_id(0) == 0)
        def _():
            for slot in range(count):
                right[slot * rows : (slot + 1) * rows, :] = refs[count + slot][...]

        for slot in range(count):
            left[slot * rows : (slot + 1) * rows, :] = refs[slot][...]
        for start in range(0, width, narrow):
            at = slice(start, start + narrow)
            out[:, at] = dot(left[...], right[:, at], TN).astype(jnp.bfloat16)

    held = () if into is None else (into,)
    return pl.pallas_call(
        kernel,
        grid=(extent // wide,),
        in_specs=[column_block(rows, wide)] * count
        + [whole(rows, width)] * count
        + [pl.BlockSpec(memory_space=pl.ANY)] * (len(held) + len(earlier)),
        out_specs=pl.BlockSpec((wide, width), lambda f: (f, half or 0)),
        out_shape=low_shape(extent, width if half is None else 2 * width),
        input_output_aliases={} if into is None else {2 * count: 0},
        scratch_shapes=[
            pltpu.VMEM((count * rows, wide), jnp.bfloat16),
            pltpu.VMEM((count * rows, width), jnp.bfloat16),
        ],
        compiler_params=pltpu.CompilerParams(vmem_limit_bytes=VMEM),
        cost_estimate=pl.CostEstimate(
            flops=2 * count * rows * width * extent, bytes_accessed=1 << 20, transcendentals=0
        ),
    )(*lefts, *rights, *held, *earlier)


def spread_product(value, weight, places, slots, *earlier):
    count = places.shape[0]
    rows, depth = value.shape
    local = rows // count
    extent = weight.shape[0]
    wide = extent // 2 if extent % 512 == 0 else extent

    def kernel(value, places, weight, *out):
        for at, slot in enumerate(slots):
            start = pl.multiple_of(places[slot] * local, 16)
            out[at][...] = dot(value[pl.ds(start, local), :], weight[...], NT).astype(jnp.bfloat16)

    return call(
        kernel,
        extent // wide,
        (value, places, weight),
        [whole(rows, depth), pl.BlockSpec(memory_space=pltpu.SMEM), row_block(wide, depth)],
        [column_block(local, wide)] * len(slots),
        [low_shape(local, extent)] * len(slots),
        2 * len(slots) * local * depth * extent,
        earlier,
    )


def cube_call(kernel, operands, specs, piece, scratch, flops, earlier):
    count, extra = len(operands), len(earlier)

    def body(me, *refs):
        away, home = refs[count + extra : count + extra + 2]
        value = kernel(*refs[:count], *refs[count + extra + 2 :])
        step = pl.program_id(0)

        @pl.when(step < 4)
        def _():
            away[...] = value

        @pl.when(step >= 4)
        def _():
            home[...] = value

    me = lax.axis_index("dp").astype(jnp.int32).reshape(1)
    return pl.pallas_call(
        body,
        grid_spec=pltpu.PrefetchScalarGridSpec(
            num_scalar_prefetch=1,
            grid=(8,),
            in_specs=specs + [pl.BlockSpec(memory_space=pl.ANY)] * extra,
            out_specs=[
                pl.BlockSpec((None,) + piece, lambda i, me: (jnp.minimum(i, 3), 0, 0)),
                pl.BlockSpec((None,) + piece, lambda i, me: (jnp.maximum(i - 4, 0), 0, 0)),
            ],
            scratch_shapes=scratch,
        ),
        out_shape=[low_shape(4, *piece)] * 2,
        compiler_params=pltpu.CompilerParams(vmem_limit_bytes=VMEM),
        cost_estimate=pl.CostEstimate(flops=flops, bytes_accessed=1 << 20, transcendentals=0),
    )(me, *operands, *earlier)


def cube_place(step, me):
    return jnp.bitwise_xor(me[0], 2 * (step % 4) + 1 - step // 4)


def cube_columns(lefts, right, *earlier):
    count = len(lefts)
    rows, wide = lefts[0].shape
    block = right.shape[1] // 8

    def kernel(*refs):
        left = refs[-1]

        @pl.when(pl.program_id(0) == 0)
        def _():
            for slot in range(count):
                turned = refs[slot][...].astype(jnp.float32).T
                left[slot * wide : (slot + 1) * wide, :] = turned.astype(jnp.bfloat16)

        return dot(left[...], refs[count][...]).astype(jnp.bfloat16)

    fixed = pl.BlockSpec((rows, wide), lambda i, me: (0, 0))
    moving = pl.BlockSpec((rows, block), lambda i, me: (0, cube_place(i, me)))
    scratch = [pltpu.VMEM((count * wide, rows), jnp.bfloat16)]
    flops = 2 * rows * count * wide * right.shape[1]
    piece = (count * wide, block)
    return cube_call(kernel, (*lefts, right), [fixed] * count + [moving], piece, scratch, flops, earlier)


def cube_rows(lefts, right, places, cost, *earlier):
    count = len(lefts)
    rows, width = lefts[0].shape
    extent = right.shape[1]
    block = width // 8

    def kernel(*refs):
        left, turned = refs[-2:]

        @pl.when(pl.program_id(0) == 0)
        def _():
            for slot in range(count):
                start = pl.multiple_of(refs[count + 1][slot] * rows, 16)
                turned[slot * rows : (slot + 1) * rows, :] = refs[count][pl.ds(start, rows), :]

        for slot in range(count):
            left[slot * rows : (slot + 1) * rows, :] = refs[slot][...]
        return dot(left[...], turned[...], TN).astype(jnp.bfloat16)

    moving = pl.BlockSpec((rows, block), lambda i, me: (0, cube_place(i, me)))
    fixed = pl.BlockSpec((count * rows, extent), lambda i, me: (0, 0))
    scratch = [
        pltpu.VMEM((count * rows, block), jnp.bfloat16),
        pltpu.VMEM((count * rows, extent), jnp.bfloat16),
    ]
    specs = [moving] * count + [fixed, pl.BlockSpec(memory_space=pltpu.SMEM)]
    return cube_call(kernel, (*lefts, right, places), specs, (block, extent), scratch, cost, earlier)


def cube_pair(home, arrived, *earlier):
    _, rows, width = home.shape
    half = rows // 2

    def kernel(home, arrived, own, over_x, over_y, top, bottom):
        total = lambda at: (
            home[at].astype(jnp.float32) + arrived[at].astype(jnp.float32)
        ).astype(jnp.bfloat16)
        own[...] = total(0)
        over_x[...] = total(1)
        over_y[...] = total(2)
        corner = total(3)
        top[...] = corner[:half]
        bottom[...] = corner[half:]

    full, part = whole(rows, width), whole(half, width)
    return call(
        kernel,
        1,
        (home, arrived),
        [whole(4, rows, width)] * 2,
        [full] * 3 + [part] * 2,
        [low_shape(rows, width)] * 3 + [low_shape(half, width)] * 2,
        0,
        earlier,
    )


def total_slots(terms, count, *earlier):
    rows, width = terms[0].shape
    local = rows // count

    def kernel(*refs):
        for slot in range(count):
            at = slice(slot * local, (slot + 1) * local)
            total = refs[0][at, :].astype(jnp.float32)
            for ref in refs[1 : len(terms)]:
                total = total + ref[at, :].astype(jnp.float32)
            refs[len(terms) + slot][...] = total.astype(jnp.bfloat16)

    return call(
        kernel,
        1,
        tuple(terms),
        [whole(rows, width)] * len(terms),
        [whole(local, width)] * count,
        [low_shape(local, width)] * count,
        0,
        earlier,
    )


def cube_turn(over_x, over_y, from_x, from_y, *earlier):
    rows, width = over_x.shape
    half = rows // 2

    def kernel(over_x, over_y, from_x, from_y, go_x, go_y):
        both = lambda one, two: (one.astype(jnp.float32) + two.astype(jnp.float32)).astype(jnp.bfloat16)
        go_y[:half, :] = both(over_y[:half, :], from_x[...])
        go_y[half:, :] = over_y[half:, :]
        go_x[:half, :] = over_x[:half, :]
        go_x[half:, :] = both(over_x[half:, :], from_y[...])

    full, part = whole(rows, width), whole(half, width)
    return call(
        kernel,
        1,
        (over_x, over_y, from_x, from_y),
        [full] * 2 + [part] * 2,
        [full] * 2,
        [low_shape(rows, width)] * 2,
        0,
        earlier,
    )


def total_of(terms, dtype, *earlier, cost=0):
    rows, width = terms[0].shape
    wide = rows // 2 if rows % 32 == 0 else rows

    def kernel(*refs):
        total = refs[0][...].astype(jnp.float32)
        for ref in refs[1:-1]:
            total = total + ref[...].astype(jnp.float32)
        refs[-1][...] = total.astype(dtype)

    block = row_block(wide, width)
    shape = jax.ShapeDtypeStruct((rows, width), dtype)
    return call(kernel, rows // wide, tuple(terms), [block] * len(terms), block, shape, 0, earlier)


def norm_grad(grads, value, gain, beside):
    width = value.shape[1]
    grad = grads[0].astype(jnp.float32)
    for term in grads[1:]:
        grad = grad + term.astype(jnp.float32)
    value = value.astype(jnp.float32)
    scale = lax.rsqrt(jnp.sum(value * value, 1, keepdims=True) * (1.0 / width) + EPS)
    scaled = value * scale
    inner = grad * gain.astype(jnp.float32)
    mean = jnp.sum(inner * scaled, 1, keepdims=True) * (1.0 / width)
    return beside.astype(jnp.float32) + scale * (inner - scaled * mean)


def norm_backward(grads, value, gain, beside, *earlier):
    rows, width = value.shape
    terms = len(grads)
    wide = 96 if rows % 96 == 0 else rows

    def kernel(*refs):
        value, gain, beside, out = refs[terms:]
        grads = [ref[...] for ref in refs[:terms]]
        out[...] = norm_grad(grads, value[...], gain[...], beside[...]).astype(out.dtype)

    block = row_block(wide, width)
    return call(
        kernel,
        rows // wide,
        (*grads, value, gain.reshape(1, width), beside),
        [block] * (terms + 1) + [whole(1, width), block],
        block,
        low_shape(rows, width),
        0,
        earlier,
    )


def norm_split(grads, value, gain, beside, right, count, *earlier):
    rows, width = value.shape
    terms = len(grads)
    wide = right.shape[0] // count

    def kernel(*refs):
        value, gain, beside, right, total, rounded = refs[terms : terms + 6]
        out = refs[terms + 6 :]

        @pl.when(pl.program_id(0) == 0)
        def _():
            for at in [slice(start, start + 96) for start in range(0, rows, 96)] if rows % 96 == 0 else [slice(0, rows)]:
                one = norm_grad([ref[at, :] for ref in refs[:terms]], value[at, :], gain[...], beside[at, :])
                total[at, :] = one
                rounded[at, :] = one.astype(jnp.bfloat16)

        part = dot(rounded[...], right[...], NT).astype(jnp.bfloat16)
        for slot in range(count):

            @pl.when(pl.program_id(0) == slot)
            def _(slot=slot):
                out[slot][...] = part

    block = whole(rows, width)
    out = call(
        kernel,
        count,
        (*grads, value, gain.reshape(1, width), beside, right),
        [block] * (terms + 1) + [whole(1, width), block, row_block(wide, width)],
        [block] * 2 + [whole(rows, wide)] * count,
        [jax.ShapeDtypeStruct((rows, width), jnp.float32), low_shape(rows, width)]
        + [low_shape(rows, wide)] * count,
        HEAVY // 32,
        earlier,
    )
    return out[0], out[1], out[2:]


def widen(terms, weight, part=0, *earlier):
    rows, width = weight.shape
    wide = rows // 2 if rows % 32 == 0 else rows
    count = len(terms)

    def kernel(*refs):
        weight, out, share = refs[count:]
        total = refs[0][...].astype(jnp.float32)
        for ref in refs[1:count]:
            total = total + ref[...].astype(jnp.float32)
        out[...] = total
        share[...] = jnp.sum(total * weight[...].astype(jnp.float32), 1, keepdims=True)

    block = row_block(wide, width)
    return call(
        kernel,
        rows // wide,
        (*terms, weight),
        [pl.BlockSpec((wide, width), lambda f: (f, part))] * count + [block],
        [block, row_block(wide, 1)],
        [jax.ShapeDtypeStruct((rows, width), jnp.float32), jax.ShapeDtypeStruct((rows, 1), jnp.float32)],
        0,
        earlier,
    )


def widen_turned(value, part):
    rows, width = value.shape
    width = width // 2
    wide = 512 if width % 512 == 0 else width
    blocks = width // wide

    def kernel(source, target):
        target[...] = source[...].astype(jnp.float32).T

    return call(
        kernel,
        blocks,
        (value,),
        [pl.BlockSpec((rows, wide), lambda f: (0, part * blocks + f))],
        row_block(wide, rows),
        jax.ShapeDtypeStruct((width, rows), jnp.float32),
        0,
    )


def after(value, *earlier):
    return lax.optimization_barrier((value,) + earlier)[0]


def ring():
    count = lax.axis_size("tensor")
    return [0] + list(range(1, count, 2)) + list(range(2, count, 2))[::-1]


def ring_shift(value, by):
    order = ring()
    count = len(order)
    return lax.ppermute(value, "tensor", [(order[k], order[(k + by) % count]) for k in range(count)])


def slot_places():
    order = ring()
    count = len(order)
    me = lax.axis_index("tensor")
    at = sum(jnp.where(me == device, place, 0) for place, device in enumerate(order))
    back = (at - jnp.arange(count, dtype=jnp.int32)) % count
    return sum(jnp.where(back == place, device, 0) for place, device in enumerate(order)).astype(jnp.int32)


def ring_gather(piece, pauses=()):
    pauses = dict(pauses)
    slots = [piece]
    for step in range(1, lax.axis_size("tensor")):
        last = slots[-1]
        if step in pauses:
            last = tied(last, *pauses[step])
        slots.append(ring_shift(last, 1))
    return slots


def direct_gather(piece):
    return [piece] + [ring_shift(piece, by) for by in range(1, lax.axis_size("tensor"))]


def ring_scatter(parts, pauses=(), heavy=0):
    pauses = dict(pauses)
    count = len(parts)
    arrivals = []
    moving = parts[1]
    for step in range(1, count):
        arrivals.append(ring_shift(moving, 1))
        if step < count - 1:
            if step + 1 in pauses:
                moving = tied_sum(
                    arrivals[-1], parts[step + 1], HEAVY if step + 1 == heavy else 0, *pauses[step + 1]
                )
            else:
                moving = add(arrivals[-1], parts[step + 1])
    return (parts[0], arrivals[-1]), arrivals


def add(left, right):
    return (left.astype(jnp.float32) + right.astype(jnp.float32)).astype(jnp.bfloat16)


def exchange(parts):
    count = len(parts)
    return [parts[0]] + [ring_shift(parts[count - q], q) for q in range(1, count)]


def flip(value, bits):
    count = lax.axis_size("dp")
    return lax.ppermute(value, "dp", [(k, k ^ bits) for k in range(count)])


def cube_pairs(parts, *earlier):
    away, home = parts
    return cube_pair(home, flip(away, 1), *earlier)


def cube_turns(pairs, *earlier):
    _, over_x, over_y, top, bottom = pairs
    return cube_turn(over_x, over_y, flip(top, 2), flip(bottom, 4), *earlier)


def cube_terms(pairs, turns):
    return (pairs[0], flip(turns[0], 2), flip(turns[1], 4))


def cube_total(pairs, turns, dtype, *earlier):
    return total_of(cube_terms(pairs, turns), dtype, *earlier)


def gather_rows(piece):
    return lax.all_gather(piece, "dp", axis=0, tiled=True)


def gather_columns(piece):
    return lax.all_gather(piece, "dp", axis=1, tiled=True)


def sum_rows(value):
    return lax.psum_scatter(value, "dp", scatter_dimension=0, tiled=True)


def sum_columns(value):
    return lax.psum_scatter(value, "dp", scatter_dimension=1, tiled=True)


def gain_sums(shares, gains, places):
    count = places.shape[0]
    rows = shares[0].shape[0]
    start = lax.axis_index("dp") * rows
    own = [share[:, 0] / lax.dynamic_slice_in_dim(gain, start, rows, 0) for share, gain in zip(shares, gains)]
    cut = jnp.stack(own).reshape(len(own), count, -1)
    pieces = [lax.dynamic_index_in_dim(cut, places[slot], 1, False) for slot in range(count)]
    return sum(exchange(pieces))


def normalize(value, gain):
    scale = lax.rsqrt(jnp.mean(value * value, axis=1, keepdims=True) + EPS)
    return (value * scale * gain[None, :], scale)


def per_device(
    tokens, lengths, attention_gain, w_inputs, w_output, feed_gain, w_gate, w_up, w_down, cotangent
):
    count = lax.axis_size("tensor")
    groups = KV // count
    local, width = tokens.shape
    rows = local * count
    low = jnp.bfloat16
    held = tables(lengths[0], rows)
    sequences = lengths.shape[1]
    gain_one = attention_gain.astype(jnp.float32)
    gain_two = feed_gain.astype(jnp.float32)

    places = slot_places()
    base = tokens.astype(jnp.float32)
    first = normalize(base, gain_one)[0].astype(low)
    inputs_full = gather_rows(w_inputs)
    first_slots = ring_gather(first)
    output_line = jnp.concatenate(direct_gather(w_output), 0)
    output_full = gather_columns(output_line)
    gate_full = gather_rows(w_gate)
    up_full = gather_rows(w_up)
    down_full = gather_columns(w_down)

    joint = project(first_slots, inputs_full, places)
    heads, query, key, value = attention_forward(joint, held, sequences, groups)
    grad_slots = ring_gather(tied(cotangent, first_slots[-1]))
    heads_own = exchange(to_slots(heads, places, grad_slots[1]))
    mixed = base + dot(jnp.concatenate(heads_own, 1), output_full)
    second = tied(normalize(mixed, gain_two)[0].astype(low), grad_slots[min(2, count - 1)])
    second_slots = ring_gather(second)
    half = max(count // 2, 1)
    ahead = feed_forward(second_slots[:half], gate_full, up_full)
    rest = feed_forward(second_slots[half:], gate_full, up_full)
    hidden, gate, up = [list(one) + list(two) for one, two in zip(ahead, rest)]
    block_parts = product(hidden, down_full)
    gate_grad, up_grad = feed_backward(grad_slots, down_full, gate, up, block_parts[0])
    block_moving = ring_shift(block_parts[1], 1)
    pick = lambda slots: ((([gate_grad[s] for s in slots]), gate_full), ([up_grad[s] for s in slots], up_full))
    part_one = sum_of_products(pick([1]), block_moving)
    others = [0] + list(range(2, count))
    part_others = sum_of_products(pick(others), part_one[0])
    second_parts = [part_others[0], part_one[0]] + list(part_others[1:])
    second_early = ring_shift(second_parts[1], 1)
    gate_wpart = weight_grad(second_slots, gate_grad, second_early)
    gate_wgrad = sum_rows(gate_wpart)
    second_grad, second_back = ring_scatter(second_parts, {3: [gate_wpart]}, 3)
    up_wpart = weight_grad(second_slots, up_grad, second_back[1], half=0)

    mixed_total, branch, heads_back = norm_split(
        second_grad, mixed, gain_two, cotangent, output_full, count, up_wpart
    )
    heads_grad = exchange(heads_back)
    both_wpart = weight_grad(grad_slots, hidden, branch, half=1, into=up_wpart)
    both_wgrad = sum_rows(both_wpart)
    block_sum, block_back = ring_scatter(block_parts, {2: [second_back[-1]], 3: [heads_grad[-1]]})
    cube = lax.axis_size("dp") == 8
    output_parts = cube_columns(heads_own, branch, both_wpart) if cube else ()
    joint_grad = attention_backward(
        query, key, value, heads, heads_grad, places, held, groups, block_back[1], both_wpart, *output_parts[:1]
    )
    first_one = spread_product(joint_grad, inputs_full, places, [1], block_back[2])
    first_others = spread_product(joint_grad, inputs_full, places, others, first_one[0])
    first_parts = [first_others[0], first_one[0]] + list(first_others[1:])
    gate_wgrad, gate_share = widen([gate_wgrad], w_gate)
    if cube:
        output_pairs = cube_pairs(output_parts, first_one[0])
        output_turns = cube_turns(output_pairs)
        inputs_parts = cube_rows(first_slots, joint_grad, places, HEAVY, output_pairs[0])
        second_pause = [output_turns[0], inputs_parts[0]]
        first_next = tied_sum(ring_shift(first_parts[1], 1), first_parts[2], 0, *second_pause)
        inputs_pairs = cube_pairs(inputs_parts, first_next)
        third_pause = [inputs_pairs[0], gate_wgrad]
        first_last = tied_sum(ring_shift(first_next, 1), first_parts[3], 0, *third_pause)
        inputs_turns = cube_turns(inputs_pairs, first_last)
        output_cut = total_slots(cube_terms(output_pairs, output_turns), count, first_last)
        first_grad, first_back = ring_scatter(first_parts, {2: second_pause, 3: third_pause})
        block_out = total_of((*block_sum, mixed), low, first_last, cost=HEAVY)
        inputs_grad, inputs_share = widen(cube_terms(inputs_pairs, inputs_turns), w_inputs)
    else:
        first_grad, first_back = ring_scatter(first_parts)
        block_out = total_of((*block_sum, mixed), low)
        output_sum = sum_columns(weight_grad([jnp.concatenate(heads_own, 1)], [branch]))
        inputs_grad = sum_rows(weight_grad(first_slots, to_slots(joint_grad, places)))
        inputs_grad, inputs_share = widen([inputs_grad], w_inputs)
        output_sum = output_sum.reshape(count, -1, output_sum.shape[1])
        output_cut = [output_sum[slot] for slot in range(count)]
    tokens_grad = norm_backward(first_grad, tokens, gain_one, mixed_total, block_out)
    up_wgrad, up_share = widen([both_wgrad], w_up, 0, tokens_grad)
    down_grad = widen_turned(both_wgrad, 1)
    gain_grads = gain_sums([inputs_share, gate_share + up_share], [gain_one, gain_two], places)
    output_grad = exchange(output_cut)
    output_grad = total_of(output_grad, jnp.float32, tokens_grad)
    return (
        block_out,
        tokens_grad,
        gain_grads[0],
        inputs_grad,
        output_grad,
        gain_grads[1],
        gate_wgrad,
        up_wgrad,
        down_grad,
    )


def solution(mesh):
    in_specs = (
        P(("dp", "tensor"), None),
        P("dp", None),
        P(),
        P("dp", "tensor"),
        P("tensor", "dp"),
        P(),
        P("dp", "tensor"),
        P("dp", "tensor"),
        P("tensor", "dp"),
        P(("dp", "tensor"), None),
    )
    out_specs = (
        P(("dp", "tensor"), None),
        P(("dp", "tensor"), None),
        P(("dp", "tensor")),
        P("dp", "tensor"),
        P("tensor", "dp"),
        P(("dp", "tensor")),
        P("dp", "tensor"),
        P("dp", "tensor"),
        P("tensor", "dp"),
    )
    return jax.shard_map(
        per_device, mesh=mesh, in_specs=in_specs, out_specs=out_specs, check_vma=False
    )
```

```python
import math

import jax
import jax.numpy as jnp
from jax import lax
from jax.experimental import pallas as pl
from jax.experimental.pallas import tpu as pltpu
from jax.sharding import PartitionSpec as P

KV = 8
HD = 64
QPK = 4
EPS = 1e-05
THETA = 500000.0
FLOOR = -1e30
LANES = 128
BLOCK = 128
PARTS = 3
VMEM = 56 << 20
HEAVY = 10**12
NT = (((1,), (1,)), ((), ()))
NN = (((1,), (0,)), ((), ()))
TN = (((0,), (0,)), ((), ()))


def layout(lens, rows_count):
    ends = jnp.cumsum(lens)
    rows = jnp.arange(rows_count, dtype=jnp.int32)
    segment = jnp.sum((rows[:, None] >= ends[None, :]).astype(jnp.int32), axis=1)
    starts = ends - lens
    numbers = jnp.arange(lens.shape[0], dtype=jnp.int32)
    picked = jnp.where(segment[:, None] == numbers[None, :], starts[None, :], 0)
    return segment, rows - jnp.sum(picked, axis=1)


def tables(lens, rows_count):
    segment, position = layout(lens, rows_count)
    index = (jnp.arange(LANES, dtype=jnp.int32) % (HD // 2)).astype(jnp.float32)
    inverse = jnp.exp(index * (-2.0 * math.log(THETA) / HD))
    angle = position.astype(jnp.float32)[:, None] * inverse[None, :]
    count = lens.shape[0]
    lane = jnp.arange(LANES, dtype=jnp.int32)[None, :] - HD
    same = lane == segment[:, None]
    inside = (lane >= 0) & (lane < count)
    extra = (lane >= count) & (lane < count + PARTS)
    key_lanes = jnp.where((same & inside) | extra, 1.0, 0.0).astype(jnp.bfloat16)
    query_lanes = jnp.where(inside & ~same, FLOOR, 0.0).astype(jnp.bfloat16)
    return jnp.cos(angle), jnp.sin(angle), query_lanes, key_lanes


def dot(left, right, dims=NN):
    return lax.dot_general(left, right, dims, preferred_element_type=jnp.float32)


def rotate(value, cosine, sine):
    low = lax.broadcasted_iota(jnp.int32, value.shape, 1) % HD < HD // 2
    up = pltpu.roll(value, LANES - HD // 2, 1)
    down = pltpu.roll(value, HD // 2, 1)
    return value * cosine + jnp.where(low, -up, down) * sine


def unrotate(value, cosine, sine):
    low = lax.broadcasted_iota(jnp.int32, value.shape, 1) % HD < HD // 2
    scaled = value * sine
    up = pltpu.roll(scaled, LANES - HD // 2, 1)
    down = pltpu.roll(scaled, HD // 2, 1)
    return value * cosine + jnp.where(low, up, -down)


def split(value, parts):
    out = []
    for _ in range(parts):
        piece = value.astype(jnp.bfloat16).astype(jnp.float32)
        out.append(piece)
        value = value - piece
    return out


def forward_kernel(count, joint, cos, sin, query_lanes, key_lanes, heads, query, key, value):
    rows = joint.shape[0]
    cosine, sine = cos[...], sin[...]
    lane = lax.broadcasted_iota(jnp.int32, (rows, LANES), 1)
    left = lane < HD
    beside = query_lanes[...].astype(jnp.float32)
    for pair in range(QPK // 2):
        both = rotate(joint[:, pair * LANES : (pair + 1) * LANES], cosine, sine) * (1.0 / math.sqrt(HD))
        query[2 * pair] = jnp.where(left, both, beside).astype(jnp.bfloat16)
        query[2 * pair + 1] = jnp.where(left, pltpu.roll(both, HD, 1), beside).astype(jnp.bfloat16)
    last = joint[:, QPK * HD : QPK * HD + LANES]
    key[...] = jnp.where(left, rotate(last, cosine, sine), key_lanes[...].astype(jnp.float32)).astype(
        jnp.bfloat16
    )
    ones = jnp.where((lane >= HD) & (lane < HD + PARTS), 1.0, 0.0)
    value[...] = jnp.where(left, pltpu.roll(last, HD, 1), ones).astype(jnp.bfloat16)
    lower = lax.broadcasted_iota(jnp.int32, (BLOCK, BLOCK), 1) <= lax.broadcasted_iota(
        jnp.int32, (BLOCK, BLOCK), 0
    )
    lower = jnp.concatenate([lower] * QPK, 0)
    narrow = lax.broadcasted_iota(jnp.int32, (QPK * BLOCK, LANES), 1)
    for block in range(rows // BLOCK):
        start = block * BLOCK
        end = start + BLOCK
        own = query[:, start:end, :].reshape(QPK * BLOCK, LANES)
        near = jnp.where(lower, dot(own, key[start:end, :], NT), FLOOR)
        top = jnp.max(near, 1, keepdims=True)
        if block:
            far = dot(own, key[0:start, :], NT)
            top = jnp.maximum(top, jnp.max(far, 1, keepdims=True))
        out = dot(jnp.exp(near - top).astype(jnp.bfloat16), value[start:end, :])
        if block:
            out = out + dot(jnp.exp(far - top).astype(jnp.bfloat16), value[0:start, :])
        total = out[:, HD : HD + 1]
        out = out * (1.0 / total)
        held = own.astype(jnp.float32)
        for part, piece in enumerate(split(top + jnp.log(total), PARTS)):
            held = jnp.where(narrow == HD + count + part, -piece, held)
        query[:, start:end, :] = held.astype(jnp.bfloat16).reshape(QPK, BLOCK, LANES)
        each = [out[head * BLOCK : (head + 1) * BLOCK] for head in range(QPK)]
        half = narrow[:BLOCK] < HD
        for pair in range(QPK // 2):
            heads[start:end, pair * LANES : (pair + 1) * LANES] = jnp.where(
                half, each[2 * pair], pltpu.roll(each[2 * pair + 1], HD, 1)
            ).astype(jnp.bfloat16)


def whole(*shape):
    return pl.BlockSpec(shape, lambda g: (0,) * len(shape))


def grouped(*shape):
    return pl.BlockSpec((None,) + shape, lambda g: (g,) + (0,) * len(shape))


def columns(rows, width):
    return pl.BlockSpec((rows, width), lambda g: (0, g))


def attention_forward(joint, held, count, groups):
    rows = joint.shape[0]
    shape = jax.ShapeDtypeStruct
    low = jnp.bfloat16
    return pl.pallas_call(
        lambda *refs: forward_kernel(count, *refs),
        grid=(groups,),
        in_specs=[columns(rows, (QPK + 2) * HD)] + [whole(rows, LANES)] * 4,
        out_specs=[
            columns(rows, QPK * HD),
            grouped(QPK, rows, LANES),
            grouped(rows, LANES),
            grouped(rows, LANES),
        ],
        out_shape=[
            shape((rows, groups * QPK * HD), low),
            shape((groups, QPK, rows, LANES), low),
            shape((groups, rows, LANES), low),
            shape((groups, rows, LANES), low),
        ],
        compiler_params=pltpu.CompilerParams(vmem_limit_bytes=VMEM),
        cost_estimate=pl.CostEstimate(
            flops=groups * 12 * rows * rows * QPK * HD,
            bytes_accessed=1 << 20,
            transcendentals=0,
        ),
    )(joint, *held)


def backward_kernel(count, *refs):
    query, key, value, heads = refs[:4]
    places, cos, sin = refs[4 + count : 7 + count]
    out, grads, query_grad, key_grad, value_grad = refs[-5:]
    rows = key.shape[0]
    local = rows // count
    for slot in range(count):
        start = pl.multiple_of(places[slot] * local, 16)
        grads[pl.ds(start, local), :] = refs[4 + slot][...]
    key_grad[...] = jnp.zeros_like(key_grad)
    value_grad[...] = jnp.zeros_like(value_grad)
    turned = key[...].astype(jnp.float32).T.astype(jnp.bfloat16)
    upper = lax.broadcasted_iota(jnp.int32, (BLOCK, BLOCK), 0) <= lax.broadcasted_iota(
        jnp.int32, (BLOCK, BLOCK), 1
    )
    upper = jnp.concatenate([upper] * QPK, 1)
    lane = lax.broadcasted_iota(jnp.int32, (QPK * BLOCK, LANES), 1)
    half = lane[:BLOCK] < HD

    def stacked(ref, start, end):
        pieces = []
        for pair in range(QPK // 2):
            both = ref[start:end, pair * LANES : (pair + 1) * LANES].astype(jnp.float32)
            pieces += [both, pltpu.roll(both, HD, 1)]
        return jnp.where(lane < HD, jnp.concatenate(pieces, 0), 0.0)

    for block in range(rows // BLOCK):
        start = block * BLOCK
        end = start + BLOCK
        own = query[:, start:end, :].reshape(QPK * BLOCK, LANES)
        grad = stacked(grads, start, end)
        inner = jnp.sum(grad * stacked(heads, start, end), 1, keepdims=True)
        low = grad.astype(jnp.bfloat16)
        for part, piece in enumerate(split(inner, PARTS)):
            grad = jnp.where(lane == HD + part, -piece, grad)
        beside = grad.astype(jnp.bfloat16)
        turned_grad = None
        for first, last in ([(0, start)] if block else []) + [(start, end)]:
            scores = dot(key[first:last, :], own, NT)
            if first == start:
                scores = jnp.where(upper, scores, FLOOR)
            probs = jnp.exp(scores)
            score_grad = (probs * dot(value[first:last, :], beside, NT)).astype(jnp.bfloat16)
            value_grad[first:last, :] += dot(probs.astype(jnp.bfloat16), low)
            key_grad[first:last, :] += dot(score_grad, own)
            piece = dot(turned[:, first:last], score_grad)
            turned_grad = piece if turned_grad is None else turned_grad + piece
        back = turned_grad.T * (1.0 / math.sqrt(HD))
        each = [back[head * BLOCK : (head + 1) * BLOCK] for head in range(QPK)]
        for pair in range(QPK // 2):
            query_grad[start:end, pair * LANES : (pair + 1) * LANES] = jnp.where(
                half, each[2 * pair], pltpu.roll(each[2 * pair + 1], HD, 1)
            )
    cosine, sine = cos[...], sin[...]
    for pair in range(QPK // 2):
        at = slice(pair * LANES, (pair + 1) * LANES)
        out[:, at] = unrotate(query_grad[:, at], cosine, sine).astype(jnp.bfloat16)
    left = lax.broadcasted_iota(jnp.int32, (rows, LANES), 1) < HD
    key_part = unrotate(jnp.where(left, key_grad[...], 0.0), cosine, sine)
    out[:, QPK * HD : QPK * HD + LANES] = jnp.where(
        left, key_part, pltpu.roll(value_grad[...], HD, 1)
    ).astype(jnp.bfloat16)


def attention_backward(query, key, value, heads, slots, places, held, groups, *earlier):
    rows = key.shape[1]
    wide = (QPK + 2) * HD
    count = len(slots)
    operands = (query, key, value, heads, *slots, places, held[0], held[1])
    return call(
        lambda *refs: backward_kernel(count, *refs),
        groups,
        operands,
        [grouped(QPK, rows, LANES), grouped(rows, LANES), grouped(rows, LANES), columns(rows, QPK * HD)]
        + [columns(rows // count, QPK * HD)] * count
        + [pl.BlockSpec(memory_space=pltpu.SMEM)]
        + [whole(rows, LANES)] * 2,
        columns(rows, wide),
        jax.ShapeDtypeStruct((rows, groups * wide), jnp.bfloat16),
        HEAVY,
        earlier,
        [
            pltpu.VMEM((rows, QPK * HD), jnp.bfloat16),
            pltpu.VMEM((rows, QPK * HD), jnp.float32),
            pltpu.VMEM((rows, LANES), jnp.float32),
            pltpu.VMEM((rows, LANES), jnp.float32),
        ],
    )


def call(kernel, grid, operands, specs, out_specs, out_shape, flops, earlier=(), scratch=()):
    count, extra = len(operands), len(earlier)
    return pl.pallas_call(
        lambda *refs: kernel(*refs[:count], *refs[count + extra :]),
        grid=(grid,),
        in_specs=specs + [pl.BlockSpec(memory_space=pl.ANY)] * extra,
        out_specs=out_specs,
        out_shape=out_shape,
        scratch_shapes=list(scratch),
        compiler_params=pltpu.CompilerParams(vmem_limit_bytes=VMEM),
        cost_estimate=pl.CostEstimate(flops=flops, bytes_accessed=1 << 20, transcendentals=0),
    )(*operands, *earlier)


def column_block(rows, wide):
    return pl.BlockSpec((rows, wide), lambda f: (0, f))


def row_block(wide, width):
    return pl.BlockSpec((wide, width), lambda f: (f, 0))


def low_shape(*shape):
    return jax.ShapeDtypeStruct(shape, jnp.bfloat16)


def block_size(extent):
    return 256 if extent % 256 == 0 else extent


def tied(value, *earlier):
    rows, width = value.shape
    wide = rows // 2 if rows % 32 == 0 else rows

    def kernel(source, target):
        target[...] = source[...]

    block = row_block(wide, width)
    return call(kernel, rows // wide, (value,), [block], block, low_shape(rows, width), 0, earlier)


def tied_sum(left, right, weight, *earlier):
    rows, width = left.shape
    wide = rows // 2 if rows % 32 == 0 else rows

    def kernel(left, right, out):
        out[...] = (left[...].astype(jnp.float32) + right[...].astype(jnp.float32)).astype(out.dtype)

    block = row_block(wide, width)
    return call(
        kernel, rows // wide, (left, right), [block] * 2, block, low_shape(rows, width), weight, earlier
    )


def project(slots, weight, places):
    count = len(slots)
    local, width = slots[0].shape
    extent = weight.shape[1]
    wide = block_size(extent)

    def kernel(*refs):
        places, weight, out = refs[count], refs[count + 1], refs[count + 2]
        for slot in range(count):
            start = pl.multiple_of(places[slot] * local, 16)
            out[pl.ds(start, local), :] = dot(refs[slot][...], weight[...])

    return call(
        kernel,
        extent // wide,
        (*slots, places, weight),
        [whole(local, width)] * count
        + [pl.BlockSpec(memory_space=pltpu.SMEM), column_block(width, wide)],
        column_block(count * local, wide),
        jax.ShapeDtypeStruct((count * local, extent), jnp.float32),
        2 * count * local * width * extent,
    )


def to_slots(value, places, *earlier):
    count = places.shape[0]
    rows, width = value.shape
    local = rows // count

    def kernel(value, places, *out):
        for slot in range(count):
            start = pl.multiple_of(places[slot] * local, 16)
            out[slot][...] = value[pl.ds(start, local), :]

    return call(
        kernel,
        1,
        (value, places),
        [whole(rows, width), pl.BlockSpec(memory_space=pltpu.SMEM)],
        [whole(local, width)] * count,
        [low_shape(local, width)] * count,
        0,
        earlier,
    )


def from_slots(slots, places, *earlier):
    count = len(slots)
    local, width = slots[0].shape

    def kernel(*refs):
        for slot in range(count):
            start = pl.multiple_of(refs[count][slot] * local, 16)
            refs[-1][pl.ds(start, local), :] = refs[slot][...]

    return call(
        kernel,
        1,
        (*slots, places),
        [whole(local, width)] * count + [pl.BlockSpec(memory_space=pltpu.SMEM)],
        whole(count * local, width),
        low_shape(count * local, width),
        0,
        earlier,
    )


def feed_forward(slots, w_gate, w_up, *earlier):
    count = len(slots)
    rows, width = slots[0].shape
    extent = w_gate.shape[1]
    wide = block_size(extent)

    def kernel(*refs):
        w_gate, w_up = refs[count], refs[count + 1]
        out = refs[count + 2 :]
        for slot in range(count):
            one = dot(refs[slot][...], w_gate[...])
            two = dot(refs[slot][...], w_up[...])
            sigma = jax.nn.sigmoid(one)
            silu = one * sigma
            slope = two * (sigma + silu * (1.0 - sigma))
            out[slot][...] = (silu * two).astype(jnp.bfloat16)
            out[count + slot][...] = slope.astype(jnp.bfloat16)
            out[2 * count + slot][...] = silu.astype(jnp.bfloat16)

    out = call(
        kernel,
        extent // wide,
        (*slots, w_gate, w_up),
        [whole(rows, width)] * count + [column_block(width, wide)] * 2,
        [column_block(rows, wide)] * (3 * count),
        [low_shape(rows, extent)] * (3 * count),
        4 * count * rows * width * extent,
        earlier,
    )
    return out[:count], out[count : 2 * count], out[2 * count :]


def feed_backward(grads, w_down, slopes, silus, *earlier):
    count = len(grads)
    rows, width = grads[0].shape
    extent = w_down.shape[0]
    wide = block_size(extent)

    def kernel(*refs):
        w_down = refs[3 * count]
        out = refs[3 * count + 1 :]
        for slot in range(count):
            hidden_grad = dot(refs[slot][...], w_down[...], NT)
            slope = refs[count + slot][...].astype(jnp.float32)
            silu = refs[2 * count + slot][...].astype(jnp.float32)
            out[slot][...] = (hidden_grad * slope).astype(jnp.bfloat16)
            out[count + slot][...] = (hidden_grad * silu).astype(jnp.bfloat16)

    out = call(
        kernel,
        extent // wide,
        (*grads, *slopes, *silus, w_down),
        [whole(rows, width)] * count
        + [column_block(rows, wide)] * (2 * count)
        + [row_block(wide, width)],
        [column_block(rows, wide)] * (2 * count),
        [low_shape(rows, extent)] * (2 * count),
        2 * count * rows * width * extent,
        earlier,
    )
    return out[:count], out[count:]


def sum_of_products(terms, *earlier):
    count = len(terms[0][0])
    rows, depth = terms[0][0][0].shape
    extent = terms[0][1].shape[0]
    wide = block_size(extent)
    total = len(terms)

    def kernel(*refs):
        weights = refs[total * count : total * count + total]
        out = refs[total * count + total :]
        for slot in range(count):
            sums = dot(refs[slot][...], weights[0][...], NT)
            for term in range(1, total):
                sums = sums + dot(refs[term * count + slot][...], weights[term][...], NT)
            out[slot][...] = sums.astype(jnp.bfloat16)

    slots = [slot for term in terms for slot in term[0]]
    return call(
        kernel,
        extent // wide,
        (*slots, *[term[1] for term in terms]),
        [whole(rows, depth)] * (total * count) + [row_block(wide, depth)] * total,
        [column_block(rows, wide)] * count,
        [low_shape(rows, extent)] * count,
        2 * total * count * rows * depth * extent,
        earlier,
    )


def product(slots, right, *earlier):
    count = len(slots)
    rows, depth = slots[0].shape
    extent = right.shape[1]
    wide = block_size(extent)

    def kernel(*refs):
        for slot in range(count):
            refs[count + 1 + slot][...] = dot(refs[slot][...], refs[count][...]).astype(jnp.bfloat16)

    return call(
        kernel,
        extent // wide,
        (*slots, right),
        [whole(rows, depth)] * count + [column_block(depth, wide)],
        [column_block(rows, wide)] * count,
        [low_shape(rows, extent)] * count,
        2 * count * rows * depth * extent,
        earlier,
    )


def weight_grad(lefts, rights, *earlier, half=None, into=None):
    count = len(lefts)
    rows, extent = lefts[0].shape
    width = rights[0].shape[1]
    wide = block_size(extent)
    narrow = 512 if width % 512 == 0 else width
    total = 2 * count + (into is not None) + len(earlier)

    def kernel(*refs):
        out, left, right = refs[total:]

        @pl.when(pl.program_id(0) == 0)
        def _():
            for slot in range(count):
                right[slot * rows : (slot + 1) * rows, :] = refs[count + slot][...]

        for slot in range(count):
            left[slot * rows : (slot + 1) * rows, :] = refs[slot][...]
        for start in range(0, width, narrow):
            at = slice(start, start + narrow)
            out[:, at] = dot(left[...], right[:, at], TN).astype(jnp.bfloat16)

    held = () if into is None else (into,)
    return pl.pallas_call(
        kernel,
        grid=(extent // wide,),
        in_specs=[column_block(rows, wide)] * count
        + [whole(rows, width)] * count
        + [pl.BlockSpec(memory_space=pl.ANY)] * (len(held) + len(earlier)),
        out_specs=pl.BlockSpec((wide, width), lambda f: (f, half or 0)),
        out_shape=low_shape(extent, width if half is None else 2 * width),
        input_output_aliases={} if into is None else {2 * count: 0},
        scratch_shapes=[
            pltpu.VMEM((count * rows, wide), jnp.bfloat16),
            pltpu.VMEM((count * rows, width), jnp.bfloat16),
        ],
        compiler_params=pltpu.CompilerParams(vmem_limit_bytes=VMEM),
        cost_estimate=pl.CostEstimate(
            flops=2 * count * rows * width * extent, bytes_accessed=1 << 20, transcendentals=0
        ),
    )(*lefts, *rights, *held, *earlier)


def spread_product(value, weight, places, slots, *earlier):
    count = places.shape[0]
    rows, depth = value.shape
    local = rows // count
    extent = weight.shape[0]
    wide = extent // 2 if extent % 512 == 0 else extent

    def kernel(value, places, weight, *out):
        for at, slot in enumerate(slots):
            start = pl.multiple_of(places[slot] * local, 16)
            out[at][...] = dot(value[pl.ds(start, local), :], weight[...], NT).astype(jnp.bfloat16)

    return call(
        kernel,
        extent // wide,
        (value, places, weight),
        [whole(rows, depth), pl.BlockSpec(memory_space=pltpu.SMEM), row_block(wide, depth)],
        [column_block(local, wide)] * len(slots),
        [low_shape(local, extent)] * len(slots),
        2 * len(slots) * local * depth * extent,
        earlier,
    )


def cube_call(kernel, operands, specs, piece, scratch, flops, earlier):
    count, extra = len(operands), len(earlier)

    def body(me, *refs):
        away, home = refs[count + extra : count + extra + 2]
        value = kernel(*refs[:count], *refs[count + extra + 2 :])
        step = pl.program_id(0)

        @pl.when(step < 4)
        def _():
            away[...] = value

        @pl.when(step >= 4)
        def _():
            home[...] = value

    me = lax.axis_index("dp").astype(jnp.int32).reshape(1)
    return pl.pallas_call(
        body,
        grid_spec=pltpu.PrefetchScalarGridSpec(
            num_scalar_prefetch=1,
            grid=(8,),
            in_specs=specs + [pl.BlockSpec(memory_space=pl.ANY)] * extra,
            out_specs=[
                pl.BlockSpec((None,) + piece, lambda i, me: (jnp.minimum(i, 3), 0, 0)),
                pl.BlockSpec((None,) + piece, lambda i, me: (jnp.maximum(i - 4, 0), 0, 0)),
            ],
            scratch_shapes=scratch,
        ),
        out_shape=[low_shape(4, *piece)] * 2,
        compiler_params=pltpu.CompilerParams(vmem_limit_bytes=VMEM),
        cost_estimate=pl.CostEstimate(flops=flops, bytes_accessed=1 << 20, transcendentals=0),
    )(me, *operands, *earlier)


def cube_place(step, me):
    return jnp.bitwise_xor(me[0], 2 * (step % 4) + 1 - step // 4)


def cube_columns(lefts, right, *earlier):
    count = len(lefts)
    rows, wide = lefts[0].shape
    block = right.shape[1] // 8

    def kernel(*refs):
        left = refs[-1]

        @pl.when(pl.program_id(0) == 0)
        def _():
            for slot in range(count):
                turned = refs[slot][...].astype(jnp.float32).T
                left[slot * wide : (slot + 1) * wide, :] = turned.astype(jnp.bfloat16)

        return dot(left[...], refs[count][...]).astype(jnp.bfloat16)

    fixed = pl.BlockSpec((rows, wide), lambda i, me: (0, 0))
    moving = pl.BlockSpec((rows, block), lambda i, me: (0, cube_place(i, me)))
    scratch = [pltpu.VMEM((count * wide, rows), jnp.bfloat16)]
    flops = 2 * rows * count * wide * right.shape[1]
    piece = (count * wide, block)
    return cube_call(kernel, (*lefts, right), [fixed] * count + [moving], piece, scratch, flops, earlier)


def cube_rows(lefts, right, places, cost, *earlier):
    count = len(lefts)
    rows, width = lefts[0].shape
    extent = right.shape[1]
    block = width // 8

    def kernel(*refs):
        left, turned = refs[-2:]

        @pl.when(pl.program_id(0) == 0)
        def _():
            for slot in range(count):
                start = pl.multiple_of(refs[count + 1][slot] * rows, 16)
                turned[slot * rows : (slot + 1) * rows, :] = refs[count][pl.ds(start, rows), :]

        for slot in range(count):
            left[slot * rows : (slot + 1) * rows, :] = refs[slot][...]
        return dot(left[...], turned[...], TN).astype(jnp.bfloat16)

    moving = pl.BlockSpec((rows, block), lambda i, me: (0, cube_place(i, me)))
    fixed = pl.BlockSpec((count * rows, extent), lambda i, me: (0, 0))
    scratch = [
        pltpu.VMEM((count * rows, block), jnp.bfloat16),
        pltpu.VMEM((count * rows, extent), jnp.bfloat16),
    ]
    specs = [moving] * count + [fixed, pl.BlockSpec(memory_space=pltpu.SMEM)]
    return cube_call(kernel, (*lefts, right, places), specs, (block, extent), scratch, cost, earlier)


def cube_pair(home, arrived, *earlier):
    _, rows, width = home.shape
    half = rows // 2

    def kernel(home, arrived, own, over_x, over_y, top, bottom):
        total = lambda at: (
            home[at].astype(jnp.float32) + arrived[at].astype(jnp.float32)
        ).astype(jnp.bfloat16)
        own[...] = total(0)
        over_x[...] = total(1)
        over_y[...] = total(2)
        corner = total(3)
        top[...] = corner[:half]
        bottom[...] = corner[half:]

    full, part = whole(rows, width), whole(half, width)
    return call(
        kernel,
        1,
        (home, arrived),
        [whole(4, rows, width)] * 2,
        [full] * 3 + [part] * 2,
        [low_shape(rows, width)] * 3 + [low_shape(half, width)] * 2,
        0,
        earlier,
    )


def cube_sums(parts, *earlier):
    away, home = parts
    arrived = flip(away, 1)
    _, rows, width = home.shape

    def kernel(home, arrived, *out):
        for at in range(4):
            total = home[at].astype(jnp.float32) + arrived[at].astype(jnp.float32)
            out[at][...] = total.astype(jnp.bfloat16)

    return call(
        kernel,
        1,
        (home, arrived),
        [whole(4, rows, width)] * 2,
        [whole(rows, width)] * 4,
        [low_shape(rows, width)] * 4,
        0,
        earlier,
    )


def total_slots(terms, count, *earlier):
    rows, width = terms[0].shape
    local = rows // count

    def kernel(*refs):
        for slot in range(count):
            at = slice(slot * local, (slot + 1) * local)
            total = refs[0][at, :].astype(jnp.float32)
            for ref in refs[1 : len(terms)]:
                total = total + ref[at, :].astype(jnp.float32)
            refs[len(terms) + slot][...] = total.astype(jnp.bfloat16)

    return call(
        kernel,
        1,
        tuple(terms),
        [whole(rows, width)] * len(terms),
        [whole(local, width)] * count,
        [low_shape(local, width)] * count,
        0,
        earlier,
    )


def cube_turn(over_x, over_y, from_x, from_y, *earlier):
    rows, width = over_x.shape
    half = rows // 2

    def kernel(over_x, over_y, from_x, from_y, go_x, go_y):
        both = lambda one, two: (one.astype(jnp.float32) + two.astype(jnp.float32)).astype(jnp.bfloat16)
        go_y[:half, :] = both(over_y[:half, :], from_x[...])
        go_y[half:, :] = over_y[half:, :]
        go_x[:half, :] = over_x[:half, :]
        go_x[half:, :] = both(over_x[half:, :], from_y[...])

    full, part = whole(rows, width), whole(half, width)
    return call(
        kernel,
        1,
        (over_x, over_y, from_x, from_y),
        [full] * 2 + [part] * 2,
        [full] * 2,
        [low_shape(rows, width)] * 2,
        0,
        earlier,
    )


def total_of(terms, dtype, *earlier, cost=0):
    rows, width = terms[0].shape
    wide = rows // 2 if rows % 32 == 0 else rows

    def kernel(*refs):
        total = refs[0][...].astype(jnp.float32)
        for ref in refs[1:-1]:
            total = total + ref[...].astype(jnp.float32)
        refs[-1][...] = total.astype(dtype)

    block = row_block(wide, width)
    shape = jax.ShapeDtypeStruct((rows, width), dtype)
    return call(kernel, rows // wide, tuple(terms), [block] * len(terms), block, shape, 0, earlier)


def norm_grad(grads, value, gain, beside):
    width = value.shape[1]
    grad = grads[0].astype(jnp.float32)
    for term in grads[1:]:
        grad = grad + term.astype(jnp.float32)
    value = value.astype(jnp.float32)
    scale = lax.rsqrt(jnp.sum(value * value, 1, keepdims=True) * (1.0 / width) + EPS)
    scaled = value * scale
    inner = grad * gain.astype(jnp.float32)
    mean = jnp.sum(inner * scaled, 1, keepdims=True) * (1.0 / width)
    return beside.astype(jnp.float32) + scale * (inner - scaled * mean)


def norm_backward(grads, value, gain, beside, *earlier):
    rows, width = value.shape
    terms = len(grads)
    wide = 96 if rows % 96 == 0 else rows

    def kernel(*refs):
        value, gain, beside, out = refs[terms:]
        grads = [ref[...] for ref in refs[:terms]]
        out[...] = norm_grad(grads, value[...], gain[...], beside[...]).astype(out.dtype)

    block = row_block(wide, width)
    return call(
        kernel,
        rows // wide,
        (*grads, value, gain.reshape(1, width), beside),
        [block] * (terms + 1) + [whole(1, width), block],
        block,
        low_shape(rows, width),
        0,
        earlier,
    )


def norm_split(grads, value, gain, beside, right, count, *earlier):
    rows, width = value.shape
    terms = len(grads)
    wide = right.shape[0] // count

    def kernel(*refs):
        value, gain, beside, right, total, rounded = refs[terms : terms + 6]
        out = refs[terms + 6 :]

        @pl.when(pl.program_id(0) == 0)
        def _():
            for at in [slice(start, start + 96) for start in range(0, rows, 96)] if rows % 96 == 0 else [slice(0, rows)]:
                one = norm_grad([ref[at, :] for ref in refs[:terms]], value[at, :], gain[...], beside[at, :])
                total[at, :] = one
                rounded[at, :] = one.astype(jnp.bfloat16)

        part = dot(rounded[...], right[...], NT).astype(jnp.bfloat16)
        for slot in range(count):

            @pl.when(pl.program_id(0) == slot)
            def _(slot=slot):
                out[slot][...] = part

    block = whole(rows, width)
    out = call(
        kernel,
        count,
        (*grads, value, gain.reshape(1, width), beside, right),
        [block] * (terms + 1) + [whole(1, width), block, row_block(wide, width)],
        [block] * 2 + [whole(rows, wide)] * count,
        [jax.ShapeDtypeStruct((rows, width), jnp.float32), low_shape(rows, width)]
        + [low_shape(rows, wide)] * count,
        HEAVY // 32,
        earlier,
    )
    return out[0], out[1], out[2:]


def widen(terms, weight, part=0, *earlier):
    rows, width = weight.shape
    wide = rows // 2 if rows % 32 == 0 else rows
    count = len(terms)

    def kernel(*refs):
        weight, out, share = refs[count:]
        total = refs[0][...].astype(jnp.float32)
        for ref in refs[1:count]:
            total = total + ref[...].astype(jnp.float32)
        out[...] = total
        share[...] = jnp.sum(total * weight[...].astype(jnp.float32), 1, keepdims=True)

    block = row_block(wide, width)
    return call(
        kernel,
        rows // wide,
        (*terms, weight),
        [pl.BlockSpec((wide, width), lambda f: (f, part))] * count + [block],
        [block, row_block(wide, 1)],
        [jax.ShapeDtypeStruct((rows, width), jnp.float32), jax.ShapeDtypeStruct((rows, 1), jnp.float32)],
        0,
        earlier,
    )


def widen_turned(value, part):
    rows, width = value.shape
    width = width // 2
    wide = 512 if width % 512 == 0 else width
    blocks = width // wide

    def kernel(source, target):
        target[...] = source[...].astype(jnp.float32).T

    return call(
        kernel,
        blocks,
        (value,),
        [pl.BlockSpec((rows, wide), lambda f: (0, part * blocks + f))],
        row_block(wide, rows),
        jax.ShapeDtypeStruct((width, rows), jnp.float32),
        0,
    )


def after(value, *earlier):
    return lax.optimization_barrier((value,) + earlier)[0]


def ring():
    count = lax.axis_size("tensor")
    return [0] + list(range(1, count, 2)) + list(range(2, count, 2))[::-1]


def ring_shift(value, by):
    order = ring()
    count = len(order)
    return lax.ppermute(value, "tensor", [(order[k], order[(k + by) % count]) for k in range(count)])


def slot_places():
    order = ring()
    count = len(order)
    me = lax.axis_index("tensor")
    at = sum(jnp.where(me == device, place, 0) for place, device in enumerate(order))
    back = (at - jnp.arange(count, dtype=jnp.int32)) % count
    return sum(jnp.where(back == place, device, 0) for place, device in enumerate(order)).astype(jnp.int32)


def ring_gather(piece, pauses=()):
    pauses = dict(pauses)
    slots = [piece]
    for step in range(1, lax.axis_size("tensor")):
        last = slots[-1]
        if step in pauses:
            last = tied(last, *pauses[step])
        slots.append(ring_shift(last, 1))
    return slots


def direct_gather(piece):
    return [piece] + [ring_shift(piece, by) for by in range(1, lax.axis_size("tensor"))]


def ring_scatter(parts, pauses=(), heavy=0):
    pauses = dict(pauses)
    count = len(parts)
    arrivals = []
    moving = parts[1]
    for step in range(1, count):
        arrivals.append(ring_shift(moving, 1))
        if step < count - 1:
            if step + 1 in pauses:
                moving = tied_sum(
                    arrivals[-1], parts[step + 1], HEAVY if step + 1 == heavy else 0, *pauses[step + 1]
                )
            else:
                moving = add(arrivals[-1], parts[step + 1])
    return (parts[0], arrivals[-1]), arrivals


def add(left, right):
    return (left.astype(jnp.float32) + right.astype(jnp.float32)).astype(jnp.bfloat16)


def exchange(parts):
    count = len(parts)
    return [parts[0]] + [ring_shift(parts[count - q], q) for q in range(1, count)]


def flip(value, bits):
    count = lax.axis_size("dp")
    return lax.ppermute(value, "dp", [(k, k ^ bits) for k in range(count)])


def cube_pairs(parts, *earlier):
    away, home = parts
    return cube_pair(home, flip(away, 1), *earlier)


def cube_turns(pairs, *earlier):
    _, over_x, over_y, top, bottom = pairs
    return cube_turn(over_x, over_y, flip(top, 2), flip(bottom, 4), *earlier)


def cube_terms(pairs, turns):
    return (pairs[0], flip(turns[0], 2), flip(turns[1], 4))


def cube_total(pairs, turns, dtype, *earlier):
    return total_of(cube_terms(pairs, turns), dtype, *earlier)


def gather_rows(piece):
    return lax.all_gather(piece, "dp", axis=0, tiled=True)


def gather_columns(piece):
    return lax.all_gather(piece, "dp", axis=1, tiled=True)


def sum_rows(value):
    return lax.psum_scatter(value, "dp", scatter_dimension=0, tiled=True)


def sum_columns(value):
    return lax.psum_scatter(value, "dp", scatter_dimension=1, tiled=True)


def gain_sums(shares, gains, places):
    count = places.shape[0]
    rows = shares[0].shape[0]
    start = lax.axis_index("dp") * rows
    own = [share[:, 0] / lax.dynamic_slice_in_dim(gain, start, rows, 0) for share, gain in zip(shares, gains)]
    cut = jnp.stack(own).reshape(len(own), count, -1)
    if count & (count - 1):
        pieces = [lax.dynamic_index_in_dim(cut, places[slot], 1, False) for slot in range(count)]
        return sum(exchange(pieces))
    me = lax.axis_index("tensor")
    total = cut.transpose(1, 0, 2).reshape(count, -1)
    bits = count // 2
    while bits:
        pair = total.reshape(2, bits, -1)
        mine = (me // bits) % 2
        keep = lax.dynamic_index_in_dim(pair, mine, 0, False)
        give = lax.dynamic_index_in_dim(pair, 1 - mine, 0, False)
        total = keep + lax.ppermute(give, "tensor", [(k, k ^ bits) for k in range(count)])
        bits //= 2
    return total.reshape(len(own), -1)


def normalize(value, gain):
    scale = lax.rsqrt(jnp.mean(value * value, axis=1, keepdims=True) + EPS)
    return (value * scale * gain[None, :], scale)


def per_device(
    tokens, lengths, attention_gain, w_inputs, w_output, feed_gain, w_gate, w_up, w_down, cotangent
):
    count = lax.axis_size("tensor")
    groups = KV // count
    local, width = tokens.shape
    rows = local * count
    low = jnp.bfloat16
    held = tables(lengths[0], rows)
    sequences = lengths.shape[1]
    gain_one = attention_gain.astype(jnp.float32)
    gain_two = feed_gain.astype(jnp.float32)

    places = slot_places()
    base = tokens.astype(jnp.float32)
    first = normalize(base, gain_one)[0].astype(low)
    inputs_full = gather_rows(w_inputs)
    first_slots = ring_gather(first)
    output_line = jnp.concatenate(direct_gather(w_output), 0)
    output_full = gather_columns(output_line)
    gate_full = gather_rows(w_gate)
    up_full = gather_rows(w_up)
    down_full = gather_columns(w_down)

    joint = project(first_slots, inputs_full, places)
    heads, query, key, value = attention_forward(joint, held, sequences, groups)
    grad_slots = ring_gather(tied(cotangent, first_slots[-1]))
    heads_own = exchange(to_slots(heads, places, grad_slots[1]))
    mixed = base + dot(jnp.concatenate(heads_own, 1), output_full)
    second = tied(normalize(mixed, gain_two)[0].astype(low), grad_slots[min(2, count - 1)])
    second_slots = ring_gather(second)
    half = max(count // 2, 1)
    ahead = feed_forward(second_slots[:half], gate_full, up_full)
    rest = feed_forward(second_slots[half:], gate_full, up_full)
    hidden, slope, silu = [list(one) + list(two) for one, two in zip(ahead, rest)]
    block_parts = product(hidden, down_full)
    down_wpart = weight_grad(hidden, grad_slots, block_parts[0])
    down_wgrad = sum_columns(down_wpart)
    gate_grad, up_grad = feed_backward(grad_slots, down_full, slope, silu, down_wpart)
    block_moving = ring_shift(block_parts[1], 1)
    pick = lambda slots: ((([gate_grad[s] for s in slots]), gate_full), ([up_grad[s] for s in slots], up_full))
    part_one = sum_of_products(pick([1]), block_moving)
    others = [0] + list(range(2, count))
    part_others = sum_of_products(pick(others), part_one[0])
    second_parts = [part_others[0], part_one[0]] + list(part_others[1:])
    second_early = ring_shift(second_parts[1], 1)
    gate_wpart = weight_grad(second_slots, gate_grad, second_early, part_others[0])
    gate_wgrad = sum_rows(gate_wpart)
    second_grad, second_back = ring_scatter(second_parts, {3: [gate_wpart, down_wgrad]}, 3)
    up_wpart = weight_grad(second_slots, up_grad, second_back[1])
    up_wgrad = sum_rows(up_wpart)

    mixed_total, branch, heads_back = norm_split(
        second_grad, mixed, gain_two, cotangent, output_full, count, up_wpart
    )
    heads_grad = exchange(heads_back)
    block_sum, block_back = ring_scatter(block_parts, {2: [gate_grad[0]], 3: [heads_grad[-1]]})
    cube = lax.axis_size("dp") == 8
    output_parts = cube_columns(heads_own, branch) if cube else ()
    joint_grad = attention_backward(
        query, key, value, heads, heads_grad, places, held, groups, block_back[1], gate_wgrad, *output_parts[:1]
    )
    first_one = spread_product(joint_grad, inputs_full, places, [1], block_back[2])
    first_others = spread_product(joint_grad, inputs_full, places, others, first_one[0])
    first_parts = [first_others[0], first_one[0]] + list(first_others[1:])
    gate_wgrad, gate_share = widen([gate_wgrad], w_gate)
    down_grad = total_of([down_wgrad], jnp.float32)
    if cube:
        output_pairs = cube_pairs(output_parts, first_one[0])
        inputs_parts = cube_rows(first_slots, joint_grad, places, HEAVY, output_pairs[0])
        second_pause = [inputs_parts[0]]
        first_next = tied_sum(ring_shift(first_parts[1], 1), first_parts[2], 0, *second_pause)
        output_turns = cube_turns(output_pairs, first_next)
        inputs_sums = cube_sums(inputs_parts, output_turns[0])
        third_pause = [inputs_sums[0], gate_wgrad, up_wgrad]
        first_last = tied_sum(ring_shift(first_next, 1), first_parts[3], 0, *third_pause)
        output_cut = total_slots(cube_terms(output_pairs, output_turns), count, first_last)
        first_grad, first_back = ring_scatter(first_parts, {2: second_pause, 3: third_pause})
        block_out = total_of((*block_sum, mixed), low, first_last, cost=HEAVY)
        inputs_terms = [inputs_sums[0]] + [flip(inputs_sums[at], 2 * at) for at in range(1, 4)]
        inputs_grad, inputs_share = widen(inputs_terms, w_inputs, 0, output_cut[0])
    else:
        first_grad, first_back = ring_scatter(first_parts)
        block_out = total_of((*block_sum, mixed), low)
        output_sum = sum_columns(weight_grad([jnp.concatenate(heads_own, 1)], [branch]))
        inputs_grad = sum_rows(weight_grad(first_slots, to_slots(joint_grad, places)))
        inputs_grad, inputs_share = widen([inputs_grad], w_inputs)
        output_sum = output_sum.reshape(count, -1, output_sum.shape[1])
        output_cut = [output_sum[slot] for slot in range(count)]
    tokens_grad = norm_backward(first_grad, tokens, gain_one, mixed_total, block_out)
    up_wgrad, up_share = widen([up_wgrad], w_up, 0, output_cut[0])
    gain_grads = gain_sums([inputs_share, gate_share + up_share], [gain_one, gain_two], places)
    output_grad = exchange(output_cut)
    output_grad = total_of(output_grad, jnp.float32, tokens_grad)
    return (
        block_out,
        tokens_grad,
        gain_grads[0],
        inputs_grad,
        output_grad,
        gain_grads[1],
        gate_wgrad,
        up_wgrad,
        down_grad,
    )


def solution(mesh):
    in_specs = (
        P(("dp", "tensor"), None),
        P("dp", None),
        P(),
        P("dp", "tensor"),
        P("tensor", "dp"),
        P(),
        P("dp", "tensor"),
        P("dp", "tensor"),
        P("tensor", "dp"),
        P(("dp", "tensor"), None),
    )
    out_specs = (
        P(("dp", "tensor"), None),
        P(("dp", "tensor"), None),
        P(("dp", "tensor")),
        P("dp", "tensor"),
        P("tensor", "dp"),
        P(("dp", "tensor")),
        P("dp", "tensor"),
        P("dp", "tensor"),
        P("tensor", "dp"),
    )
    return jax.shard_map(
        per_device, mesh=mesh, in_specs=in_specs, out_specs=out_specs, check_vma=False
    )
```

```python
import math

import jax
import jax.numpy as jnp
from jax import lax
from jax.experimental import pallas as pl
from jax.experimental.pallas import tpu as pltpu
from jax.sharding import PartitionSpec as P

KV = 8
HD = 64
QPK = 4
EPS = 1e-05
THETA = 500000.0
FLOOR = -1e30
LANES = 128
BLOCK = 128
PARTS = 3
VMEM = 56 << 20
HEAVY = 10**12
NT = (((1,), (1,)), ((), ()))
NN = (((1,), (0,)), ((), ()))
TN = (((0,), (0,)), ((), ()))


def layout(lens, rows_count):
    ends = jnp.cumsum(lens)
    rows = jnp.arange(rows_count, dtype=jnp.int32)
    segment = jnp.sum((rows[:, None] >= ends[None, :]).astype(jnp.int32), axis=1)
    starts = ends - lens
    numbers = jnp.arange(lens.shape[0], dtype=jnp.int32)
    picked = jnp.where(segment[:, None] == numbers[None, :], starts[None, :], 0)
    return segment, rows - jnp.sum(picked, axis=1)


def tables(lens, rows_count):
    segment, position = layout(lens, rows_count)
    index = (jnp.arange(LANES, dtype=jnp.int32) % (HD // 2)).astype(jnp.float32)
    inverse = jnp.exp(index * (-2.0 * math.log(THETA) / HD))
    angle = position.astype(jnp.float32)[:, None] * inverse[None, :]
    count = lens.shape[0]
    lane = jnp.arange(LANES, dtype=jnp.int32)[None, :] - HD
    same = lane == segment[:, None]
    inside = (lane >= 0) & (lane < count)
    extra = (lane >= count) & (lane < count + PARTS)
    key_lanes = jnp.where((same & inside) | extra, 1.0, 0.0).astype(jnp.bfloat16)
    query_lanes = jnp.where(inside & ~same, FLOOR, 0.0).astype(jnp.bfloat16)
    return jnp.cos(angle), jnp.sin(angle), query_lanes, key_lanes


def dot(left, right, dims=NN):
    return lax.dot_general(left, right, dims, preferred_element_type=jnp.float32)


def rotate(value, cosine, sine):
    low = lax.broadcasted_iota(jnp.int32, value.shape, 1) % HD < HD // 2
    up = pltpu.roll(value, LANES - HD // 2, 1)
    down = pltpu.roll(value, HD // 2, 1)
    return value * cosine + jnp.where(low, -up, down) * sine


def unrotate(value, cosine, sine):
    low = lax.broadcasted_iota(jnp.int32, value.shape, 1) % HD < HD // 2
    scaled = value * sine
    up = pltpu.roll(scaled, LANES - HD // 2, 1)
    down = pltpu.roll(scaled, HD // 2, 1)
    return value * cosine + jnp.where(low, up, -down)


def split(value, parts):
    out = []
    for _ in range(parts):
        piece = value.astype(jnp.bfloat16).astype(jnp.float32)
        out.append(piece)
        value = value - piece
    return out


def forward_kernel(count, joint, cos, sin, query_lanes, key_lanes, heads, query, key, value):
    rows = joint.shape[0]
    cosine, sine = cos[...], sin[...]
    lane = lax.broadcasted_iota(jnp.int32, (rows, LANES), 1)
    left = lane < HD
    beside = query_lanes[...].astype(jnp.float32)
    for pair in range(QPK // 2):
        both = rotate(joint[:, pair * LANES : (pair + 1) * LANES], cosine, sine) * (1.0 / math.sqrt(HD))
        query[2 * pair] = jnp.where(left, both, beside).astype(jnp.bfloat16)
        query[2 * pair + 1] = jnp.where(left, pltpu.roll(both, HD, 1), beside).astype(jnp.bfloat16)
    last = joint[:, QPK * HD : QPK * HD + LANES]
    key[...] = jnp.where(left, rotate(last, cosine, sine), key_lanes[...].astype(jnp.float32)).astype(
        jnp.bfloat16
    )
    ones = jnp.where((lane >= HD) & (lane < HD + PARTS), 1.0, 0.0)
    value[...] = jnp.where(left, pltpu.roll(last, HD, 1), ones).astype(jnp.bfloat16)
    lower = lax.broadcasted_iota(jnp.int32, (BLOCK, BLOCK), 1) <= lax.broadcasted_iota(
        jnp.int32, (BLOCK, BLOCK), 0
    )
    lower = jnp.concatenate([lower] * QPK, 0)
    narrow = lax.broadcasted_iota(jnp.int32, (QPK * BLOCK, LANES), 1)
    for block in range(rows // BLOCK):
        start = block * BLOCK
        end = start + BLOCK
        own = query[:, start:end, :].reshape(QPK * BLOCK, LANES)
        near = jnp.where(lower, dot(own, key[start:end, :], NT), FLOOR)
        top = jnp.max(near, 1, keepdims=True)
        if block:
            far = dot(own, key[0:start, :], NT)
            top = jnp.maximum(top, jnp.max(far, 1, keepdims=True))
        out = dot(jnp.exp(near - top).astype(jnp.bfloat16), value[start:end, :])
        if block:
            out = out + dot(jnp.exp(far - top).astype(jnp.bfloat16), value[0:start, :])
        total = out[:, HD : HD + 1]
        out = out * (1.0 / total)
        held = own.astype(jnp.float32)
        for part, piece in enumerate(split(top + jnp.log(total), PARTS)):
            held = jnp.where(narrow == HD + count + part, -piece, held)
        query[:, start:end, :] = held.astype(jnp.bfloat16).reshape(QPK, BLOCK, LANES)
        each = [out[head * BLOCK : (head + 1) * BLOCK] for head in range(QPK)]
        half = narrow[:BLOCK] < HD
        for pair in range(QPK // 2):
            heads[start:end, pair * LANES : (pair + 1) * LANES] = jnp.where(
                half, each[2 * pair], pltpu.roll(each[2 * pair + 1], HD, 1)
            ).astype(jnp.bfloat16)


def whole(*shape):
    return pl.BlockSpec(shape, lambda g: (0,) * len(shape))


def grouped(*shape):
    return pl.BlockSpec((None,) + shape, lambda g: (g,) + (0,) * len(shape))


def columns(rows, width):
    return pl.BlockSpec((rows, width), lambda g: (0, g))


def attention_forward(joint, held, count, groups):
    rows = joint.shape[0]
    shape = jax.ShapeDtypeStruct
    low = jnp.bfloat16
    return pl.pallas_call(
        lambda *refs: forward_kernel(count, *refs),
        grid=(groups,),
        in_specs=[columns(rows, (QPK + 2) * HD)] + [whole(rows, LANES)] * 4,
        out_specs=[
            columns(rows, QPK * HD),
            grouped(QPK, rows, LANES),
            grouped(rows, LANES),
            grouped(rows, LANES),
        ],
        out_shape=[
            shape((rows, groups * QPK * HD), low),
            shape((groups, QPK, rows, LANES), low),
            shape((groups, rows, LANES), low),
            shape((groups, rows, LANES), low),
        ],
        compiler_params=pltpu.CompilerParams(vmem_limit_bytes=VMEM),
        cost_estimate=pl.CostEstimate(
            flops=groups * 12 * rows * rows * QPK * HD,
            bytes_accessed=1 << 20,
            transcendentals=0,
        ),
    )(joint, *held)


def backward_kernel(count, *refs):
    query, key, value, heads = refs[:4]
    places, cos, sin = refs[4 + count : 7 + count]
    out, grads, query_grad, key_grad, value_grad = refs[-5:]
    rows = key.shape[0]
    local = rows // count
    for slot in range(count):
        start = pl.multiple_of(places[slot] * local, 16)
        grads[pl.ds(start, local), :] = refs[4 + slot][...]
    key_grad[...] = jnp.zeros_like(key_grad)
    value_grad[...] = jnp.zeros_like(value_grad)
    turned = key[...].astype(jnp.float32).T.astype(jnp.bfloat16)
    upper = lax.broadcasted_iota(jnp.int32, (BLOCK, BLOCK), 0) <= lax.broadcasted_iota(
        jnp.int32, (BLOCK, BLOCK), 1
    )
    upper = jnp.concatenate([upper] * QPK, 1)
    lane = lax.broadcasted_iota(jnp.int32, (QPK * BLOCK, LANES), 1)
    half = lane[:BLOCK] < HD

    def stacked(ref, start, end):
        pieces = []
        for pair in range(QPK // 2):
            both = ref[start:end, pair * LANES : (pair + 1) * LANES].astype(jnp.float32)
            pieces += [both, pltpu.roll(both, HD, 1)]
        return jnp.where(lane < HD, jnp.concatenate(pieces, 0), 0.0)

    for block in range(rows // BLOCK):
        start = block * BLOCK
        end = start + BLOCK
        own = query[:, start:end, :].reshape(QPK * BLOCK, LANES)
        grad = stacked(grads, start, end)
        inner = jnp.sum(grad * stacked(heads, start, end), 1, keepdims=True)
        low = grad.astype(jnp.bfloat16)
        for part, piece in enumerate(split(inner, PARTS)):
            grad = jnp.where(lane == HD + part, -piece, grad)
        beside = grad.astype(jnp.bfloat16)
        turned_grad = None
        for first, last in ([(0, start)] if block else []) + [(start, end)]:
            scores = dot(key[first:last, :], own, NT)
            if first == start:
                scores = jnp.where(upper, scores, FLOOR)
            probs = jnp.exp(scores)
            score_grad = (probs * dot(value[first:last, :], beside, NT)).astype(jnp.bfloat16)
            value_grad[first:last, :] += dot(probs.astype(jnp.bfloat16), low)
            key_grad[first:last, :] += dot(score_grad, own)
            piece = dot(turned[:, first:last], score_grad)
            turned_grad = piece if turned_grad is None else turned_grad + piece
        back = turned_grad.T * (1.0 / math.sqrt(HD))
        each = [back[head * BLOCK : (head + 1) * BLOCK] for head in range(QPK)]
        for pair in range(QPK // 2):
            query_grad[start:end, pair * LANES : (pair + 1) * LANES] = jnp.where(
                half, each[2 * pair], pltpu.roll(each[2 * pair + 1], HD, 1)
            )
    cosine, sine = cos[...], sin[...]
    for pair in range(QPK // 2):
        at = slice(pair * LANES, (pair + 1) * LANES)
        out[:, at] = unrotate(query_grad[:, at], cosine, sine).astype(jnp.bfloat16)
    left = lax.broadcasted_iota(jnp.int32, (rows, LANES), 1) < HD
    key_part = unrotate(jnp.where(left, key_grad[...], 0.0), cosine, sine)
    out[:, QPK * HD : QPK * HD + LANES] = jnp.where(
        left, key_part, pltpu.roll(value_grad[...], HD, 1)
    ).astype(jnp.bfloat16)


def attention_backward(query, key, value, heads, slots, places, held, groups, *earlier):
    rows = key.shape[1]
    wide = (QPK + 2) * HD
    count = len(slots)
    operands = (query, key, value, heads, *slots, places, held[0], held[1])
    return call(
        lambda *refs: backward_kernel(count, *refs),
        groups,
        operands,
        [grouped(QPK, rows, LANES), grouped(rows, LANES), grouped(rows, LANES), columns(rows, QPK * HD)]
        + [columns(rows // count, QPK * HD)] * count
        + [pl.BlockSpec(memory_space=pltpu.SMEM)]
        + [whole(rows, LANES)] * 2,
        columns(rows, wide),
        jax.ShapeDtypeStruct((rows, groups * wide), jnp.bfloat16),
        HEAVY,
        earlier,
        [
            pltpu.VMEM((rows, QPK * HD), jnp.bfloat16),
            pltpu.VMEM((rows, QPK * HD), jnp.float32),
            pltpu.VMEM((rows, LANES), jnp.float32),
            pltpu.VMEM((rows, LANES), jnp.float32),
        ],
    )


def call(kernel, grid, operands, specs, out_specs, out_shape, flops, earlier=(), scratch=()):
    count, extra = len(operands), len(earlier)
    return pl.pallas_call(
        lambda *refs: kernel(*refs[:count], *refs[count + extra :]),
        grid=(grid,),
        in_specs=specs + [pl.BlockSpec(memory_space=pl.ANY)] * extra,
        out_specs=out_specs,
        out_shape=out_shape,
        scratch_shapes=list(scratch),
        compiler_params=pltpu.CompilerParams(vmem_limit_bytes=VMEM),
        cost_estimate=pl.CostEstimate(flops=flops, bytes_accessed=1 << 20, transcendentals=0),
    )(*operands, *earlier)


def column_block(rows, wide):
    return pl.BlockSpec((rows, wide), lambda f: (0, f))


def row_block(wide, width):
    return pl.BlockSpec((wide, width), lambda f: (f, 0))


def low_shape(*shape):
    return jax.ShapeDtypeStruct(shape, jnp.bfloat16)


def block_size(extent):
    return 256 if extent % 256 == 0 else extent


def tied(value, *earlier):
    rows, width = value.shape
    wide = rows // 2 if rows % 32 == 0 else rows

    def kernel(source, target):
        target[...] = source[...]

    block = row_block(wide, width)
    return call(kernel, rows // wide, (value,), [block], block, low_shape(rows, width), 0, earlier)


def tied_sum(left, right, weight, *earlier):
    rows, width = left.shape
    wide = rows // 2 if rows % 32 == 0 else rows

    def kernel(left, right, out):
        out[...] = (left[...].astype(jnp.float32) + right[...].astype(jnp.float32)).astype(out.dtype)

    block = row_block(wide, width)
    return call(
        kernel, rows // wide, (left, right), [block] * 2, block, low_shape(rows, width), weight, earlier
    )


def project(slots, weight, places):
    count = len(slots)
    local, width = slots[0].shape
    extent = weight.shape[1]
    wide = block_size(extent)

    def kernel(*refs):
        places, weight, out = refs[count], refs[count + 1], refs[count + 2]
        for slot in range(count):
            start = pl.multiple_of(places[slot] * local, 16)
            out[pl.ds(start, local), :] = dot(refs[slot][...], weight[...])

    return call(
        kernel,
        extent // wide,
        (*slots, places, weight),
        [whole(local, width)] * count
        + [pl.BlockSpec(memory_space=pltpu.SMEM), column_block(width, wide)],
        column_block(count * local, wide),
        jax.ShapeDtypeStruct((count * local, extent), jnp.float32),
        2 * count * local * width * extent,
    )


def to_slots(value, places, *earlier):
    count = places.shape[0]
    rows, width = value.shape
    local = rows // count

    def kernel(value, places, *out):
        for slot in range(count):
            start = pl.multiple_of(places[slot] * local, 16)
            out[slot][...] = value[pl.ds(start, local), :]

    return call(
        kernel,
        1,
        (value, places),
        [whole(rows, width), pl.BlockSpec(memory_space=pltpu.SMEM)],
        [whole(local, width)] * count,
        [low_shape(local, width)] * count,
        0,
        earlier,
    )


def from_slots(slots, places, *earlier):
    count = len(slots)
    local, width = slots[0].shape

    def kernel(*refs):
        for slot in range(count):
            start = pl.multiple_of(refs[count][slot] * local, 16)
            refs[-1][pl.ds(start, local), :] = refs[slot][...]

    return call(
        kernel,
        1,
        (*slots, places),
        [whole(local, width)] * count + [pl.BlockSpec(memory_space=pltpu.SMEM)],
        whole(count * local, width),
        low_shape(count * local, width),
        0,
        earlier,
    )


def feed_forward(slots, w_gate, w_up, *earlier):
    count = len(slots)
    rows, width = slots[0].shape
    extent = w_gate.shape[1]
    wide = block_size(extent)

    def kernel(*refs):
        w_gate, w_up = refs[count], refs[count + 1]
        out = refs[count + 2 :]
        for slot in range(count):
            one = dot(refs[slot][...], w_gate[...])
            two = dot(refs[slot][...], w_up[...])
            sigma = jax.nn.sigmoid(one)
            silu = one * sigma
            slope = two * (sigma + silu * (1.0 - sigma))
            out[slot][...] = (silu * two).astype(jnp.bfloat16)
            out[count + slot][...] = slope.astype(jnp.bfloat16)
            out[2 * count + slot][...] = silu.astype(jnp.bfloat16)

    out = call(
        kernel,
        extent // wide,
        (*slots, w_gate, w_up),
        [whole(rows, width)] * count + [column_block(width, wide)] * 2,
        [column_block(rows, wide)] * (3 * count),
        [low_shape(rows, extent)] * (3 * count),
        4 * count * rows * width * extent,
        earlier,
    )
    return out[:count], out[count : 2 * count], out[2 * count :]


def feed_backward(grads, w_down, slopes, silus, *earlier):
    count = len(grads)
    rows, width = grads[0].shape
    extent = w_down.shape[0]
    wide = block_size(extent)

    def kernel(*refs):
        w_down = refs[3 * count]
        out = refs[3 * count + 1 :]
        for slot in range(count):
            hidden_grad = dot(refs[slot][...], w_down[...], NT)
            slope = refs[count + slot][...].astype(jnp.float32)
            silu = refs[2 * count + slot][...].astype(jnp.float32)
            out[slot][...] = (hidden_grad * slope).astype(jnp.bfloat16)
            out[count + slot][...] = (hidden_grad * silu).astype(jnp.bfloat16)

    out = call(
        kernel,
        extent // wide,
        (*grads, *slopes, *silus, w_down),
        [whole(rows, width)] * count
        + [column_block(rows, wide)] * (2 * count)
        + [row_block(wide, width)],
        [column_block(rows, wide)] * (2 * count),
        [low_shape(rows, extent)] * (2 * count),
        2 * count * rows * width * extent,
        earlier,
    )
    return out[:count], out[count:]


def sum_of_products(terms, *earlier):
    count = len(terms[0][0])
    rows, depth = terms[0][0][0].shape
    extent = terms[0][1].shape[0]
    wide = block_size(extent)
    total = len(terms)

    def kernel(*refs):
        weights = refs[total * count : total * count + total]
        out = refs[total * count + total :]
        for slot in range(count):
            sums = dot(refs[slot][...], weights[0][...], NT)
            for term in range(1, total):
                sums = sums + dot(refs[term * count + slot][...], weights[term][...], NT)
            out[slot][...] = sums.astype(jnp.bfloat16)

    slots = [slot for term in terms for slot in term[0]]
    return call(
        kernel,
        extent // wide,
        (*slots, *[term[1] for term in terms]),
        [whole(rows, depth)] * (total * count) + [row_block(wide, depth)] * total,
        [column_block(rows, wide)] * count,
        [low_shape(rows, extent)] * count,
        2 * total * count * rows * depth * extent,
        earlier,
    )


def product(slots, right, *earlier):
    count = len(slots)
    rows, depth = slots[0].shape
    extent = right.shape[1]
    wide = block_size(extent)

    def kernel(*refs):
        for slot in range(count):
            refs[count + 1 + slot][...] = dot(refs[slot][...], refs[count][...]).astype(jnp.bfloat16)

    return call(
        kernel,
        extent // wide,
        (*slots, right),
        [whole(rows, depth)] * count + [column_block(depth, wide)],
        [column_block(rows, wide)] * count,
        [low_shape(rows, extent)] * count,
        2 * count * rows * depth * extent,
        earlier,
    )


def weight_grad(lefts, rights, *earlier, half=None, into=None):
    count = len(lefts)
    rows, extent = lefts[0].shape
    width = rights[0].shape[1]
    wide = block_size(extent)
    narrow = 512 if width % 512 == 0 else width
    total = 2 * count + (into is not None) + len(earlier)

    def kernel(*refs):
        out, left, right = refs[total:]

        @pl.when(pl.program_id(0) == 0)
        def _():
            for slot in range(count):
                right[slot * rows : (slot + 1) * rows, :] = refs[count + slot][...]

        for slot in range(count):
            left[slot * rows : (slot + 1) * rows, :] = refs[slot][...]
        for start in range(0, width, narrow):
            at = slice(start, start + narrow)
            out[:, at] = dot(left[...], right[:, at], TN).astype(jnp.bfloat16)

    held = () if into is None else (into,)
    return pl.pallas_call(
        kernel,
        grid=(extent // wide,),
        in_specs=[column_block(rows, wide)] * count
        + [whole(rows, width)] * count
        + [pl.BlockSpec(memory_space=pl.ANY)] * (len(held) + len(earlier)),
        out_specs=pl.BlockSpec((wide, width), lambda f: (f, half or 0)),
        out_shape=low_shape(extent, width if half is None else 2 * width),
        input_output_aliases={} if into is None else {2 * count: 0},
        scratch_shapes=[
            pltpu.VMEM((count * rows, wide), jnp.bfloat16),
            pltpu.VMEM((count * rows, width), jnp.bfloat16),
        ],
        compiler_params=pltpu.CompilerParams(vmem_limit_bytes=VMEM),
        cost_estimate=pl.CostEstimate(
            flops=2 * count * rows * width * extent, bytes_accessed=1 << 20, transcendentals=0
        ),
    )(*lefts, *rights, *held, *earlier)


def spread_product(value, weight, places, slots, *earlier):
    count = places.shape[0]
    rows, depth = value.shape
    local = rows // count
    extent = weight.shape[0]
    wide = extent // 2 if extent % 512 == 0 else extent

    def kernel(value, places, weight, *out):
        for at, slot in enumerate(slots):
            start = pl.multiple_of(places[slot] * local, 16)
            out[at][...] = dot(value[pl.ds(start, local), :], weight[...], NT).astype(jnp.bfloat16)

    return call(
        kernel,
        extent // wide,
        (value, places, weight),
        [whole(rows, depth), pl.BlockSpec(memory_space=pltpu.SMEM), row_block(wide, depth)],
        [column_block(local, wide)] * len(slots),
        [low_shape(local, extent)] * len(slots),
        2 * len(slots) * local * depth * extent,
        earlier,
    )


def cube_call(kernel, operands, specs, piece, scratch, flops, earlier):
    count, extra = len(operands), len(earlier)

    def body(me, *refs):
        away, home = refs[count + extra : count + extra + 2]
        value = kernel(*refs[:count], *refs[count + extra + 2 :])
        step = pl.program_id(0)

        @pl.when(step < 4)
        def _():
            away[...] = value

        @pl.when(step >= 4)
        def _():
            home[...] = value

    me = lax.axis_index("dp").astype(jnp.int32).reshape(1)
    return pl.pallas_call(
        body,
        grid_spec=pltpu.PrefetchScalarGridSpec(
            num_scalar_prefetch=1,
            grid=(8,),
            in_specs=specs + [pl.BlockSpec(memory_space=pl.ANY)] * extra,
            out_specs=[
                pl.BlockSpec((None,) + piece, lambda i, me: (jnp.minimum(i, 3), 0, 0)),
                pl.BlockSpec((None,) + piece, lambda i, me: (jnp.maximum(i - 4, 0), 0, 0)),
            ],
            scratch_shapes=scratch,
        ),
        out_shape=[low_shape(4, *piece)] * 2,
        compiler_params=pltpu.CompilerParams(vmem_limit_bytes=VMEM),
        cost_estimate=pl.CostEstimate(flops=flops, bytes_accessed=1 << 20, transcendentals=0),
    )(me, *operands, *earlier)


def cube_place(step, me):
    return jnp.bitwise_xor(me[0], 2 * (step % 4) + 1 - step // 4)


def cube_columns(lefts, right, *earlier):
    count = len(lefts)
    rows, wide = lefts[0].shape
    block = right.shape[1] // 8

    def kernel(*refs):
        left = refs[-1]

        @pl.when(pl.program_id(0) == 0)
        def _():
            for slot in range(count):
                turned = refs[slot][...].astype(jnp.float32).T
                left[slot * wide : (slot + 1) * wide, :] = turned.astype(jnp.bfloat16)

        return dot(left[...], refs[count][...]).astype(jnp.bfloat16)

    fixed = pl.BlockSpec((rows, wide), lambda i, me: (0, 0))
    moving = pl.BlockSpec((rows, block), lambda i, me: (0, cube_place(i, me)))
    scratch = [pltpu.VMEM((count * wide, rows), jnp.bfloat16)]
    flops = 2 * rows * count * wide * right.shape[1]
    piece = (count * wide, block)
    return cube_call(kernel, (*lefts, right), [fixed] * count + [moving], piece, scratch, flops, earlier)


def cube_rows(lefts, right, places, cost, *earlier):
    count = len(lefts)
    rows, width = lefts[0].shape
    extent = right.shape[1]
    block = width // 8

    def kernel(*refs):
        left, turned = refs[-2:]

        @pl.when(pl.program_id(0) == 0)
        def _():
            for slot in range(count):
                start = pl.multiple_of(refs[count + 1][slot] * rows, 16)
                turned[slot * rows : (slot + 1) * rows, :] = refs[count][pl.ds(start, rows), :]

        for slot in range(count):
            left[slot * rows : (slot + 1) * rows, :] = refs[slot][...]
        return dot(left[...], turned[...], TN).astype(jnp.bfloat16)

    moving = pl.BlockSpec((rows, block), lambda i, me: (0, cube_place(i, me)))
    fixed = pl.BlockSpec((count * rows, extent), lambda i, me: (0, 0))
    scratch = [
        pltpu.VMEM((count * rows, block), jnp.bfloat16),
        pltpu.VMEM((count * rows, extent), jnp.bfloat16),
    ]
    specs = [moving] * count + [fixed, pl.BlockSpec(memory_space=pltpu.SMEM)]
    return cube_call(kernel, (*lefts, right, places), specs, (block, extent), scratch, cost, earlier)


def cube_pair(home, arrived, *earlier):
    _, rows, width = home.shape
    half = rows // 2

    def kernel(home, arrived, own, over_x, over_y, top, bottom):
        total = lambda at: (
            home[at].astype(jnp.float32) + arrived[at].astype(jnp.float32)
        ).astype(jnp.bfloat16)
        own[...] = total(0)
        over_x[...] = total(1)
        over_y[...] = total(2)
        corner = total(3)
        top[...] = corner[:half]
        bottom[...] = corner[half:]

    full, part = whole(rows, width), whole(half, width)
    return call(
        kernel,
        1,
        (home, arrived),
        [whole(4, rows, width)] * 2,
        [full] * 3 + [part] * 2,
        [low_shape(rows, width)] * 3 + [low_shape(half, width)] * 2,
        0,
        earlier,
    )


def cube_sums(parts, *earlier):
    away, home = parts
    arrived = flip(away, 1)
    _, rows, width = home.shape

    def kernel(home, arrived, *out):
        for at in range(4):
            total = home[at].astype(jnp.float32) + arrived[at].astype(jnp.float32)
            out[at][...] = total.astype(jnp.bfloat16)

    return call(
        kernel,
        1,
        (home, arrived),
        [whole(4, rows, width)] * 2,
        [whole(rows, width)] * 4,
        [low_shape(rows, width)] * 4,
        0,
        earlier,
    )


def total_slots(terms, count, *earlier):
    rows, width = terms[0].shape
    local = rows // count

    def kernel(*refs):
        for slot in range(count):
            at = slice(slot * local, (slot + 1) * local)
            total = refs[0][at, :].astype(jnp.float32)
            for ref in refs[1 : len(terms)]:
                total = total + ref[at, :].astype(jnp.float32)
            refs[len(terms) + slot][...] = total.astype(jnp.bfloat16)

    return call(
        kernel,
        1,
        tuple(terms),
        [whole(rows, width)] * len(terms),
        [whole(local, width)] * count,
        [low_shape(local, width)] * count,
        0,
        earlier,
    )


def cube_turn(over_x, over_y, from_x, from_y, *earlier):
    rows, width = over_x.shape
    half = rows // 2

    def kernel(over_x, over_y, from_x, from_y, go_x, go_y):
        both = lambda one, two: (one.astype(jnp.float32) + two.astype(jnp.float32)).astype(jnp.bfloat16)
        go_y[:half, :] = both(over_y[:half, :], from_x[...])
        go_y[half:, :] = over_y[half:, :]
        go_x[:half, :] = over_x[:half, :]
        go_x[half:, :] = both(over_x[half:, :], from_y[...])

    full, part = whole(rows, width), whole(half, width)
    return call(
        kernel,
        1,
        (over_x, over_y, from_x, from_y),
        [full] * 2 + [part] * 2,
        [full] * 2,
        [low_shape(rows, width)] * 2,
        0,
        earlier,
    )


def total_of(terms, dtype, *earlier, cost=0):
    rows, width = terms[0].shape
    wide = rows // 2 if rows % 32 == 0 else rows

    def kernel(*refs):
        total = refs[0][...].astype(jnp.float32)
        for ref in refs[1:-1]:
            total = total + ref[...].astype(jnp.float32)
        refs[-1][...] = total.astype(dtype)

    block = row_block(wide, width)
    shape = jax.ShapeDtypeStruct((rows, width), dtype)
    return call(kernel, rows // wide, tuple(terms), [block] * len(terms), block, shape, 0, earlier)


def norm_grad(grads, value, gain, beside):
    width = value.shape[1]
    grad = grads[0].astype(jnp.float32)
    for term in grads[1:]:
        grad = grad + term.astype(jnp.float32)
    value = value.astype(jnp.float32)
    scale = lax.rsqrt(jnp.sum(value * value, 1, keepdims=True) * (1.0 / width) + EPS)
    scaled = value * scale
    inner = grad * gain.astype(jnp.float32)
    mean = jnp.sum(inner * scaled, 1, keepdims=True) * (1.0 / width)
    return beside.astype(jnp.float32) + scale * (inner - scaled * mean)


def norm_backward(grads, value, gain, beside, *earlier):
    rows, width = value.shape
    terms = len(grads)
    wide = 96 if rows % 96 == 0 else rows

    def kernel(*refs):
        value, gain, beside, out = refs[terms:]
        grads = [ref[...] for ref in refs[:terms]]
        out[...] = norm_grad(grads, value[...], gain[...], beside[...]).astype(out.dtype)

    block = row_block(wide, width)
    return call(
        kernel,
        rows // wide,
        (*grads, value, gain.reshape(1, width), beside),
        [block] * (terms + 1) + [whole(1, width), block],
        block,
        low_shape(rows, width),
        0,
        earlier,
    )


def norm_split(grads, value, gain, beside, right, count, *earlier):
    rows, width = value.shape
    terms = len(grads)
    wide = right.shape[0] // count

    def kernel(*refs):
        value, gain, beside, right, total, rounded = refs[terms : terms + 6]
        out = refs[terms + 6 :]

        @pl.when(pl.program_id(0) == 0)
        def _():
            for at in [slice(start, start + 96) for start in range(0, rows, 96)] if rows % 96 == 0 else [slice(0, rows)]:
                one = norm_grad([ref[at, :] for ref in refs[:terms]], value[at, :], gain[...], beside[at, :])
                total[at, :] = one
                rounded[at, :] = one.astype(jnp.bfloat16)

        part = dot(rounded[...], right[...], NT).astype(jnp.bfloat16)
        for slot in range(count):

            @pl.when(pl.program_id(0) == slot)
            def _(slot=slot):
                out[slot][...] = part

    block = whole(rows, width)
    out = call(
        kernel,
        count,
        (*grads, value, gain.reshape(1, width), beside, right),
        [block] * (terms + 1) + [whole(1, width), block, row_block(wide, width)],
        [block] * 2 + [whole(rows, wide)] * count,
        [jax.ShapeDtypeStruct((rows, width), jnp.float32), low_shape(rows, width)]
        + [low_shape(rows, wide)] * count,
        0,
        earlier,
    )
    return out[0], out[1], out[2:]


def widen(terms, weight, part=0, *earlier):
    rows, width = weight.shape
    wide = rows // 2 if rows % 32 == 0 else rows
    count = len(terms)

    def kernel(*refs):
        weight, out, share = refs[count:]
        total = refs[0][...].astype(jnp.float32)
        for ref in refs[1:count]:
            total = total + ref[...].astype(jnp.float32)
        out[...] = total
        share[...] = jnp.sum(total * weight[...].astype(jnp.float32), 1, keepdims=True)

    block = row_block(wide, width)
    return call(
        kernel,
        rows // wide,
        (*terms, weight),
        [pl.BlockSpec((wide, width), lambda f: (f, part))] * count + [block],
        [block, row_block(wide, 1)],
        [jax.ShapeDtypeStruct((rows, width), jnp.float32), jax.ShapeDtypeStruct((rows, 1), jnp.float32)],
        0,
        earlier,
    )


def widen_turned(value, part):
    rows, width = value.shape
    width = width // 2
    wide = 512 if width % 512 == 0 else width
    blocks = width // wide

    def kernel(source, target):
        target[...] = source[...].astype(jnp.float32).T

    return call(
        kernel,
        blocks,
        (value,),
        [pl.BlockSpec((rows, wide), lambda f: (0, part * blocks + f))],
        row_block(wide, rows),
        jax.ShapeDtypeStruct((width, rows), jnp.float32),
        0,
    )


def after(value, *earlier):
    return lax.optimization_barrier((value,) + earlier)[0]


def ring():
    count = lax.axis_size("tensor")
    return [0] + list(range(1, count, 2)) + list(range(2, count, 2))[::-1]


def ring_shift(value, by):
    order = ring()
    count = len(order)
    return lax.ppermute(value, "tensor", [(order[k], order[(k + by) % count]) for k in range(count)])


def slot_places():
    order = ring()
    count = len(order)
    me = lax.axis_index("tensor")
    at = sum(jnp.where(me == device, place, 0) for place, device in enumerate(order))
    back = (at - jnp.arange(count, dtype=jnp.int32)) % count
    return sum(jnp.where(back == place, device, 0) for place, device in enumerate(order)).astype(jnp.int32)


def ring_gather(piece, pauses=()):
    pauses = dict(pauses)
    slots = [piece]
    for step in range(1, lax.axis_size("tensor")):
        last = slots[-1]
        if step in pauses:
            last = tied(last, *pauses[step])
        slots.append(ring_shift(last, 1))
    return slots


def direct_gather(piece):
    return [piece] + [ring_shift(piece, by) for by in range(1, lax.axis_size("tensor"))]


def ring_scatter(parts, pauses=(), heavy=0):
    pauses = dict(pauses)
    count = len(parts)
    arrivals = []
    moving = parts[1]
    for step in range(1, count):
        arrivals.append(ring_shift(moving, 1))
        if step < count - 1:
            if step + 1 in pauses:
                moving = tied_sum(
                    arrivals[-1], parts[step + 1], HEAVY if step + 1 == heavy else 0, *pauses[step + 1]
                )
            else:
                moving = add(arrivals[-1], parts[step + 1])
    return (parts[0], arrivals[-1]), arrivals


def add(left, right):
    return (left.astype(jnp.float32) + right.astype(jnp.float32)).astype(jnp.bfloat16)


def exchange(parts):
    count = len(parts)
    return [parts[0]] + [ring_shift(parts[count - q], q) for q in range(1, count)]


def flip(value, bits):
    count = lax.axis_size("dp")
    return lax.ppermute(value, "dp", [(k, k ^ bits) for k in range(count)])


def cube_pairs(parts, *earlier):
    away, home = parts
    return cube_pair(home, flip(away, 1), *earlier)


def cube_turns(pairs, *earlier):
    _, over_x, over_y, top, bottom = pairs
    return cube_turn(over_x, over_y, flip(top, 2), flip(bottom, 4), *earlier)


def cube_terms(pairs, turns):
    return (pairs[0], flip(turns[0], 2), flip(turns[1], 4))


def cube_total(pairs, turns, dtype, *earlier):
    return total_of(cube_terms(pairs, turns), dtype, *earlier)


def gather_rows(piece):
    return lax.all_gather(piece, "dp", axis=0, tiled=True)


def gather_columns(piece):
    return lax.all_gather(piece, "dp", axis=1, tiled=True)


def sum_rows(value):
    return lax.psum_scatter(value, "dp", scatter_dimension=0, tiled=True)


def sum_columns(value):
    return lax.psum_scatter(value, "dp", scatter_dimension=1, tiled=True)


def gain_sums(shares, gains, places):
    count = places.shape[0]
    rows = shares[0].shape[0]
    start = lax.axis_index("dp") * rows
    own = [share[:, 0] / lax.dynamic_slice_in_dim(gain, start, rows, 0) for share, gain in zip(shares, gains)]
    cut = jnp.stack(own).reshape(len(own), count, -1)
    if count & (count - 1):
        pieces = [lax.dynamic_index_in_dim(cut, places[slot], 1, False) for slot in range(count)]
        return sum(exchange(pieces))
    me = lax.axis_index("tensor")
    total = cut.transpose(1, 0, 2).reshape(count, -1)
    bits = count // 2
    while bits:
        pair = total.reshape(2, bits, -1)
        mine = (me // bits) % 2
        keep = lax.dynamic_index_in_dim(pair, mine, 0, False)
        give = lax.dynamic_index_in_dim(pair, 1 - mine, 0, False)
        total = keep + lax.ppermute(give, "tensor", [(k, k ^ bits) for k in range(count)])
        bits //= 2
    return total.reshape(len(own), -1)


def normalize(value, gain):
    scale = lax.rsqrt(jnp.mean(value * value, axis=1, keepdims=True) + EPS)
    return (value * scale * gain[None, :], scale)


def per_device(
    tokens, lengths, attention_gain, w_inputs, w_output, feed_gain, w_gate, w_up, w_down, cotangent
):
    count = lax.axis_size("tensor")
    groups = KV // count
    local, width = tokens.shape
    rows = local * count
    low = jnp.bfloat16
    held = tables(lengths[0], rows)
    sequences = lengths.shape[1]
    gain_one = attention_gain.astype(jnp.float32)
    gain_two = feed_gain.astype(jnp.float32)

    places = slot_places()
    base = tokens.astype(jnp.float32)
    first = normalize(base, gain_one)[0].astype(low)
    inputs_full = gather_rows(w_inputs)
    first_slots = ring_gather(first)
    output_line = jnp.concatenate(direct_gather(w_output), 0)
    output_full = gather_columns(output_line)
    gate_full = gather_rows(w_gate)
    up_full = gather_rows(w_up)
    down_full = gather_columns(w_down)

    joint = project(first_slots, inputs_full, places)
    heads, query, key, value = attention_forward(joint, held, sequences, groups)
    grad_slots = ring_gather(tied(cotangent, first_slots[max(count - 2, 0)]))
    heads_own = exchange(to_slots(heads, places, grad_slots[1]))
    mixed = base + dot(jnp.concatenate(heads_own, 1), output_full)
    second = tied(normalize(mixed, gain_two)[0].astype(low), grad_slots[min(2, count - 1)])
    second_slots = ring_gather(second)
    half = max(count // 2, 1)
    ahead = feed_forward(second_slots[:half], gate_full, up_full)
    rest = feed_forward(second_slots[half:], gate_full, up_full)
    hidden, slope, silu = [list(one) + list(two) for one, two in zip(ahead, rest)]
    block_parts = product(hidden, down_full)
    down_wpart = weight_grad(hidden, grad_slots, block_parts[0])
    down_wgrad = sum_columns(down_wpart)
    gate_grad, up_grad = feed_backward(grad_slots, down_full, slope, silu, down_wpart)
    block_moving = ring_shift(block_parts[1], 1)
    pick = lambda slots: ((([gate_grad[s] for s in slots]), gate_full), ([up_grad[s] for s in slots], up_full))
    part_one = sum_of_products(pick([1]), block_moving)
    others = [0] + list(range(2, count))
    part_others = sum_of_products(pick(others), part_one[0])
    second_parts = [part_others[0], part_one[0]] + list(part_others[1:])
    second_early = ring_shift(second_parts[1], 1)
    gate_wpart = weight_grad(second_slots, gate_grad, second_early, part_others[0])
    gate_wgrad = sum_rows(gate_wpart)
    second_grad, second_back = ring_scatter(second_parts, {3: [gate_wpart, down_wgrad]}, 3)
    up_wpart = weight_grad(second_slots, up_grad, second_back[1])
    up_wgrad = sum_rows(up_wpart)

    mixed_total, branch, heads_back = norm_split(
        second_grad, mixed, gain_two, cotangent, output_full, count, up_wpart
    )
    heads_grad = exchange(heads_back)
    block_sum, block_back = ring_scatter(block_parts, {2: [gate_grad[0]], 3: [heads_grad[-1]]})
    cube = lax.axis_size("dp") == 8
    output_parts = cube_columns(heads_own, branch) if cube else ()
    joint_grad = attention_backward(
        query, key, value, heads, heads_grad, places, held, groups, block_back[1], gate_wgrad, *output_parts[:1]
    )
    first_one = spread_product(joint_grad, inputs_full, places, [1], block_back[2])
    first_others = spread_product(joint_grad, inputs_full, places, others, first_one[0])
    first_parts = [first_others[0], first_one[0]] + list(first_others[1:])
    gate_wgrad, gate_share = widen([gate_wgrad], w_gate)
    down_grad = total_of([down_wgrad], jnp.float32)
    if cube:
        output_pairs = cube_pairs(output_parts, first_one[0])
        inputs_parts = cube_rows(first_slots, joint_grad, places, 0, output_pairs[0])
        second_pause = [inputs_parts[0]]
        first_next = tied_sum(ring_shift(first_parts[1], 1), first_parts[2], 0, *second_pause)
        output_turns = cube_turns(output_pairs, first_next)
        inputs_sums = cube_sums(inputs_parts, output_turns[0])
        third_pause = [inputs_sums[0], gate_wgrad, up_wgrad]
        first_last = tied_sum(ring_shift(first_next, 1), first_parts[3], 0, *third_pause)
        output_cut = total_slots(cube_terms(output_pairs, output_turns), count, first_last)
        first_grad, first_back = ring_scatter(first_parts, {2: second_pause, 3: third_pause})
        block_out = total_of((*block_sum, mixed), low, first_last, cost=HEAVY)
        inputs_terms = [inputs_sums[0]] + [flip(inputs_sums[at], 2 * at) for at in range(1, 4)]
        inputs_grad, inputs_share = widen(inputs_terms, w_inputs, 0, output_cut[0])
    else:
        first_grad, first_back = ring_scatter(first_parts)
        block_out = total_of((*block_sum, mixed), low)
        output_sum = sum_columns(weight_grad([jnp.concatenate(heads_own, 1)], [branch]))
        inputs_grad = sum_rows(weight_grad(first_slots, to_slots(joint_grad, places)))
        inputs_grad, inputs_share = widen([inputs_grad], w_inputs)
        output_sum = output_sum.reshape(count, -1, output_sum.shape[1])
        output_cut = [output_sum[slot] for slot in range(count)]
    tokens_grad = norm_backward(first_grad, tokens, gain_one, mixed_total, block_out)
    up_wgrad, up_share = widen([up_wgrad], w_up, 0, output_cut[0])
    gain_grads = gain_sums([inputs_share, gate_share + up_share], [gain_one, gain_two], places)
    output_grad = exchange(output_cut)
    output_grad = total_of(output_grad, jnp.float32, tokens_grad)
    return (
        block_out,
        tokens_grad,
        gain_grads[0],
        inputs_grad,
        output_grad,
        gain_grads[1],
        gate_wgrad,
        up_wgrad,
        down_grad,
    )


def solution(mesh):
    in_specs = (
        P(("dp", "tensor"), None),
        P("dp", None),
        P(),
        P("dp", "tensor"),
        P("tensor", "dp"),
        P(),
        P("dp", "tensor"),
        P("dp", "tensor"),
        P("tensor", "dp"),
        P(("dp", "tensor"), None),
    )
    out_specs = (
        P(("dp", "tensor"), None),
        P(("dp", "tensor"), None),
        P(("dp", "tensor")),
        P("dp", "tensor"),
        P("tensor", "dp"),
        P(("dp", "tensor")),
        P("dp", "tensor"),
        P("dp", "tensor"),
        P("tensor", "dp"),
    )
    return jax.shard_map(
        per_device, mesh=mesh, in_specs=in_specs, out_specs=out_specs, check_vma=False
    )
```
